128 devices in a mesh: dp: 4 (over x), fsdp: 16 (over z, y_hi, core), seq: 2 (over y_lo).
Axes of the slice: x: 4, y: 4 (y_hi: 2, y_lo: 2; y = y_hi * 2 + y_lo), z: 4, core: 2. Of those that a mesh axis runs over, the one named last changes fastest.
Arguments:
- tokens: bfloat16 [32768, 1152], P(('dp', 'fsdp', 'seq')), may hold values from -6 to 6
- w_query: bfloat16 [1152, 1024], P('fsdp'), may hold values from -0.1875 to 0.1875
- w_key: bfloat16 [1152, 256], P('fsdp'), may hold values from -0.1875 to 0.1875
- w_value: bfloat16 [1152, 256], P('fsdp'), may hold values from -0.1875 to 0.1875
- w_out: bfloat16 [1024, 1152], P('fsdp'), may hold values from -0.1875 to 0.1875
- w_gate: bfloat16 [1152, 6912], P('fsdp'), may hold values from -0.1875 to 0.1875
- w_up: bfloat16 [1152, 6912], P('fsdp'), may hold values from -0.1875 to 0.1875
- w_down: bfloat16 [6912, 1152], P('fsdp'), may hold values from -0.078125 to 0.078125
- pre_attn_gain: bfloat16 [1152], P('fsdp'), may hold values from -0.29882812 to 0.29882812
- post_attn_gain: bfloat16 [1152], P('fsdp'), may hold values from -0.29882812 to 0.29882812
- pre_mlp_gain: bfloat16 [1152], P('fsdp'), may hold values from -0.29882812 to 0.29882812
- post_mlp_gain: bfloat16 [1152], P('fsdp'), may hold values from -0.29882812 to 0.29882812
- query_gain: bfloat16 [256], P('fsdp'), may hold values from 0 to 0.59765625
- key_gain: bfloat16 [256], P('fsdp'), may hold values from 0 to 0.59765625
- cotangent: bfloat16 [32768, 1152], P(('dp', 'fsdp', 'seq')), may hold values from -6 to 6
Outputs:
- layer_out: bfloat16 [32768, 1152], P(('dp', 'fsdp', 'seq'))
- grad_tokens: bfloat16 [32768, 1152], P(('dp', 'fsdp', 'seq'))
- grad_w_query: float32 [1152, 1024], P('fsdp')
- grad_w_key: float32 [1152, 256], P('fsdp')
- grad_w_value: float32 [1152, 256], P('fsdp')
- grad_w_out: float32 [1024, 1152], P('fsdp')
- grad_w_gate: float32 [1152, 6912], P('fsdp')
- grad_w_up: float32 [1152, 6912], P('fsdp')
- grad_w_down: float32 [6912, 1152], P('fsdp')
- grad_pre_attn_gain: float32 [1152], P('fsdp')
- grad_post_attn_gain: float32 [1152], P('fsdp')
- grad_pre_mlp_gain: float32 [1152], P('fsdp')
- grad_post_mlp_gain: float32 [1152], P('fsdp')
- grad_query_gain: float32 [256], P('fsdp')
- grad_key_gain: float32 [256], P('fsdp')
The draws below stay inside these ranges and needn't reach their ends.
All inputs are finite; a program needn't handle non-finite values.
Results may differ from the reference program's by a relative error of at most 0.025.
Values may be sent and summed in bfloat16 or wider, within the bound.
A program may use at most 256 MiB of HBM per device.

```python
import math
import jax
import jax.numpy as jnp
from jax import lax

D = 1152
H = 4
HD = 256
FF = 6912
SEQ = 512
TOKENS = 32768


def block_levels(rng, shape, pieces, smallest, top_value):
    level, own = 1.0, jax.random.fold_in(rng, 6)
    for axis_at, blocks in pieces:
        draws = jnp.exp(jax.random.uniform(jax.random.fold_in(own, axis_at), (blocks,), jnp.float32, smallest / len(pieces), top_value / len(pieces)))
        level = level * jnp.repeat(draws, shape[axis_at] // blocks).reshape([-1 if axis == axis_at else 1 for axis in range(len(shape))])
    return level


def scatter_about(rng, shape, width, bound, cuts=(), kind=jnp.bfloat16):
    values = jax.random.normal(rng, shape, jnp.float32) * width
    if len(cuts) > 0:
        values = block_levels(rng, shape, cuts, -0.22, 0.18) * values
    return jnp.clip(values, min=-bound, max=bound).astype(kind)


def setup_inputs(seed: int = 0) -> dict:
    keys = jax.random.split(jax.random.key(seed), 16)
    tokens = scatter_about(keys[0], (TOKENS, D), 1.0, 6.0, ((0, 128),))
    w_query = scatter_about(keys[1], (D, H * HD), D ** -0.5, 0.1875, ((0, 16),))
    w_key = scatter_about(keys[2], (D, HD), D ** -0.5, 0.1875, ((0, 16),))
    w_value = scatter_about(keys[3], (D, HD), D ** -0.5, 0.1875, ((0, 16),))
    w_out = scatter_about(keys[4], (H * HD, D), (H * HD) ** -0.5, 0.1875, ((0, 16),))
    w_gate = scatter_about(keys[5], (D, FF), D ** -0.5, 0.1875, ((0, 16),))
    w_up = scatter_about(keys[6], (D, FF), D ** -0.5, 0.1875, ((0, 16),))
    w_down = scatter_about(keys[7], (FF, D), FF ** -0.5, 0.078125, ((0, 16),))
    pre_attn_gain = jnp.clip(jax.random.uniform(keys[8], (D,), jnp.float32, -0.29882812, 0.29882812) * block_levels(keys[8], (D,), ((0, 16),), -0.4, 0.0), -0.29882812, 0.29882812).astype(jnp.bfloat16)
    post_attn_gain = jnp.clip(jax.random.uniform(keys[9], (D,), jnp.float32, -0.29882812, 0.29882812) * block_levels(keys[9], (D,), ((0, 16),), -0.4, 0.0), -0.29882812, 0.29882812).astype(jnp.bfloat16)
    pre_mlp_gain = jnp.clip(jax.random.uniform(keys[10], (D,), jnp.float32, -0.29882812, 0.29882812) * block_levels(keys[10], (D,), ((0, 16),), -0.4, 0.0), -0.29882812, 0.29882812).astype(jnp.bfloat16)
    post_mlp_gain = jnp.clip(jax.random.uniform(keys[11], (D,), jnp.float32, -0.29882812, 0.29882812) * block_levels(keys[11], (D,), ((0, 16),), -0.4, 0.0), -0.29882812, 0.29882812).astype(jnp.bfloat16)
    query_gain = jnp.clip(0.59765625 * jax.random.uniform(keys[12], (HD,), jnp.float32) ** block_levels(keys[12], (HD,), ((0, 16),), -0.2, 0.2), 0.0, 0.59765625).astype(jnp.bfloat16)
    key_gain = jnp.clip(0.59765625 * jax.random.uniform(keys[13], (HD,), jnp.float32) ** block_levels(keys[13], (HD,), ((0, 16),), -0.2, 0.2), 0.0, 0.59765625).astype(jnp.bfloat16)
    cotangent = scatter_about(keys[14], (TOKENS, D), 1.0, 6.0, ((0, 128),))
    return dict(tokens=tokens, w_query=w_query, w_key=w_key, w_value=w_value, w_out=w_out, w_gate=w_gate, w_up=w_up, w_down=w_down, pre_attn_gain=pre_attn_gain, post_attn_gain=post_attn_gain, pre_mlp_gain=pre_mlp_gain, post_mlp_gain=post_mlp_gain, query_gain=query_gain, key_gain=key_gain, cotangent=cotangent)


@jax.custom_vjp
def low(v):
    return lax.optimization_barrier(v.astype(jnp.bfloat16)).astype(jnp.float32)

@jax.custom_vjp
def low_back(v):
    return v

def low_keep(v):
    return (low(v), None)

def low_pass(kept, grad):
    return (grad,)

def back_keep(v):
    return (v, None)

def back_low(kept, grad):
    return (low(grad),)
low.defvjp(low_keep, low_pass)
low_back.defvjp(back_keep, back_low)

def rms_norm(values, scale_gain):
    factor = lax.rsqrt(lax.optimization_barrier(jnp.mean(values * values, axis=-1, keepdims=True)) + 1e-06)
    return values * factor * (1.0 + scale_gain)

def rotate(values, positions):
    half_dim = values.shape[-1] // 2
    frequency = jnp.exp(jnp.arange(half_dim, dtype=jnp.float32) * (-2.0 * math.log(1000000.0) / values.shape[-1]))
    angles = positions[:, None] * frequency[None, :]
    cosine = jnp.cos(angles)[:, None, :]
    sine_part = jnp.sin(angles)[:, None, :]
    first_half = values[..., :half_dim]
    second_half = values[..., half_dim:]
    return jnp.concatenate([first_half * cosine - second_half * sine_part, second_half * cosine + first_half * sine_part], axis=-1)

def dense(left_side, right_side):
    return jnp.dot(left_side, right_side, precision=lax.Precision.HIGHEST)

def block_forward(inputs, w_query, w_key, w_value, w_out, w_gate, w_up, w_down, pre_attn_gain, post_attn_gain, pre_mlp_gain, post_mlp_gain, query_gain, key_gain):
    groups, length, model_width = inputs.shape
    head_dim = w_key.shape[1]
    head_count = w_query.shape[1] // head_dim
    positions = jnp.arange(length).astype(jnp.float32)
    normed = low(rms_norm(inputs, pre_attn_gain))
    query_pre = low_back(dense(normed, w_query)).reshape(groups, length, head_count, head_dim)
    key_pre = low_back(dense(normed, w_key)).reshape(groups, length, 1, head_dim)
    value_rows = low(low_back(dense(normed, w_value)))
    queries = low(low_back(rotate(rms_norm(query_pre, query_gain), positions) * head_dim ** (-0.5)))
    key_rows = low(low_back(rotate(rms_norm(key_pre, key_gain), positions)))[:, :, 0, :]
    scores = low_back(jnp.einsum('gihd,gjd->ghij', queries, key_rows, precision=lax.Precision.HIGHEST))
    places = jnp.arange(length)
    allowed = places[None, :] <= places[:, None]
    scores = jnp.where(allowed, scores, -1e+30)
    weights = low(jax.nn.softmax(scores, axis=-1))
    context = low(low_back(jnp.einsum('ghij,gjd->gihd', weights, value_rows, precision=lax.Precision.HIGHEST)))
    context = context.reshape(groups, length, head_count * head_dim)
    attended = low_back(dense(context, w_out))
    middle = inputs + rms_norm(attended, post_attn_gain)
    mlp_in = low(rms_norm(middle, pre_mlp_gain))
    gate_pre = low_back(dense(mlp_in, w_gate))
    up_pre = low_back(dense(mlp_in, w_up))
    hidden = low(jax.nn.gelu(gate_pre, approximate=True) * up_pre)
    mixed = low_back(dense(hidden, w_down))
    return middle + rms_norm(mixed, post_mlp_gain)

def reference(tokens, w_query, w_key, w_value, w_out, w_gate, w_up, w_down, pre_attn_gain, post_attn_gain, pre_mlp_gain, post_mlp_gain, query_gain, key_gain, cotangent):
    params = tuple((member.astype(jnp.float32) for member in (w_query, w_key, w_value, w_out, w_gate, w_up, w_down, pre_attn_gain, post_attn_gain, pre_mlp_gain, post_mlp_gain, query_gain, key_gain)))
    total_seqs = TOKENS // SEQ
    group_size = math.gcd(total_seqs, max(1, 2048 // SEQ))
    steps_count = total_seqs // group_size
    inputs = tokens.astype(jnp.float32).reshape(steps_count, group_size, SEQ, D)
    cot_groups = cotangent.astype(jnp.float32).reshape(steps_count, group_size, SEQ, D)

    def one_group(running, member):
        group_in, group_cot = member
        result, pull_back = jax.vjp(block_forward, group_in, *params)
        gradients = pull_back(group_cot)
        running = tuple((summed + addend for summed, addend in zip(running, gradients[1:])))
        return (running, (result, gradients[0]))
    start_sums = tuple((jnp.zeros_like(member) for member in params))
    totals, (results, input_grads) = lax.scan(one_group, start_sums, (inputs, cot_groups))
    layer_out = results.reshape(TOKENS, D).astype(jnp.bfloat16)
    grad_tokens = input_grads.reshape(TOKENS, D).astype(jnp.bfloat16)
    return (layer_out, grad_tokens, totals[0], totals[1], totals[2], totals[3], totals[4], totals[5], totals[6], totals[7], totals[8], totals[9], totals[10], totals[11], totals[12])
```

```python
import functools
import math

import jax
import jax.numpy as jnp
from jax import lax
from jax.experimental import pallas as pl
from jax.experimental.pallas import tpu as pltpu
from jax.sharding import PartitionSpec as P

F32, BF16 = jnp.float32, jnp.bfloat16
MESH = pl.DeviceIdType.MESH
NN = (((1,), (0,)), ((), ()))
NT = (((1,), (1,)), ((), ()))
TN = (((0,), (0,)), ((), ()))
EPS = 1e-06
MIB = 2**20
PART = 112
CORE_UNITS = 8 * PART


def dot(a, b, dims=NN):
    return lax.dot_general(a, b, dims, preferred_element_type=F32)


class Place:
    def __init__(self):
        shard = lax.axis_index("fsdp")
        self.x = lax.axis_index("dp")
        self.z = shard // 4
        self.yh = lax.rem(shard // 2, 2)
        self.c = lax.rem(shard, 2)
        self.yl = lax.axis_index("seq")

    def to(self, dx=0, dy=0, dz=0, dc=0):
        x, z, yh, yl, c = self.x, self.z, self.yh, self.yl, self.c
        if dx:
            x = lax.rem(x + dx, 4)
        if dz:
            z = lax.rem(z + dz, 4)
        if dy:
            y = lax.rem(yh * 2 + yl + dy, 4)
            yh, yl = y // 2, lax.rem(y, 2)
        if dc:
            c = 1 - c
        return (x, (z * 2 + yh) * 2 + c, yl)

    def mate(self):
        return self.to(dc=1)

    def pair(self):
        return (self.x, (self.z * 2 + self.yh) * 2 + self.c, 1 - self.yl)


def greet(peers):
    barrier = pltpu.get_barrier_semaphore()
    for peer in peers:
        pl.semaphore_signal(barrier, inc=1, device_id=peer, device_id_type=MESH)
    pl.semaphore_wait(barrier, len(peers))


class Lines:
    def __init__(self, send, recv):
        self.send, self.recv, self.used, self.open = send, recv, 0, []

    def copy(self, src, dst, device):
        k = self.used
        self.used += 1
        made = pltpu.make_async_remote_copy(
            src_ref=src,
            dst_ref=dst,
            send_sem=self.send.at[k],
            recv_sem=self.recv.at[k],
            device_id=device,
            device_id_type=MESH,
        )
        made.start()
        self.open.append(made)
        return made

    def drain(self):
        for made in self.open:
            made.wait_send()
        self.open = []


def gate_terms(gate, up):
    k, c = math.sqrt(2.0 / math.pi), 0.044715
    square = gate * gate
    t = jnp.tanh(gate * (k + (k * c) * square))
    half = 0.5 + 0.5 * t
    act = gate * half
    slope = half + 0.5 * gate * (1.0 - t * t) * (k + (3.0 * k * c) * square)
    return act, slope * up, act * up


class RingGather:
    def __init__(self, here, lines, own, full):
        self.here, self.lines, self.own, self.full = here, lines, own, full

    def start(self):
        here, own, full, copy = self.here, self.own, self.full, self.lines.copy
        n = own.shape[0]
        h = n // 2
        right, left = here.to(dx=1), here.to(dx=3)
        lo, hi = pl.ds(0, h), pl.ds(h, h)
        self.core = copy(own, full.at[0, pl.ds(n, n)], here.mate())
        self.a0 = copy(own.at[lo], full.at[3, lo], right)
        self.b0 = copy(own.at[hi], full.at[1, hi], left)
        self.a1 = copy(own.at[hi], full.at[3, hi], right)
        self.b1 = copy(own.at[lo], full.at[1, lo], left)
        full[0, :n] = own[...]

    def ready0(self):
        self.core.wait_recv()

    def relay(self):
        here, full, copy = self.here, self.full, self.lines.copy
        n = self.own.shape[0]
        h = n // 2
        lo, hi, both, other = pl.ds(0, h), pl.ds(h, h), pl.ds(0, n), pl.ds(n, n)
        right, left, mate = here.to(dx=1), here.to(dx=3), here.mate()
        self.a0.wait_recv()
        self.a2 = copy(full.at[3, lo], full.at[2, lo], right)
        self.b0.wait_recv()
        self.b2 = copy(full.at[1, hi], full.at[2, hi], left)
        self.a1.wait_recv()
        self.f3 = copy(full.at[3, both], full.at[3, other], mate)
        self.b1.wait_recv()
        self.f1 = copy(full.at[1, both], full.at[1, other], mate)

    def ready3(self):
        self.f3.wait_recv()

    def ready1(self):
        self.f1.wait_recv()

    def ready2(self):
        n = self.own.shape[0]
        self.a2.wait_recv()
        self.b2.wait_recv()
        f2 = self.lines.copy(
            self.full.at[2, pl.ds(0, n)], self.full.at[2, pl.ds(n, n)], self.here.mate()
        )
        f2.wait_recv()


class RingSum:
    def __init__(self, here, lines, mine, landed, cross, stage_core, stage_ring):
        self.here, self.lines, self.mine = here, lines, mine
        self.landed, self.cross = landed, cross
        self.stage_core, self.stage_ring = stage_core, stage_ring
        self.pending = []

    def add(self, r, term):
        here = self.here
        self.stage_core[r] = term(1).astype(BF16)
        made = self.lines.copy(self.stage_core.at[r], self.cross.at[r], here.mate())
        near = term(0)
        made.wait_recv()
        near = near + self.cross[r].astype(F32)
        if r == 0:
            self.mine[...] = near
        else:
            self.stage_ring[r - 1] = near.astype(BF16)
            self.pending.append(
                self.lines.copy(
                    self.stage_ring.at[r - 1], self.landed.at[3 - r], here.to(dx=r)
                )
            )

    def total(self):
        for made in self.pending:
            made.wait_recv()
        out = self.mine[...]
        for j in range(3):
            out = out + self.landed[j].astype(F32)
        return out


def norm_back(v, u, n):
    r = lax.rsqrt(jnp.sum(v * v, axis=-1, keepdims=True) * (1.0 / n) + EPS)
    inner = jnp.sum(u * v, axis=-1, keepdims=True) * (1.0 / n)
    return r, r * u - v * (r * r * r * inner)


def mlp_kernel(
    own_x, middle, cot, gain_in, gain_out, w_gate, w_up, w_down,
    layer_out, middle_grad, d_gain_in, d_gain_out, d_in, d_down,
    xs, gs, act, slope, hidden, cross_f, cross_b, landed_f, landed_b, stage_core, stage_ring,
    mine, mixed_grad, send, recv,
):
    here = Place()
    greet([here.mate()] + [here.to(dx=d) for d in (1, 2, 3)])
    lines = Lines(send, recv)
    n, width = own_x.shape

    ring = RingGather(here, lines, own_x, xs)
    sums = RingSum(here, lines, mine, landed_f, cross_f, stage_core, stage_ring)
    ring.start()

    def forward(r):
        x = xs[r]
        a, s, h = gate_terms(dot(x, w_gate[...]), dot(x, w_up[...]))
        act[r] = a.astype(BF16)
        slope[r] = s.astype(BF16)
        hidden[r] = h.astype(BF16)
        sums.add(r, lambda q: dot(hidden[r, q * n : (q + 1) * n], w_down[...]))

    ring.ready0()
    forward(0)
    ring.relay()
    ring.ready3()
    forward(3)
    ring.ready1()
    forward(1)
    ring.ready2()
    forward(2)
    mixed = sums.total()
    lines.drain()

    cot_f = cot[...].astype(F32)
    u = cot_f * (1.0 + gain_out[...])
    factor, grad = norm_back(mixed, u, width)
    layer_out[...] = (middle[...] + mixed * factor * (1.0 + gain_out[...])).astype(BF16)
    d_gain_out[...] = jnp.sum(cot_f * mixed * factor, axis=0, keepdims=True)
    mixed_grad[...] = grad.astype(BF16)

    ring = RingGather(here, lines, mixed_grad, gs)
    sums = RingSum(here, lines, mine, landed_b, cross_b, stage_core, stage_ring)
    ring.start()

    def backward(r):
        hidden_grad = dot(gs[r], w_down[...], NT)
        act[r] = (hidden_grad * act[r].astype(F32)).astype(BF16)
        slope[r] = (hidden_grad * slope[r].astype(F32)).astype(BF16)

        def term(q):
            rows = slice(q * n, (q + 1) * n)
            return dot(slope[r, rows], w_gate[...], NT) + dot(act[r, rows], w_up[...], NT)

        sums.add(r, term)

    ring.ready0()
    backward(0)
    ring.relay()
    ring.ready3()
    backward(3)
    ring.ready1()
    backward(1)
    ring.ready2()
    backward(2)

    flat = lambda ref: ref[...].reshape(ref.shape[0] * ref.shape[1], ref.shape[2])
    grad_down = dot(flat(hidden), flat(gs), TN)
    for k in range(8):
        for p in range(4):
            rows = min(32, PART - 32 * p)
            at = PART * k + 32 * p
            d_down[k // 2, k % 2, p // 2, p % 2, :rows] = grad_down[at : at + rows].astype(BF16)
        d_down[k // 2, k % 2, 1, 1, PART - 96 :] = jnp.zeros((128 - PART, width), BF16)
    for mat, side in ((0, slope), (1, act)):
        grad_side = dot(flat(xs), flat(side), TN)
        for f in range(16):
            d_in[f // 4, (f // 2) % 2, mat, f % 2] = grad_side[72 * f : 72 * f + 72].astype(BF16)

    update = sums.total()
    base = middle[...]
    u = update * (1.0 + gain_in[...])
    factor, grad = norm_back(base, u, width)
    d_gain_in[...] = jnp.sum(update * base * factor, axis=0, keepdims=True)
    middle_grad[...] = cot[...].astype(F32) + grad
    lines.drain()


def mlp_block(own_x, middle, cot, gain_in, gain_out, w_gate, w_up, w_down):
    n, width = own_x.shape
    units = w_gate.shape[1]
    vmem = pl.BlockSpec(memory_space=pltpu.VMEM)
    shape = jax.ShapeDtypeStruct
    scratch = (
        [pltpu.VMEM((4, 2 * n, width), BF16)] * 2
        + [pltpu.VMEM((4, 2 * n, units), BF16)] * 3
        + [pltpu.VMEM((4, n, width), BF16)] * 2
        + [pltpu.VMEM((3, n, width), BF16)] * 2
        + [pltpu.VMEM((4, n, width), BF16), pltpu.VMEM((3, n, width), BF16)]
        + [pltpu.VMEM((n, width), F32), pltpu.VMEM((n, width), BF16)]
        + [pltpu.SemaphoreType.DMA((34,)), pltpu.SemaphoreType.DMA((34,))]
    )
    return pl.pallas_call(
        mlp_kernel,
        out_shape=(
            shape((n, width), BF16),
            shape((n, width), F32),
            shape((1, width), F32),
            shape((1, width), F32),
            shape((4, 2, 2, 2, width // 16, units), BF16),
            shape((4, 2, 2, 2, 32, width), BF16),
        ),
        in_specs=[vmem] * 8,
        out_specs=(vmem,) * 6,
        scratch_shapes=scratch,
        compiler_params=pltpu.CompilerParams(
            collective_id=1, has_side_effects=True, vmem_limit_bytes=63 * MIB
        ),
        name="mlp_block",
    )(own_x, middle, cot, gain_in, gain_out, w_gate, w_up, w_down)


def plane_peers(here):
    return [here.to(dz=d) for d in (1, 2, 3)] + [here.to(dy=d) for d in (1, 2, 3)]


def plane_gather_first(here, lines, local, pairs):
    z, yh, yl = here.z, here.yh, here.yl
    hops = []
    for k, (own, full) in enumerate(pairs):
        keep = pltpu.make_async_copy(own.at[yl], full.at[z, yh, yl], local.at[k])
        keep.start()
        by_z = [lines.copy(own.at[yl, 0], full.at[z, yh, yl, 0], here.to(dz=d)) for d in (1, 3, 2)]
        by_y = [lines.copy(own.at[yl, 1], full.at[z, yh, yl, 1], here.to(dy=d)) for d in (1, 3, 2)]
        keep.wait()
        hops.append((by_z, by_y))
    return hops


def plane_gather_second(here, lines, pairs, hops):
    z, yh, yl = here.z, here.yh, here.yl
    last = []
    for (_, full), (by_z, by_y) in zip(pairs, hops):
        for made in by_z:
            made.wait_recv()
        block = full.at[:, yh, yl, 0]
        last += [lines.copy(block, block, here.to(dy=d)) for d in (1, 3, 2)]
        for made in by_y:
            made.wait_recv()
        block = full.at[z, :, :, 1]
        last += [lines.copy(block, block, here.to(dz=d)) for d in (1, 3, 2)]
    return last


def gather_kernel(
    own_qkv, own_out, own_in, own_down, full_qkv, full_out, full_in, full_down,
    chip_in, send, recv, local,
):
    here = Place()
    greet([here.mate()] + plane_peers(here))
    lines = Lines(send, recv)
    c = here.c
    across = lines.copy(own_in.at[1 - c], chip_in.at[:, c], here.mate())
    keep = pltpu.make_async_copy(own_in.at[c], chip_in.at[:, c], local.at[4])
    keep.start()
    attn = [(own_qkv, full_qkv.at[:, :, c]), (own_out, full_out.at[:, :, c])]
    hops = plane_gather_first(here, lines, local, attn)
    keep.wait()
    across.wait_recv()
    mlp = [(chip_in, full_in), (own_down, full_down)]
    last = plane_gather_second(here, lines, attn, hops)
    hops = plane_gather_first(here, lines, local, mlp)
    for made in last:
        made.wait_recv()
    cores = [lines.copy(full.at[:, :, c], full.at[:, :, c], here.mate()) for full in (full_qkv, full_out)]
    last = plane_gather_second(here, lines, mlp, hops)
    for made in last + cores:
        made.wait_recv()
    lines.drain()


def gather_block(own_qkv, own_out, own_in, own_down):
    hbm = pl.BlockSpec(memory_space=pl.ANY)
    shape = lambda *s: jax.ShapeDtypeStruct(s, BF16)
    piece = lambda a: a.shape[2:]
    return pl.pallas_call(
        gather_kernel,
        out_shape=(
            shape(4, 2, 2, 2, 2, *piece(own_qkv)),
            shape(4, 2, 2, 2, 2, *piece(own_out)),
            shape(4, 2, 2, 2, *own_in.shape[2:]),
            shape(4, 2, 2, 2, *piece(own_down)),
        ),
        in_specs=[hbm] * 4,
        out_specs=(hbm,) * 4,
        scratch_shapes=[
            pltpu.VMEM(own_in.shape, BF16),
            pltpu.SemaphoreType.DMA((51,)),
            pltpu.SemaphoreType.DMA((51,)),
            pltpu.SemaphoreType.DMA((5,)),
        ],
        compiler_params=pltpu.CompilerParams(
            collective_id=0, has_side_effects=True, vmem_limit_bytes=60 * MIB
        ),
        name="gather_weights",
    )(own_qkv, own_out, own_in, own_down)


class PlaneSum:
    def __init__(self, here, lines, grads, landed_a, sums_a, landed_b, sums_b, last_a, last_b):
        self.here, self.lines, self.grads = here, lines, grads
        self.landed_a, self.sums_a, self.last_a = landed_a, sums_a, last_a
        self.landed_b, self.sums_b, self.last_b = landed_b, sums_b, last_b

    @staticmethod
    def scratch(piece):
        vm = lambda *lead: pltpu.VMEM((*lead, *piece), BF16)
        return [vm(3, 4), vm(4), vm(3, 2, 2), vm(2, 2), vm(3), vm(3)]

    def first(self):
        here, g, copy = self.here, self.grads, self.lines.copy
        self.a, self.b = [], []
        for d in (1, 3, 2):
            _, shard, yl = here.to(dy=d)
            yh = lax.rem(shard // 2, 2)
            self.a.append(copy(g.at[:, yh, yl, 0], self.landed_a.at[d - 1], here.to(dy=d)))
            z = here.to(dz=d)[1] // 4
            self.b.append(copy(g.at[z, :, :, 1], self.landed_b.at[d - 1], here.to(dz=d)))

    def second(self):
        here, g, copy = self.here, self.grads, self.lines.copy
        for made in self.a:
            made.wait_recv()
        for k in range(4):
            total = g[k, here.yh, here.yl, 0].astype(F32)
            for j in range(3):
                total = total + self.landed_a[j, k].astype(F32)
            self.sums_a[k] = total.astype(BF16)
        self.a = []
        for d in (1, 3, 2):
            z = here.to(dz=d)[1] // 4
            self.a.append(copy(self.sums_a.at[z], self.last_a.at[d - 1], here.to(dz=d)))
        for made in self.b:
            made.wait_recv()
        for k in range(4):
            total = g[here.z, k // 2, k % 2, 1].astype(F32)
            for j in range(3):
                total = total + self.landed_b[j, k // 2, k % 2].astype(F32)
            self.sums_b[k // 2, k % 2] = total.astype(BF16)
        self.b = []
        for d in (1, 3, 2):
            _, shard, yl = here.to(dy=d)
            yh = lax.rem(shard // 2, 2)
            self.b.append(copy(self.sums_b.at[yh, yl], self.last_b.at[d - 1], here.to(dy=d)))

    def result(self, path):
        here = self.here
        for made in (self.a, self.b)[path]:
            made.wait_recv()
        own = self.sums_a[here.z] if path == 0 else self.sums_b[here.yh, here.yl]
        last = (self.last_a, self.last_b)[path]
        total = own.astype(F32)
        for j in range(3):
            total = total + last[j].astype(F32)
        return total


def reduce_kernel(
    g_in, g_down, g_qkv, g_out, o_in, o_down, o_qkv, o_out,
    chip_qkv, chip_out, cross_qkv, cross_out, swap, half_qkv, half_out, land_qkv, land_out, *rest,
):
    here = Place()
    send, recv = rest[-2:]
    x, yl, c = here.x, here.yl, here.c
    greet([here.mate()] + plane_peers(here) + [here.to(dx=d) for d in (1, 2, 3)])
    lines = Lines(send, recv)
    copy = lines.copy
    cross = [
        copy(g.at[:, :, 1 - c], land, here.mate()) for g, land in ((g_qkv, cross_qkv), (g_out, cross_out))
    ]
    sums = [
        PlaneSum(here, lines, g, *rest[6 * k : 6 * k + 6])
        for k, g in enumerate((g_in, g_down, chip_qkv, chip_out))
    ]
    sums[0].first()
    sums[1].first()
    for made, g, land, chip in (
        (cross[0], g_qkv, cross_qkv, chip_qkv),
        (cross[1], g_out, cross_out, chip_out),
    ):
        made.wait_recv()
        for z in range(4):
            for yh in range(2):
                chip[z, yh] = (g[z, yh, c].astype(F32) + land[z, yh].astype(F32)).astype(BF16)
    sums[2].first()
    sums[3].first()
    for part in sums:
        part.second()

    swap[0] = sums[0].result(0).astype(BF16)
    swap[1] = sums[0].result(1).astype(BF16)
    across = copy(swap.at[1 - c], o_in.at[x, yl, c], here.mate())
    o_in[x, yl, c] = swap[c]
    for path in (0, 1):
        o_down[x, yl, path] = sums[1].result(path).astype(BF16)
    to_pair = [copy(o_down.at[x, yl], o_down.at[x, yl], here.pair())]
    across.wait_recv()
    to_pair.append(copy(o_in.at[x, yl], o_in.at[x, yl], here.pair()))
    for path in (0, 1):
        half_qkv[path] = sums[2].result(path).astype(BF16)
        half_out[path] = sums[3].result(path).astype(BF16)
    by_x = []
    for d in (1, 3, 2):
        by_x.append(copy(half_qkv, land_qkv.at[d - 1], here.to(dx=d)))
        by_x.append(copy(half_out, land_out.at[d - 1], here.to(dx=d)))
    for made in to_pair:
        made.wait_recv()
    spread = []
    for d in (1, 3, 2):
        spread.append(copy(o_in.at[x], o_in.at[x], here.to(dx=d)))
        spread.append(copy(o_down.at[x], o_down.at[x], here.to(dx=d)))
    for made in by_x:
        made.wait_recv()
    for half, land, out in ((half_qkv, land_qkv, o_qkv), (half_out, land_out, o_out)):
        for path in (0, 1):
            total = half[path].astype(F32)
            for j in range(3):
                total = total + land[j, path].astype(F32)
            out[yl, path] = total.astype(BF16)
    ends = [copy(o.at[yl], o.at[yl], here.pair()) for o in (o_qkv, o_out)]
    for made in spread + ends:
        made.wait_recv()
    lines.drain()


def reduce_block(g_in, g_down, g_qkv, g_out):
    vmem = pl.BlockSpec(memory_space=pltpu.VMEM)
    shape = lambda *s: jax.ShapeDtypeStruct(s, BF16)
    p_in, p_down, p_qkv, p_out = g_in.shape[4:], g_down.shape[4:], g_qkv.shape[5:], g_out.shape[5:]
    vm = lambda *s: pltpu.VMEM(s, BF16)
    scratch = [vm(4, 2, 2, 2, *p_qkv), vm(4, 2, 2, 2, *p_out)] * 2
    scratch += [vm(2, *p_in), vm(2, *p_qkv), vm(2, *p_out), vm(3, 2, *p_qkv), vm(3, 2, *p_out)]
    for piece in (p_in, p_down, p_qkv, p_out):
        scratch += PlaneSum.scratch(piece)
    scratch += [pltpu.SemaphoreType.DMA((67,))] * 2
    return pl.pallas_call(
        reduce_kernel,
        out_shape=(
            shape(4, 2, 2, *p_in),
            shape(4, 2, 2, *p_down),
            shape(2, 2, *p_qkv),
            shape(2, 2, *p_out),
        ),
        in_specs=[vmem] * 4,
        out_specs=(vmem,) * 4,
        scratch_shapes=scratch,
        compiler_params=pltpu.CompilerParams(
            collective_id=2, has_side_effects=True, vmem_limit_bytes=60 * MIB
        ),
        name="reduce_grads",
    )(g_in, g_down, g_qkv, g_out)


def rms_norm(values, scale_gain):
    factor = lax.rsqrt(jnp.mean(values * values, axis=-1, keepdims=True) + EPS)
    return values * factor * (1.0 + scale_gain)


def rotate(values, positions):
    half_dim = values.shape[-1] // 2
    frequency = jnp.exp(
        jnp.arange(half_dim, dtype=F32) * (-2.0 * math.log(1000000.0) / values.shape[-1])
    )
    angles = positions[:, None] * frequency[None, :]
    cosine = jnp.cos(angles)[:, None, :]
    sine_part = jnp.sin(angles)[:, None, :]
    first_half = values[..., :half_dim]
    second_half = values[..., half_dim:]
    return jnp.concatenate(
        [
            first_half * cosine - second_half * sine_part,
            second_half * cosine + first_half * sine_part,
        ],
        axis=-1,
    )


def swap_pair(value):
    return lax.ppermute(value, "seq", [(0, 1), (1, 0)])


def body(
    tokens,
    w_query,
    w_key,
    w_value,
    w_out,
    w_gate,
    w_up,
    w_down,
    pre_attn_gain,
    post_attn_gain,
    pre_mlp_gain,
    post_mlp_gain,
    query_gain,
    key_gain,
    cotangent,
):
    n, width = tokens.shape
    rows = w_query.shape[0]
    head_dim = w_key.shape[1]
    heads = w_query.shape[1] // head_dim
    units = w_gate.shape[1]
    out_width = heads * head_dim
    block = units // 16
    x_at = lax.axis_index("dp")
    gains = (pre_attn_gain, post_attn_gain, pre_mlp_gain, post_mlp_gain, query_gain, key_gain)

    qkv = jnp.concatenate([w_query, w_key, w_value], axis=1)
    gain_row = jnp.concatenate(gains)
    gain_row = jnp.pad(gain_row, (0, qkv.shape[1] - gain_row.shape[0]))[None, :]
    qkv = jnp.concatenate([qkv, jnp.pad(gain_row, ((0, 7), (0, 0)))], axis=0)
    own_qkv = qkv.reshape(rows + 8, 2, 2, -1).transpose(1, 2, 0, 3)
    own_out = w_out.reshape(2, 2, -1, width)

    def columns(w):
        w = jnp.pad(w.reshape(rows, 8, 2, block), ((0, 0),) * 3 + ((0, 4 * PART - block),))
        w = lax.dynamic_slice_in_dim(w, x_at * PART, PART, axis=3)
        return w.transpose(2, 0, 1, 3).reshape(2, rows, 8 * PART)

    own_in = jnp.stack([columns(w_gate), columns(w_up)], axis=1)
    down = jnp.pad(w_down, ((0, 4 * PART - block), (0, 0)))
    down = lax.dynamic_slice_in_dim(down, x_at * PART, PART, axis=0)
    own_down = jnp.pad(down, ((0, 128 - PART), (0, 0))).reshape(2, 2, 32, width)

    full_qkv, full_out, full_in, full_down = gather_block(own_qkv, own_out, own_in, own_down)
    gain_rows = full_qkv[:, :, :, 0, 0, rows, :].reshape(16, -1).astype(F32)
    piece = width // 16
    gain_set = [gain_rows[:, piece * k : piece * (k + 1)].reshape(1, -1) for k in range(4)]
    piece_h = head_dim // 16
    at = 4 * piece
    gain_set += [
        gain_rows[:, at + piece_h * k : at + piece_h * (k + 1)].reshape(-1) for k in range(2)
    ]
    attn_gain_in, attn_gain_out, mlp_gain_in, mlp_gain_out, query_scale, key_scale = gain_set
    full_qkv = full_qkv[..., :rows, :].reshape(16, 4, rows, -1).transpose(0, 2, 1, 3)
    full_qkv = full_qkv.reshape(width, out_width + 2 * head_dim)
    full_out = full_out.reshape(out_width, width)
    gate_up = full_in.transpose(2, 0, 1, 3, 4, 5).reshape(2, width, CORE_UNITS)
    full_down = full_down.reshape(8, 128, width)[:, :PART].reshape(CORE_UNITS, width)

    seq_start = lax.axis_index("seq") * n
    query_places = seq_start + jnp.arange(n, dtype=jnp.int32)
    positions = query_places.astype(F32)
    inputs = tokens.astype(F32)
    normed_f, attn_in_pull = jax.vjp(rms_norm, inputs, attn_gain_in[0])
    normed = normed_f.astype(BF16)
    qkv_pre = dot(normed, full_qkv)
    query_pre = qkv_pre[:, :out_width].reshape(n, heads, head_dim)
    key_pre = qkv_pre[:, out_width : out_width + head_dim].reshape(n, 1, head_dim)
    value_local = qkv_pre[:, out_width + head_dim :].astype(BF16)

    def shape_heads(query_in, key_in, query_gain_f, key_gain_f):
        query_out = rotate(rms_norm(query_in, query_gain_f), positions) * head_dim ** (-0.5)
        key_out = rotate(rms_norm(key_in, key_gain_f), positions)
        return (query_out, key_out)

    (query_f, key_f), heads_pull = jax.vjp(shape_heads, query_pre, key_pre, query_scale, key_scale)
    queries = query_f.astype(BF16)
    kv_local = jnp.concatenate([key_f[:, 0, :].astype(BF16), value_local], axis=1)
    kv_other = swap_pair(kv_local)
    low_half = lax.axis_index("seq") == 0
    kv = jnp.concatenate(
        [jnp.where(low_half, kv_local, kv_other), jnp.where(low_half, kv_other, kv_local)], axis=0
    )
    key_rows, value_rows = kv[:, :head_dim], kv[:, head_dim:]
    seq_length = kv.shape[0]
    allowed = jnp.arange(seq_length, dtype=jnp.int32)[None, :] <= query_places[:, None]
    scores = jnp.einsum("ihd,jd->hij", queries, key_rows, preferred_element_type=F32)
    scores = jnp.where(allowed[None, :, :], scores, -1e30)
    row_peak = jnp.max(scores, axis=-1, keepdims=True)
    exp_terms = jnp.exp(scores - row_peak)
    row_total = jnp.sum(exp_terms, axis=-1, keepdims=True)
    prob_rows = exp_terms / row_total
    probs_bf = prob_rows.astype(BF16)
    context = jnp.einsum("hij,jd->ihd", probs_bf, value_rows, preferred_element_type=F32)
    context = context.astype(BF16).reshape(n, out_width)
    attended = dot(context, full_out)
    post_attn, attn_out_pull = jax.vjp(rms_norm, attended, attn_gain_out[0])
    middle = inputs + post_attn
    mlp_in = rms_norm(middle, mlp_gain_in[0]).astype(BF16)

    layer_out, middle_grad, grad_gain_c, grad_gain_d, g_in, g_down = mlp_block(
        mlp_in, middle, cotangent, mlp_gain_in, mlp_gain_out, gate_up[0], gate_up[1], full_down
    )

    attended_grad_f, grad_gain_b = attn_out_pull(middle_grad)
    attended_grad = attended_grad_f.astype(BF16)
    context_grad = dot(attended_grad, full_out, NT).astype(BF16).reshape(n, heads, head_dim)
    prob_grad = jnp.einsum("ihd,jd->hij", context_grad, value_rows, preferred_element_type=F32)
    row_dot = jnp.sum(prob_rows * prob_grad, axis=-1, keepdims=True)
    score_grad = (prob_rows * (prob_grad - row_dot)).astype(BF16)
    query_grad = jnp.einsum("hij,jd->ihd", score_grad, key_rows, preferred_element_type=F32)
    query_grad = query_grad.astype(BF16)
    key_part = jnp.einsum("hij,ihd->jd", score_grad, queries, preferred_element_type=F32)
    value_part = jnp.einsum("hij,ihd->jd", probs_bf, context_grad, preferred_element_type=F32)
    kv_part = jnp.concatenate([key_part, value_part], axis=1)
    kept = jnp.where(low_half, kv_part[:n], kv_part[n:])
    given = jnp.where(low_half, kv_part[n:], kv_part[:n]).astype(BF16)
    kv_grad = (kept + swap_pair(given).astype(F32)).astype(BF16)
    key_grad, value_grad = kv_grad[:, :head_dim], kv_grad[:, head_dim:]
    query_pre_grad, key_pre_grad, grad_query_scale, grad_key_scale = heads_pull(
        (query_grad.astype(F32), key_grad.astype(F32)[:, None, :])
    )
    attn_side = jnp.concatenate(
        [
            query_pre_grad.astype(BF16).reshape(n, out_width),
            key_pre_grad.reshape(n, head_dim).astype(BF16),
            value_grad,
        ],
        axis=1,
    )
    normed_grad = dot(attn_side, full_qkv, NT)
    input_part, grad_gain_a = attn_in_pull(normed_grad)
    grad_tokens = (middle_grad + input_part).astype(BF16)

    g_qkv = dot(normed, attn_side, TN).astype(BF16).reshape(16, rows, -1)
    gain_grads = [
        g.reshape(16, -1)
        for g in (grad_gain_a, grad_gain_b, grad_gain_c, grad_gain_d, grad_query_scale, grad_key_scale)
    ]
    gain_grads = jnp.concatenate(gain_grads, axis=1).astype(BF16)
    gain_grads = jnp.pad(gain_grads, ((0, 0), (0, g_qkv.shape[2] - gain_grads.shape[1])))
    gain_grads = jnp.pad(gain_grads[:, None, :], ((0, 0), (0, 7), (0, 0)))
    g_qkv = jnp.concatenate([g_qkv, gain_grads], axis=1)
    g_qkv = g_qkv.reshape(4, 2, 2, rows + 8, 2, 2, -1).transpose(0, 1, 2, 4, 5, 3, 6)
    g_out = dot(context, attended_grad, TN).astype(BF16).reshape(4, 2, 2, 2, 2, -1, width)

    o_in, o_down, o_qkv, o_out = reduce_block(g_in, g_down, g_qkv, g_out)

    o_qkv = o_qkv.astype(F32)
    gain_out = o_qkv[0, 0, rows]
    grad_qkv = o_qkv[:, :, :rows].transpose(2, 0, 1, 3).reshape(rows, -1)
    grad_w_out = o_out.astype(F32).reshape(-1, width)

    def whole(part):
        part = part.reshape(4, 2, rows, 8, PART).transpose(2, 3, 1, 0, 4)
        return part.reshape(rows, 16, 4 * PART)[..., :block].reshape(rows, units).astype(F32)

    grad_w_down = o_down.reshape(4, 128, width)[:, :PART].reshape(-1, width)[:block].astype(F32)
    cuts = [0] + [piece * k for k in range(1, 5)] + [at + piece_h, at + 2 * piece_h]
    gain_outs = [gain_out[a:b] for a, b in zip(cuts[:-1], cuts[1:])]
    return (
        layer_out,
        grad_tokens,
        grad_qkv[:, :out_width],
        grad_qkv[:, out_width : out_width + head_dim],
        grad_qkv[:, out_width + head_dim :],
        grad_w_out,
        whole(o_in[:, 0]),
        whole(o_in[:, 1]),
        grad_w_down,
        *gain_outs,
    )


def solution(mesh):
    tokens = P(("dp", "fsdp", "seq"), None)
    weight, gain = P("fsdp", None), P("fsdp")
    return jax.shard_map(
        body,
        mesh=mesh,
        in_specs=(tokens,) + (weight,) * 7 + (gain,) * 6 + (tokens,),
        out_specs=(tokens,) * 2 + (weight,) * 7 + (gain,) * 6,
        check_vma=False,
    )
```

```python
import functools
import math

import jax
import jax.numpy as jnp
from jax import lax
from jax.experimental import pallas as pl
from jax.experimental.pallas import tpu as pltpu
from jax.sharding import PartitionSpec as P

F32, BF16 = jnp.float32, jnp.bfloat16
MESH = pl.DeviceIdType.MESH
NN = (((1,), (0,)), ((), ()))
NT = (((1,), (1,)), ((), ()))
TN = (((0,), (0,)), ((), ()))
EPS = 1e-06
MIB = 2**20
PART = 112
CORE_UNITS = 8 * PART


def dot(a, b, dims=NN):
    return lax.dot_general(a, b, dims, preferred_element_type=F32)


class Place:
    def __init__(self):
        shard = lax.axis_index("fsdp")
        self.x = lax.axis_index("dp")
        self.z = shard // 4
        self.yh = lax.rem(shard // 2, 2)
        self.c = lax.rem(shard, 2)
        self.yl = lax.axis_index("seq")

    def to(self, dx=0, dy=0, dz=0, dc=0):
        x, z, yh, yl, c = self.x, self.z, self.yh, self.yl, self.c
        if dx:
            x = lax.rem(x + dx, 4)
        if dz:
            z = lax.rem(z + dz, 4)
        if dy:
            y = lax.rem(yh * 2 + yl + dy, 4)
            yh, yl = y // 2, lax.rem(y, 2)
        if dc:
            c = 1 - c
        return (x, (z * 2 + yh) * 2 + c, yl)

    def mate(self):
        return self.to(dc=1)

    def pair(self):
        return (self.x, (self.z * 2 + self.yh) * 2 + self.c, 1 - self.yl)


def greet(peers):
    barrier = pltpu.get_barrier_semaphore()
    for peer in peers:
        pl.semaphore_signal(barrier, inc=1, device_id=peer, device_id_type=MESH)
    pl.semaphore_wait(barrier, len(peers))


class Lines:
    def __init__(self, send, recv):
        self.send, self.recv, self.used, self.open = send, recv, 0, []

    def copy(self, src, dst, device):
        k = self.used
        self.used += 1
        made = pltpu.make_async_remote_copy(
            src_ref=src,
            dst_ref=dst,
            send_sem=self.send.at[k],
            recv_sem=self.recv.at[k],
            device_id=device,
            device_id_type=MESH,
        )
        made.start()
        self.open.append(made)
        return made

    def drain(self):
        for made in self.open:
            made.wait_send()
        self.open = []


def gate_terms(gate, up):
    k, c = math.sqrt(2.0 / math.pi), 0.044715
    square = gate * gate
    t = jnp.tanh(gate * (k + (k * c) * square))
    half = 0.5 + 0.5 * t
    act = gate * half
    slope = half + 0.5 * gate * (1.0 - t * t) * (k + (3.0 * k * c) * square)
    return act, slope * up, act * up


class RingGather:
    def __init__(self, here, lines, own, full):
        self.here, self.lines, self.own, self.full = here, lines, own, full

    def start(self):
        here, own, full, copy = self.here, self.own, self.full, self.lines.copy
        n = own.shape[0]
        h = n // 2
        right, left = here.to(dx=1), here.to(dx=3)
        lo, hi = pl.ds(0, h), pl.ds(h, h)
        self.core = copy(own, full.at[0, pl.ds(n, n)], here.mate())
        self.a0 = copy(own.at[lo], full.at[3, lo], right)
        self.b0 = copy(own.at[hi], full.at[1, hi], left)
        self.a1 = copy(own.at[hi], full.at[3, hi], right)
        self.b1 = copy(own.at[lo], full.at[1, lo], left)
        full[0, :n] = own[...]

    def ready0(self):
        self.core.wait_recv()

    def relay(self):
        here, full, copy = self.here, self.full, self.lines.copy
        n = self.own.shape[0]
        h = n // 2
        lo, hi, both, other = pl.ds(0, h), pl.ds(h, h), pl.ds(0, n), pl.ds(n, n)
        right, left, mate = here.to(dx=1), here.to(dx=3), here.mate()
        self.a0.wait_recv()
        self.a2 = copy(full.at[3, lo], full.at[2, lo], right)
        self.b0.wait_recv()
        self.b2 = copy(full.at[1, hi], full.at[2, hi], left)
        self.a1.wait_recv()
        self.f3 = copy(full.at[3, both], full.at[3, other], mate)
        self.b1.wait_recv()
        self.f1 = copy(full.at[1, both], full.at[1, other], mate)

    def ready3(self):
        self.f3.wait_recv()

    def ready1(self):
        self.f1.wait_recv()

    def ready2(self):
        n = self.own.shape[0]
        self.a2.wait_recv()
        self.b2.wait_recv()
        f2 = self.lines.copy(
            self.full.at[2, pl.ds(0, n)], self.full.at[2, pl.ds(n, n)], self.here.mate()
        )
        f2.wait_recv()


class RingSum:
    def __init__(self, here, lines, mine, landed, cross, stage_core, stage_ring):
        self.here, self.lines, self.mine = here, lines, mine
        self.landed, self.cross = landed, cross
        self.stage_core, self.stage_ring = stage_core, stage_ring
        self.pending = []

    def add(self, r, term):
        here = self.here
        self.stage_core[r] = term(1).astype(BF16)
        made = self.lines.copy(self.stage_core.at[r], self.cross.at[r], here.mate())
        near = term(0)
        made.wait_recv()
        near = near + self.cross[r].astype(F32)
        if r == 0:
            self.mine[...] = near
        else:
            self.stage_ring[r - 1] = near.astype(BF16)
            self.pending.append(
                self.lines.copy(
                    self.stage_ring.at[r - 1], self.landed.at[3 - r], here.to(dx=r)
                )
            )

    def total(self):
        for made in self.pending:
            made.wait_recv()
        out = self.mine[...]
        for j in range(3):
            out = out + self.landed[j].astype(F32)
        return out


def norm_back(v, u, n):
    r = lax.rsqrt(jnp.sum(v * v, axis=-1, keepdims=True) * (1.0 / n) + EPS)
    inner = jnp.sum(u * v, axis=-1, keepdims=True) * (1.0 / n)
    return r, r * u - v * (r * r * r * inner)


def mlp_kernel(
    own_x, middle, cot, gain_in, gain_out, w_gate, w_up, w_down,
    layer_out, middle_grad, d_gain_in, d_gain_out, d_in, d_down,
    xs, gs, act, slope, hidden, cross_f, cross_b, landed_f, landed_b, stage_core, stage_ring,
    mine, mixed_grad, send, recv,
):
    here = Place()
    greet([here.mate()] + [here.to(dx=d) for d in (1, 2, 3)])
    lines = Lines(send, recv)
    n, width = own_x.shape

    ring = RingGather(here, lines, own_x, xs)
    sums = RingSum(here, lines, mine, landed_f, cross_f, stage_core, stage_ring)
    ring.start()

    def forward(r):
        x = xs[r]
        a, s, h = gate_terms(dot(x, w_gate[...]), dot(x, w_up[...]))
        act[r] = a.astype(BF16)
        slope[r] = s.astype(BF16)
        hidden[r] = h.astype(BF16)
        sums.add(r, lambda q: dot(hidden[r, q * n : (q + 1) * n], w_down[...]))

    ring.ready0()
    forward(0)
    ring.relay()
    ring.ready3()
    forward(3)
    ring.ready1()
    forward(1)
    ring.ready2()
    forward(2)
    mixed = sums.total()
    lines.drain()

    cot_f = cot[...].astype(F32)
    u = cot_f * (1.0 + gain_out[...])
    factor, grad = norm_back(mixed, u, width)
    layer_out[...] = (middle[...] + mixed * factor * (1.0 + gain_out[...])).astype(BF16)
    d_gain_out[...] = jnp.sum(cot_f * mixed * factor, axis=0, keepdims=True)
    mixed_grad[...] = grad.astype(BF16)

    ring = RingGather(here, lines, mixed_grad, gs)
    sums = RingSum(here, lines, mine, landed_b, cross_b, stage_core, stage_ring)
    ring.start()

    def backward(r):
        hidden_grad = dot(gs[r], w_down[...], NT)
        act[r] = (hidden_grad * act[r].astype(F32)).astype(BF16)
        slope[r] = (hidden_grad * slope[r].astype(F32)).astype(BF16)

        def term(q):
            rows = slice(q * n, (q + 1) * n)
            return dot(slope[r, rows], w_gate[...], NT) + dot(act[r, rows], w_up[...], NT)

        sums.add(r, term)

    ring.ready0()
    backward(0)
    ring.relay()
    ring.ready3()
    backward(3)
    ring.ready1()
    backward(1)
    ring.ready2()
    backward(2)

    flat = lambda ref: ref[...].reshape(ref.shape[0] * ref.shape[1], ref.shape[2])
    grad_down = dot(flat(hidden), flat(gs), TN)
    for k in range(8):
        for p in range(4):
            rows = min(32, PART - 32 * p)
            at = PART * k + 32 * p
            d_down[k // 2, k % 2, p // 2, p % 2, :rows] = grad_down[at : at + rows].astype(BF16)
        d_down[k // 2, k % 2, 1, 1, PART - 96 :] = jnp.zeros((128 - PART, width), BF16)
    for mat, side in ((0, slope), (1, act)):
        grad_side = dot(flat(xs), flat(side), TN)
        for f in range(16):
            d_in[f // 4, (f // 2) % 2, mat, f % 2] = grad_side[72 * f : 72 * f + 72].astype(BF16)

    update = sums.total()
    base = middle[...]
    u = update * (1.0 + gain_in[...])
    factor, grad = norm_back(base, u, width)
    d_gain_in[...] = jnp.sum(update * base * factor, axis=0, keepdims=True)
    middle_grad[...] = cot[...].astype(F32) + grad
    lines.drain()


def mlp_block(own_x, middle, cot, gain_in, gain_out, w_gate, w_up, w_down):
    n, width = own_x.shape
    units = w_gate.shape[1]
    vmem = pl.BlockSpec(memory_space=pltpu.VMEM)
    shape = jax.ShapeDtypeStruct
    scratch = (
        [pltpu.VMEM((4, 2 * n, width), BF16)] * 2
        + [pltpu.VMEM((4, 2 * n, units), BF16)] * 3
        + [pltpu.VMEM((4, n, width), BF16)] * 2
        + [pltpu.VMEM((3, n, width), BF16)] * 2
        + [pltpu.VMEM((4, n, width), BF16), pltpu.VMEM((3, n, width), BF16)]
        + [pltpu.VMEM((n, width), F32), pltpu.VMEM((n, width), BF16)]
        + [pltpu.SemaphoreType.DMA((34,)), pltpu.SemaphoreType.DMA((34,))]
    )
    return pl.pallas_call(
        mlp_kernel,
        out_shape=(
            shape((n, width), BF16),
            shape((n, width), F32),
            shape((1, width), F32),
            shape((1, width), F32),
            shape((4, 2, 2, 2, width // 16, units), BF16),
            shape((4, 2, 2, 2, 32, width), BF16),
        ),
        in_specs=[vmem] * 8,
        out_specs=(vmem,) * 6,
        scratch_shapes=scratch,
        compiler_params=pltpu.CompilerParams(
            collective_id=1, has_side_effects=True, vmem_limit_bytes=63 * MIB
        ),
        name="mlp_block",
    )(own_x, middle, cot, gain_in, gain_out, w_gate, w_up, w_down)


def plane_peers(here):
    return [here.to(dz=d) for d in (1, 2, 3)] + [here.to(dy=d) for d in (1, 2, 3)]


def plane_gather_first(here, lines, local, pairs):
    z, yh, yl = here.z, here.yh, here.yl
    hops = []
    for k, (own, full) in enumerate(pairs):
        keep = pltpu.make_async_copy(own.at[yl], full.at[z, yh, yl], local.at[k])
        keep.start()
        by_z = [lines.copy(own.at[yl, 0], full.at[z, yh, yl, 0], here.to(dz=d)) for d in (1, 3, 2)]
        by_y = [lines.copy(own.at[yl, 1], full.at[z, yh, yl, 1], here.to(dy=d)) for d in (1, 3, 2)]
        keep.wait()
        hops.append((by_z, by_y))
    return hops


def plane_gather_second(here, lines, pairs, hops):
    z, yh, yl = here.z, here.yh, here.yl
    last = []
    for (_, full), (by_z, by_y) in zip(pairs, hops):
        for made in by_z:
            made.wait_recv()
        block = full.at[:, yh, yl, 0]
        last += [lines.copy(block, block, here.to(dy=d)) for d in (1, 3, 2)]
        for made in by_y:
            made.wait_recv()
        block = full.at[z, :, :, 1]
        last += [lines.copy(block, block, here.to(dz=d)) for d in (1, 3, 2)]
    return last


def head_forward(pre, scale, cosine, sine, factor):
    r = lax.rsqrt(jnp.mean(pre * pre, axis=-1, keepdims=True) + EPS)
    v = pre * r * (1.0 + scale)
    half = v.shape[1] // 2
    a, b = v[:, :half], v[:, half:]
    turned = jnp.concatenate([a * cosine - b * sine, b * cosine + a * sine], axis=1)
    return (turned * factor).astype(BF16)


def head_backward(grad, pre, scale, cosine, sine, factor):
    grad = grad * factor
    half = grad.shape[1] // 2
    a, b = grad[:, :half], grad[:, half:]
    dy = jnp.concatenate([a * cosine + b * sine, b * cosine - a * sine], axis=1)
    r, out = norm_back(pre, dy * (1.0 + scale), pre.shape[1])
    return out.astype(BF16), jnp.sum(dy * pre * r, axis=0, keepdims=True)


def attend_kernel(
    tokens, cosine, sine, own_qkv, own_out, own_in, own_down,
    full_in, full_down, w_qkv, w_out, gains, normed, queries, kv, probs, context, attended, qkv_pre,
    middle, mlp_in,
    full_qkv, chip_in, send, recv, local,
):
    here = Place()
    greet([here.mate()] + plane_peers(here))
    lines = Lines(send, recv)
    c, yl = here.c, here.yl
    n, width = tokens.shape
    head_dim = 2 * cosine.shape[1]
    heads = queries.shape[1] // head_dim
    rows = width // 16
    across = lines.copy(own_in.at[1 - c], chip_in.at[:, c], here.mate())
    qkv, out = (own_qkv, full_qkv.at[:, :, c]), (own_out, w_out.at[:, :, c])
    mlp = [(chip_in, full_in), (own_down, full_down)]
    hops = plane_gather_first(here, lines, local, [qkv, out])
    chip_in[:, c] = own_in[c]
    x = tokens[...].astype(F32)
    lean = x * lax.rsqrt(jnp.mean(x * x, axis=-1, keepdims=True) + EPS)
    last_qkv = plane_gather_second(here, lines, [qkv], hops[:1])
    last_out = plane_gather_second(here, lines, [out], hops[1:])
    across.wait_recv()
    hops = plane_gather_first(here, lines, local, mlp)
    for made in last_qkv:
        made.wait_recv()
    core_qkv = lines.copy(full_qkv.at[:, :, c], full_qkv.at[:, :, c], here.mate())
    last_in = plane_gather_second(here, lines, mlp[:1], hops[:1])
    last_down = plane_gather_second(here, lines, mlp[1:], hops[1:])
    core_qkv.wait_recv()
    for p in range(4):
        total = jnp.zeros((8, full_qkv.shape[-1]), F32)
        cols = slice(p * full_qkv.shape[-1], (p + 1) * full_qkv.shape[-1])
        for f in range(16):
            part = full_qkv[f // 4, (f // 2) % 2, f % 2, p // 2, p % 2]
            w_qkv[rows * f : rows * f + rows, cols] = part[:rows]
            total = total + part.astype(F32)[rows : rows + 8]
        gains[:, cols] = total
    normed[...] = (lean * (1.0 + gains[0:1, :width])).astype(BF16)
    qkv_pre[...] = dot(normed[...], w_qkv[...])
    cos_v, sin_v = cosine[...], sine[...]
    q_scale, k_scale = (gains[k : k + 1, width : width + head_dim] for k in (0, 1))
    at = heads * head_dim
    key = head_forward(qkv_pre[:, at : at + head_dim], k_scale, cos_v, sin_v, 1.0)
    kv[yl, :, :head_dim] = key
    kv[yl, :, head_dim:] = qkv_pre[:, at + head_dim :].astype(BF16)
    kv_sent = lines.copy(kv.at[yl], kv.at[yl], here.pair())
    for h in range(heads):
        cols = slice(h * head_dim, (h + 1) * head_dim)
        queries[:, cols] = head_forward(qkv_pre[:, cols], q_scale, cos_v, sin_v, head_dim**-0.5)
    for made in last_out:
        made.wait_recv()
    core_out = lines.copy(w_out.at[:, :, c], w_out.at[:, :, c], here.mate())
    kv_sent.wait_recv()
    keys = kv[:, :, :head_dim].reshape(2 * n, head_dim)
    values = kv[:, :, head_dim:].reshape(2 * n, head_dim)
    row = lax.broadcasted_iota(jnp.int32, (n, 2 * n), 0) + yl * n
    allowed = lax.broadcasted_iota(jnp.int32, (n, 2 * n), 1) <= row
    for h in range(heads):
        cols = slice(h * head_dim, (h + 1) * head_dim)
        scores = jnp.where(allowed, dot(queries[:, cols], keys, NT), -1e30)
        terms = jnp.exp(scores - jnp.max(scores, axis=-1, keepdims=True))
        low = (terms * (1.0 / jnp.sum(terms, axis=-1, keepdims=True))).astype(BF16)
        probs[h] = low
        context[:, cols] = dot(low, values).astype(BF16)
    core_out.wait_recv()
    att = dot(context[...], w_out[...].reshape(heads * head_dim, width))
    attended[...] = att
    r = lax.rsqrt(jnp.mean(att * att, axis=-1, keepdims=True) + EPS)
    mid = x + att * r * (1.0 + gains[1:2, :width])
    middle[...] = mid
    r = lax.rsqrt(jnp.mean(mid * mid, axis=-1, keepdims=True) + EPS)
    mlp_in[...] = (mid * r * (1.0 + gains[2:3, :width])).astype(BF16)
    for made in last_in + last_down:
        made.wait_recv()
    lines.drain()


def attend_block(tokens, cosine, sine, own_qkv, own_out, own_in, own_down):
    n, width = tokens.shape
    vmem, hbm = pl.BlockSpec(memory_space=pltpu.VMEM), pl.BlockSpec(memory_space=pl.ANY)
    shape = jax.ShapeDtypeStruct
    p_qkv, p_out, p_in, p_down = own_qkv.shape[2:], own_out.shape[2:], own_in.shape[2:], own_down.shape[2:]
    cols, head_dim = 4 * p_qkv[1], 2 * cosine.shape[1]
    out_width = cols - 2 * head_dim
    return pl.pallas_call(
        attend_kernel,
        out_shape=(
            shape((4, 2, 2, 2, *p_in), BF16),
            shape((4, 2, 2, 2, *p_down), BF16),
            shape((width, cols), BF16),
            shape((4, 2, 2, 2, 2, *p_out), BF16),
            shape((8, cols), F32),
            shape((n, width), BF16),
            shape((n, out_width), BF16),
            shape((2, n, 2 * head_dim), BF16),
            shape((out_width // head_dim, n, 2 * n), BF16),
            shape((n, out_width), BF16),
            shape((n, width), F32),
            shape((n, cols), F32),
            shape((n, width), F32),
            shape((n, width), BF16),
        ),
        in_specs=[vmem] * 7,
        out_specs=(hbm,) * 2 + (vmem,) * 12,
        scratch_shapes=[
            pltpu.VMEM((4, 2, 2, 2, 2, *p_qkv), BF16),
            pltpu.VMEM(own_in.shape, BF16),
            pltpu.SemaphoreType.DMA((52,)),
            pltpu.SemaphoreType.DMA((52,)),
            pltpu.SemaphoreType.DMA((2,)),
        ],
        compiler_params=pltpu.CompilerParams(
            collective_id=0, has_side_effects=True, vmem_limit_bytes=60 * MIB
        ),
        name="attend",
    )(tokens, cosine, sine, own_qkv, own_out, own_in, own_down)


class PlaneSum:
    def __init__(self, here, lines, grads, landed_a, sums_a, landed_b, sums_b, last_a, last_b):
        self.here, self.lines, self.grads = here, lines, grads
        self.landed_a, self.sums_a, self.last_a = landed_a, sums_a, last_a
        self.landed_b, self.sums_b, self.last_b = landed_b, sums_b, last_b

    @staticmethod
    def scratch(piece):
        vm = lambda *lead: pltpu.VMEM((*lead, *piece), BF16)
        return [vm(3, 4), vm(4), vm(3, 2, 2), vm(2, 2), vm(3), vm(3)]

    def first(self):
        here, g, copy = self.here, self.grads, self.lines.copy
        self.a, self.b = [], []
        for d in (1, 3, 2):
            _, shard, yl = here.to(dy=d)
            yh = lax.rem(shard // 2, 2)
            self.a.append(copy(g.at[:, yh, yl, 0], self.landed_a.at[d - 1], here.to(dy=d)))
            z = here.to(dz=d)[1] // 4
            self.b.append(copy(g.at[z, :, :, 1], self.landed_b.at[d - 1], here.to(dz=d)))

    def second(self):
        here, g, copy = self.here, self.grads, self.lines.copy
        for made in self.a:
            made.wait_recv()
        for k in range(4):
            total = g[k, here.yh, here.yl, 0].astype(F32)
            for j in range(3):
                total = total + self.landed_a[j, k].astype(F32)
            self.sums_a[k] = total.astype(BF16)
        self.a = []
        for d in (1, 3, 2):
            z = here.to(dz=d)[1] // 4
            self.a.append(copy(self.sums_a.at[z], self.last_a.at[d - 1], here.to(dz=d)))
        for made in self.b:
            made.wait_recv()
        for k in range(4):
            total = g[here.z, k // 2, k % 2, 1].astype(F32)
            for j in range(3):
                total = total + self.landed_b[j, k // 2, k % 2].astype(F32)
            self.sums_b[k // 2, k % 2] = total.astype(BF16)
        self.b = []
        for d in (1, 3, 2):
            _, shard, yl = here.to(dy=d)
            yh = lax.rem(shard // 2, 2)
            self.b.append(copy(self.sums_b.at[yh, yl], self.last_b.at[d - 1], here.to(dy=d)))

    def result(self, path):
        here = self.here
        for made in (self.a, self.b)[path]:
            made.wait_recv()
        own = self.sums_a[here.z] if path == 0 else self.sums_b[here.yh, here.yl]
        last = (self.last_a, self.last_b)[path]
        total = own.astype(F32)
        for j in range(3):
            total = total + last[j].astype(F32)
        return total


def retreat_kernel(
    middle_grad, attended, context, probs, kv, queries, qkv_pre, normed, tokens, cosine, sine,
    w_qkv, w_out, gains, d_gain_in, d_gain_out, g_in, g_down,
    grad_tokens, o_in, o_down, o_qkv, o_out,
    context_grad, attn_side, kv_part, kv_give, kv_land, g_qkv, g_out, d_gains,
    chip_qkv, chip_out, cross_qkv, cross_out, swap, half_qkv, half_out, land_qkv, land_out, *rest,
):
    here = Place()
    send, recv = rest[-2:]
    x, yl, c = here.x, here.yl, here.c
    greet([here.mate()] + plane_peers(here) + [here.to(dx=d) for d in (1, 2, 3)])
    lines = Lines(send, recv)
    copy = lines.copy
    n, width = middle_grad.shape
    head_dim = 2 * cosine.shape[1]
    heads = queries.shape[1] // head_dim
    rows = width // 16
    at = heads * head_dim
    sums = [
        PlaneSum(here, lines, g, *rest[6 * k : 6 * k + 6])
        for k, g in enumerate((g_in, g_down, chip_qkv, chip_out))
    ]
    sums[0].first()
    sums[1].first()

    att, dy = attended[...], middle_grad[...]
    r, grad = norm_back(att, dy * (1.0 + gains[1:2, :width]), width)
    d_gains[...] = jnp.zeros_like(d_gains)
    d_gains[1:2, :width] = jnp.sum(dy * att * r, axis=0, keepdims=True)
    d_gains[2:3, :width] = d_gain_in[...]
    d_gains[3:4, :width] = d_gain_out[...]
    attended_grad = grad.astype(BF16)
    out_full = w_out[...].reshape(at, width)
    context_grad[...] = dot(attended_grad, out_full, NT).astype(BF16)
    grad_out = dot(context[...], attended_grad, TN)
    g_out[...] = grad_out.astype(BF16).reshape(g_out.shape)
    give_out = copy(g_out.at[:, :, 1 - c], cross_out, here.mate())

    keys = kv[:, :, :head_dim].reshape(2 * n, head_dim)
    values = kv[:, :, head_dim:].reshape(2 * n, head_dim)
    cos_v, sin_v = cosine[...], sine[...]
    q_scale, k_scale = (gains[k : k + 1, width : width + head_dim] for k in (0, 1))
    d_query = jnp.zeros((1, head_dim), F32)
    for h in range(heads):
        cols = slice(h * head_dim, (h + 1) * head_dim)
        low = probs[h]
        high = low.astype(F32)
        prob_grad = dot(context_grad[:, cols], values, NT)
        inner = jnp.sum(high * prob_grad, axis=-1, keepdims=True)
        score_grad = (high * (prob_grad - inner)).astype(BF16)
        key_part = dot(score_grad, queries[:, cols], TN)
        value_part = dot(low, context_grad[:, cols], TN)
        if h == 0:
            kv_part[:, :, :head_dim] = key_part.reshape(2, n, head_dim)
            kv_part[:, :, head_dim:] = value_part.reshape(2, n, head_dim)
        else:
            kv_part[:, :, :head_dim] += key_part.reshape(2, n, head_dim)
            kv_part[:, :, head_dim:] += value_part.reshape(2, n, head_dim)
        query_grad = dot(score_grad, keys).astype(BF16).astype(F32)
        side, d_scale = head_backward(
            query_grad, qkv_pre[:, cols], q_scale, cos_v, sin_v, head_dim**-0.5
        )
        attn_side[:, cols] = side
        d_query = d_query + d_scale
    kv_give[...] = kv_part[1 - yl].astype(BF16)
    kv_sent = copy(kv_give, kv_land, here.pair())
    sums[0].second()
    sums[1].second()
    kv_sent.wait_recv()
    kv_grad = (kv_part[yl] + kv_land[...].astype(F32)).astype(BF16)
    side, d_key = head_backward(
        kv_grad[:, :head_dim].astype(F32), qkv_pre[:, at : at + head_dim], k_scale, cos_v, sin_v, 1.0
    )
    attn_side[:, at : at + head_dim] = side
    attn_side[:, at + head_dim :] = kv_grad[:, head_dim:]
    d_gains[0:1, width : width + head_dim] = d_query
    d_gains[1:2, width : width + head_dim] = d_key

    give_out.wait_recv()
    for z in range(4):
        for yh in range(2):
            chip_out[z, yh] = (g_out[z, yh, c].astype(F32) + cross_out[z, yh].astype(F32)).astype(BF16)
    sums[3].first()

    normed_grad = dot(attn_side[...], w_qkv[...], NT)
    tok = tokens[...].astype(F32)
    r, grad = norm_back(tok, normed_grad * (1.0 + gains[0:1, :width]), width)
    grad_tokens[...] = (middle_grad[...] + grad).astype(BF16)
    d_gains[0:1, :width] = jnp.sum(normed_grad * tok * r, axis=0, keepdims=True)
    grad_qkv = dot(normed[...], attn_side[...], TN)
    for p in range(4):
        cols = slice(p * g_qkv.shape[-1], (p + 1) * g_qkv.shape[-1])
        tail = d_gains[:, cols].astype(BF16)
        for f in range(16):
            spot = (f // 4, (f // 2) % 2, f % 2, p // 2, p % 2)
            block = jnp.concatenate(
                [grad_qkv[rows * f : rows * f + rows, cols], d_gains[:, cols]], axis=0
            )
            g_qkv[spot] = block.astype(BF16)
    give_qkv = copy(g_qkv.at[:, :, 1 - c], cross_qkv, here.mate())

    swap[0] = sums[0].result(0).astype(BF16)
    swap[1] = sums[0].result(1).astype(BF16)
    across = copy(swap.at[1 - c], o_in.at[x, yl, c], here.mate())
    o_in[x, yl, c] = swap[c]
    for path in (0, 1):
        o_down[x, yl, path] = sums[1].result(path).astype(BF16)
    to_pair = [copy(o_down.at[x, yl], o_down.at[x, yl], here.pair())]
    across.wait_recv()
    to_pair.append(copy(o_in.at[x, yl], o_in.at[x, yl], here.pair()))

    give_qkv.wait_recv()
    for z in range(4):
        for yh in range(2):
            chip_qkv[z, yh] = (g_qkv[z, yh, c].astype(F32) + cross_qkv[z, yh].astype(F32)).astype(BF16)
    sums[2].first()
    for made in to_pair:
        made.wait_recv()
    spread = []
    for d in (1, 3, 2):
        spread.append(copy(o_in.at[x], o_in.at[x], here.to(dx=d)))
        spread.append(copy(o_down.at[x], o_down.at[x], here.to(dx=d)))
    sums[3].second()
    sums[2].second()
    for path in (0, 1):
        half_out[path] = sums[3].result(path).astype(BF16)
        half_qkv[path] = sums[2].result(path).astype(BF16)
    by_x = []
    for d in (1, 3, 2):
        by_x.append(copy(half_qkv, land_qkv.at[d - 1], here.to(dx=d)))
        by_x.append(copy(half_out, land_out.at[d - 1], here.to(dx=d)))
    for made in by_x:
        made.wait_recv()
    for half, land, out in ((half_qkv, land_qkv, o_qkv), (half_out, land_out, o_out)):
        for path in (0, 1):
            total = half[path].astype(F32)
            for j in range(3):
                total = total + land[j, path].astype(F32)
            out[yl, path] = total.astype(BF16)
    ends = [copy(o.at[yl], o.at[yl], here.pair()) for o in (o_qkv, o_out)]
    for made in spread + ends:
        made.wait_recv()
    lines.drain()


def retreat_block(*args):
    vmem = pl.BlockSpec(memory_space=pltpu.VMEM)
    shape = jax.ShapeDtypeStruct
    n, width = args[0].shape
    out_width, head_dim = args[5].shape[1], 2 * args[9].shape[1]
    cols = args[6].shape[1]
    g_in, g_down, w_out = args[-2], args[-1], args[12]
    p_in, p_down, p_out = g_in.shape[4:], g_down.shape[4:], w_out.shape[5:]
    p_qkv = (width // 16 + 8, cols // 4)
    vm = lambda *s: pltpu.VMEM(s, BF16)
    scratch = [vm(n, out_width), vm(n, cols), pltpu.VMEM((2, n, 2 * head_dim), F32)]
    scratch += [vm(n, 2 * head_dim)] * 2
    scratch += [vm(4, 2, 2, 2, 2, *p_qkv), vm(4, 2, 2, 2, 2, *p_out), pltpu.VMEM((8, cols), F32)]
    scratch += [vm(4, 2, 2, 2, *p_qkv), vm(4, 2, 2, 2, *p_out)] * 2
    scratch += [vm(2, *p_in), vm(2, *p_qkv), vm(2, *p_out), vm(3, 2, *p_qkv), vm(3, 2, *p_out)]
    for piece in (p_in, p_down, p_qkv, p_out):
        scratch += PlaneSum.scratch(piece)
    scratch += [pltpu.SemaphoreType.DMA((68,))] * 2
    low = lambda *s: shape(s, BF16)
    return pl.pallas_call(
        retreat_kernel,
        out_shape=(
            low(n, width),
            low(4, 2, 2, *p_in),
            low(4, 2, 2, *p_down),
            low(2, 2, *p_qkv),
            low(2, 2, *p_out),
        ),
        in_specs=[vmem] * len(args),
        out_specs=(vmem,) * 5,
        scratch_shapes=scratch,
        compiler_params=pltpu.CompilerParams(
            collective_id=2, has_side_effects=True, vmem_limit_bytes=63 * MIB
        ),
        name="retreat",
    )(*args)


def body(
    tokens,
    w_query,
    w_key,
    w_value,
    w_out,
    w_gate,
    w_up,
    w_down,
    pre_attn_gain,
    post_attn_gain,
    pre_mlp_gain,
    post_mlp_gain,
    query_gain,
    key_gain,
    cotangent,
):
    n, width = tokens.shape
    rows = w_query.shape[0]
    head_dim = w_key.shape[1]
    out_width = w_query.shape[1]
    units = w_gate.shape[1]
    block = units // 16
    x_at, shard = lax.axis_index("dp"), lax.axis_index("fsdp")

    mine = jnp.arange(16) == shard
    spread = lambda g: jnp.where(mine[:, None], g[None, :], 0).reshape(1, -1)
    gains_d = [spread(g) for g in (pre_attn_gain, post_attn_gain, pre_mlp_gain, post_mlp_gain)]
    gains_h = jnp.concatenate([spread(query_gain), spread(key_gain)], axis=0)
    tail = jnp.concatenate(
        [
            jnp.pad(jnp.concatenate(gains_d, axis=0), ((0, 4), (0, 0))),
            jnp.pad(gains_h, ((0, 6), (0, out_width + head_dim - width))),
        ],
        axis=1,
    )
    qkv = jnp.concatenate([w_query, w_key, w_value], axis=1)
    own_qkv = jnp.concatenate([qkv, tail], axis=0)
    own_qkv = own_qkv.reshape(rows + 8, 2, 2, -1).transpose(1, 2, 0, 3)
    own_out = w_out.reshape(2, 2, -1, width)

    def columns(w):
        w = jnp.pad(w.reshape(rows, 8, 2, block), ((0, 0),) * 3 + ((0, 4 * PART - block),))
        w = lax.dynamic_slice_in_dim(w, x_at * PART, PART, axis=3)
        return w.transpose(2, 0, 1, 3).reshape(2, rows, 8 * PART)

    own_in = jnp.stack([columns(w_gate), columns(w_up)], axis=1)
    down = jnp.pad(w_down, ((0, 4 * PART - block), (0, 0)))
    down = lax.dynamic_slice_in_dim(down, x_at * PART, PART, axis=0)
    own_down = jnp.pad(down, ((0, 128 - PART), (0, 0))).reshape(2, 2, 32, width)

    positions = (lax.axis_index("seq") * n + jnp.arange(n, dtype=jnp.int32)).astype(F32)
    frequency = jnp.exp(
        jnp.arange(head_dim // 2, dtype=F32) * (-2.0 * math.log(1000000.0) / head_dim)
    )
    angles = positions[:, None] * frequency[None, :]
    cosine, sine = jnp.cos(angles), jnp.sin(angles)

    (
        full_in, full_down, w_qkv, w_out_full, gains, normed, queries, kv, probs, context, attended,
        qkv_pre, middle, mlp_in,
    ) = attend_block(tokens, cosine, sine, own_qkv, own_out, own_in, own_down)
    gate_up = full_in.transpose(2, 0, 1, 3, 4, 5).reshape(2, width, CORE_UNITS)
    full_down = full_down.reshape(8, 128, width)[:, :PART].reshape(CORE_UNITS, width)

    layer_out, middle_grad, d_gain_in, d_gain_out, g_in, g_down = mlp_block(
        mlp_in, middle, cotangent, gains[2:3, :width], gains[3:4, :width],
        gate_up[0], gate_up[1], full_down,
    )
    grad_tokens, o_in, o_down, o_qkv, o_out = retreat_block(
        middle_grad, attended, context, probs, kv, queries, qkv_pre, normed, tokens, cosine, sine,
        w_qkv, w_out_full, gains, d_gain_in, d_gain_out, g_in, g_down,
    )

    o_qkv = o_qkv.astype(F32)
    grad_qkv = o_qkv[:, :, :rows].transpose(2, 0, 1, 3).reshape(rows, -1)
    tail = o_qkv[:, :, rows:].transpose(2, 0, 1, 3).reshape(8, -1)
    grad_w_out = o_out.astype(F32).reshape(-1, width)
    gain_outs = [lax.dynamic_slice_in_dim(tail[k], shard * rows, rows) for k in range(4)]
    piece = head_dim // 16
    gain_outs += [lax.dynamic_slice_in_dim(tail[k], width + shard * piece, piece) for k in range(2)]

    def whole(part):
        part = part.reshape(4, 2, rows, 8, PART).transpose(2, 3, 1, 0, 4)
        return part.reshape(rows, 16, 4 * PART)[..., :block].reshape(rows, units).astype(F32)

    grad_w_down = o_down.reshape(4, 128, width)[:, :PART].reshape(-1, width)[:block].astype(F32)
    return (
        layer_out,
        grad_tokens,
        grad_qkv[:, :out_width],
        grad_qkv[:, out_width : out_width + head_dim],
        grad_qkv[:, out_width + head_dim :],
        grad_w_out,
        whole(o_in[:, 0]),
        whole(o_in[:, 1]),
        grad_w_down,
        *gain_outs,
    )


def solution(mesh):
    tokens = P(("dp", "fsdp", "seq"), None)
    weight, gain = P("fsdp", None), P("fsdp")
    return jax.shard_map(
        body,
        mesh=mesh,
        in_specs=(tokens,) + (weight,) * 7 + (gain,) * 6 + (tokens,),
        out_specs=(tokens,) * 2 + (weight,) * 7 + (gain,) * 6,
        check_vma=False,
    )
```

```python
import functools
import math

import jax
import jax.numpy as jnp
from jax import lax
from jax.experimental import pallas as pl
from jax.experimental.pallas import tpu as pltpu
from jax.sharding import PartitionSpec as P

F32, BF16 = jnp.float32, jnp.bfloat16
MESH = pl.DeviceIdType.MESH
NN = (((1,), (0,)), ((), ()))
NT = (((1,), (1,)), ((), ()))
TN = (((0,), (0,)), ((), ()))
EPS = 1e-06
MIB = 2**20
PART = 112
CORE_UNITS = 8 * PART


def dot(a, b, dims=NN):
    return lax.dot_general(a, b, dims, preferred_element_type=F32)


class Place:
    def __init__(self):
        shard = lax.axis_index("fsdp")
        self.x = lax.axis_index("dp")
        self.z = shard // 4
        self.yh = lax.rem(shard // 2, 2)
        self.c = lax.rem(shard, 2)
        self.yl = lax.axis_index("seq")

    def to(self, dx=0, dy=0, dz=0, dc=0):
        x, z, yh, yl, c = self.x, self.z, self.yh, self.yl, self.c
        if dx:
            x = lax.rem(x + dx, 4)
        if dz:
            z = lax.rem(z + dz, 4)
        if dy:
            y = lax.rem(yh * 2 + yl + dy, 4)
            yh, yl = y // 2, lax.rem(y, 2)
        if dc:
            c = 1 - c
        return (x, (z * 2 + yh) * 2 + c, yl)

    def mate(self):
        return self.to(dc=1)

    def pair(self):
        return (self.x, (self.z * 2 + self.yh) * 2 + self.c, 1 - self.yl)


def greet(peers):
    barrier = pltpu.get_barrier_semaphore()
    for peer in peers:
        pl.semaphore_signal(barrier, inc=1, device_id=peer, device_id_type=MESH)
    pl.semaphore_wait(barrier, len(peers))


class Moves:
    def __init__(self, sems):
        self.sems, self.used, self.open = sems, 0, []

    def start(self, src, dst):
        made = pltpu.make_async_copy(src, dst, self.sems.at[self.used])
        self.used += 1
        made.start()
        return made

    def store(self, src, dst):
        self.open.append(self.start(src, dst))

    def drain(self):
        for made in self.open:
            made.wait()
        self.open = []


class Lines:
    def __init__(self, send, recv):
        self.send, self.recv, self.used, self.open = send, recv, 0, []

    def copy(self, src, dst, device):
        k = self.used
        self.used += 1
        made = pltpu.make_async_remote_copy(
            src_ref=src,
            dst_ref=dst,
            send_sem=self.send.at[k],
            recv_sem=self.recv.at[k],
            device_id=device,
            device_id_type=MESH,
        )
        made.start()
        self.open.append(made)
        return made

    def drain(self):
        for made in self.open:
            made.wait_send()
        self.open = []


def gate_terms(gate, up):
    k, c = math.sqrt(2.0 / math.pi), 0.044715
    square = gate * gate
    t = jnp.tanh(gate * (k + (k * c) * square))
    half = 0.5 + 0.5 * t
    act = gate * half
    slope = half + 0.5 * gate * (1.0 - t * t) * (k + (3.0 * k * c) * square)
    return act, slope * up, act * up


class RingGather:
    def __init__(self, here, lines, own, full):
        self.here, self.lines, self.own, self.full = here, lines, own, full

    def start(self):
        here, own, full, copy = self.here, self.own, self.full, self.lines.copy
        n = own.shape[0]
        h = n // 2
        right, left = here.to(dx=1), here.to(dx=3)
        lo, hi = pl.ds(0, h), pl.ds(h, h)
        self.core = copy(own, full.at[0, pl.ds(n, n)], here.mate())
        self.a0 = copy(own.at[lo], full.at[3, lo], right)
        self.b0 = copy(own.at[hi], full.at[1, hi], left)
        self.a1 = copy(own.at[hi], full.at[3, hi], right)
        self.b1 = copy(own.at[lo], full.at[1, lo], left)
        full[0, :n] = own[...]

    def ready0(self):
        self.core.wait_recv()

    def relay(self):
        here, full, copy = self.here, self.full, self.lines.copy
        n = self.own.shape[0]
        h = n // 2
        lo, hi, both, other = pl.ds(0, h), pl.ds(h, h), pl.ds(0, n), pl.ds(n, n)
        right, left, mate = here.to(dx=1), here.to(dx=3), here.mate()
        self.a0.wait_recv()
        self.a2 = copy(full.at[3, lo], full.at[2, lo], right)
        self.b0.wait_recv()
        self.b2 = copy(full.at[1, hi], full.at[2, hi], left)
        self.a1.wait_recv()
        self.f3 = copy(full.at[3, both], full.at[3, other], mate)
        self.b1.wait_recv()
        self.f1 = copy(full.at[1, both], full.at[1, other], mate)

    def ready3(self):
        self.f3.wait_recv()

    def ready1(self):
        self.f1.wait_recv()

    def ready2(self):
        n = self.own.shape[0]
        self.a2.wait_recv()
        self.b2.wait_recv()
        f2 = self.lines.copy(
            self.full.at[2, pl.ds(0, n)], self.full.at[2, pl.ds(n, n)], self.here.mate()
        )
        f2.wait_recv()


class RingSum:
    def __init__(self, here, lines, mine, landed, cross, stage_core, stage_ring):
        self.here, self.lines, self.mine = here, lines, mine
        self.landed, self.cross = landed, cross
        self.stage_core, self.stage_ring = stage_core, stage_ring
        self.pending = []

    def add(self, r, term):
        here = self.here
        self.stage_core[r] = term(1).astype(BF16)
        made = self.lines.copy(self.stage_core.at[r], self.cross.at[r], here.mate())
        near = term(0)
        made.wait_recv()
        near = near + self.cross[r].astype(F32)
        if r == 0:
            self.mine[...] = near
        else:
            self.stage_ring[r - 1] = near.astype(BF16)
            self.pending.append(
                self.lines.copy(
                    self.stage_ring.at[r - 1], self.landed.at[3 - r], here.to(dx=r)
                )
            )

    def total(self):
        for made in self.pending:
            made.wait_recv()
        out = self.mine[...]
        for j in range(3):
            out = out + self.landed[j].astype(F32)
        return out


def norm_back(v, u, n):
    r = lax.rsqrt(jnp.sum(v * v, axis=-1, keepdims=True) * (1.0 / n) + EPS)
    inner = jnp.sum(u * v, axis=-1, keepdims=True) * (1.0 / n)
    return r, r * u - v * (r * r * r * inner)


def mlp_kernel(
    xs_h, middle_h, cot_h, gains, w_gate_h, w_up_h, w_down_h,
    layer_out, middle_grad, d_gain_in, d_gain_out, d_in_h, half_down,
    xs, middle, cot, w_gate, w_up, w_down, d_in, gs, act, slope, hidden, cross_f, cross_b, landed_f, landed_b, stage_core, stage_ring,
    mine, mixed_grad, d_down, *rest,
):
    here = Place()
    moves = Moves(rest[-1])
    load_first = [
        moves.start(a, b)
        for a, b in ((xs_h.at[2], xs.at[2]), (w_gate_h, w_gate), (w_up_h, w_up), (w_down_h, w_down))
    ]
    load_xs = {r: moves.start(xs_h.at[r], xs.at[r]) for r in (3, 1, 0)}
    load_last = [moves.start(a, b) for a, b in ((middle_h, middle), (cot_h, cot))]
    greet([here.mate()] + [here.to(dx=d) for d in (1, 2, 3)] + plane_peers(here))
    lines = Lines(*rest[-3:-1])
    n, width = middle.shape
    gain_in, gain_out = gains[2:3, :width], gains[3:4, :width]

    sums = RingSum(here, lines, mine, landed_f, cross_f, stage_core, stage_ring)
    down_sum = PlaneSum(here, lines, d_down, *rest[:6])

    def forward(r):
        x = xs[r]
        a, s, h = gate_terms(dot(x, w_gate[...]), dot(x, w_up[...]))
        act[r] = a.astype(BF16)
        slope[r] = s.astype(BF16)
        hidden[r] = h.astype(BF16)
        sums.add(r, lambda q: dot(hidden[r, q * n : (q + 1) * n], w_down[...]))

    for made in load_first:
        made.wait()
    forward(2)
    for r in (3, 1, 0):
        load_xs[r].wait()
        forward(r)
    for made in load_last:
        made.wait()
    mixed = sums.total()
    lines.drain()

    cot_f = cot[...].astype(F32)
    u = cot_f * (1.0 + gain_out)
    factor, grad = norm_back(mixed, u, width)
    layer_out[...] = (middle[...] + mixed * factor * (1.0 + gain_out)).astype(BF16)
    d_gain_out[...] = jnp.sum(cot_f * mixed * factor, axis=0, keepdims=True)
    mixed_grad[...] = grad.astype(BF16)

    ring = RingGather(here, lines, mixed_grad, gs)
    sums = RingSum(here, lines, mine, landed_b, cross_b, stage_core, stage_ring)
    ring.start()

    def backward(r):
        hidden_grad = dot(gs[r], w_down[...], NT)
        act[r] = (hidden_grad * act[r].astype(F32)).astype(BF16)
        slope[r] = (hidden_grad * slope[r].astype(F32)).astype(BF16)

        def term(q):
            rows = slice(q * n, (q + 1) * n)
            return dot(slope[r, rows], w_gate[...], NT) + dot(act[r, rows], w_up[...], NT)

        sums.add(r, term)

    ring.ready0()
    backward(0)
    ring.relay()
    ring.ready3()
    backward(3)
    ring.ready1()
    backward(1)
    ring.ready2()
    backward(2)

    flat = lambda ref: ref[...].reshape(ref.shape[0] * ref.shape[1], ref.shape[2])
    grad_down = dot(flat(hidden), flat(gs), TN)
    for k in range(8):
        for p in range(4):
            rows = min(32, PART - 32 * p)
            at = PART * k + 32 * p
            d_down[k // 2, k % 2, p // 2, p % 2, :rows] = grad_down[at : at + rows].astype(BF16)
        d_down[k // 2, k % 2, 1, 1, PART - 96 :] = jnp.zeros((128 - PART, width), BF16)
    down_sum.first()
    for mat, side in ((0, slope), (1, act)):
        grad_side = dot(flat(xs), flat(side), TN)
        for f in range(16):
            d_in[f // 4, (f // 2) % 2, mat, f % 2] = grad_side[72 * f : 72 * f + 72].astype(BF16)
        moves.store(d_in.at[:, :, mat], d_in_h.at[:, :, mat])
    down_sum.second()

    update = sums.total()
    base = middle[...]
    u = update * (1.0 + gain_in)
    factor, grad = norm_back(base, u, width)
    d_gain_in[...] = jnp.sum(update * base * factor, axis=0, keepdims=True)
    middle_grad[...] = cot[...].astype(F32) + grad
    for path in (0, 1):
        half_down[path] = down_sum.result(path).astype(BF16)
    lines.drain()
    moves.drain()


def mlp_block(xs, middle, cot, gains, w_gate, w_up, w_down):
    n, width = middle.shape
    units = w_gate.shape[1]
    vmem, hbm = pl.BlockSpec(memory_space=pltpu.VMEM), pl.BlockSpec(memory_space=pl.ANY)
    shape = jax.ShapeDtypeStruct
    d_in = shape((4, 2, 2, 2, width // 16, units), BF16)
    scratch = (
        [pltpu.VMEM(a.shape, a.dtype) for a in (xs, middle, cot, w_gate, w_up, w_down, d_in)]
        + [pltpu.VMEM((4, 2 * n, width), BF16)]
        + [pltpu.VMEM((4, 2 * n, units), BF16)] * 3
        + [pltpu.VMEM((4, n, width), BF16)] * 2
        + [pltpu.VMEM((3, n, width), BF16)] * 2
        + [pltpu.VMEM((4, n, width), BF16), pltpu.VMEM((3, n, width), BF16)]
        + [pltpu.VMEM((n, width), F32), pltpu.VMEM((n, width), BF16)]
        + [pltpu.VMEM((4, 2, 2, 2, 32, width), BF16)]
        + PlaneSum.scratch((32, width))
        + [pltpu.SemaphoreType.DMA((36,))] * 2
        + [pltpu.SemaphoreType.DMA((11,))]
    )
    return pl.pallas_call(
        mlp_kernel,
        out_shape=(
            shape((n, width), BF16),
            shape((n, width), F32),
            shape((1, width), F32),
            shape((1, width), F32),
            d_in,
            shape((2, 32, width), BF16),
        ),
        in_specs=[hbm] * 3 + [vmem] + [hbm] * 3,
        out_specs=(vmem,) * 4 + (hbm, vmem),
        scratch_shapes=scratch,
        compiler_params=pltpu.CompilerParams(
            collective_id=1, has_side_effects=True, vmem_limit_bytes=63 * MIB
        ),
        name="mlp_block",
    )(xs, middle, cot, gains, w_gate, w_up, w_down)


def plane_peers(here):
    return [here.to(dz=d) for d in (1, 2, 3)] + [here.to(dy=d) for d in (1, 2, 3)]


class PlaneGather:
    def __init__(self, here, lines, local, own, full):
        self.here, self.lines, self.local, self.own, self.full = here, lines, local, own, full

    def first(self):
        here, own, full, copy = self.here, self.own, self.full, self.lines.copy
        z, yh, yl = here.z, here.yh, here.yl
        keep = pltpu.make_async_copy(own.at[yl], full.at[z, yh, yl], self.local)
        keep.start()
        self.a, self.b = [], []
        for d in (1, 3, 2):
            self.a.append(copy(own.at[yl, 0], full.at[z, yh, yl, 0], here.to(dz=d)))
            self.b.append(copy(own.at[yl, 1], full.at[z, yh, yl, 1], here.to(dy=d)))
        keep.wait()

    def blocks(self, dy, dz):
        _, shard, yl = self.here.to(dy=dy)
        yh = lax.rem(shard // 2, 2)
        z = self.here.to(dz=dz)[1] // 4
        full = self.full
        return (
            [full.at[pl.ds(0, 2), yh, yl, 0], full.at[pl.ds(2, 2), yh, yl, 0]],
            [full.at[z, 0, :, 1], full.at[z, 1, :, 1]],
        )

    def second(self):
        here, copy = self.here, self.lines.copy
        for made in self.a + self.b:
            made.wait_recv()
        by_y, by_z = self.blocks(0, 0)
        self.early, self.late = [], []
        for block, up, down in (
            (by_y, here.to(dy=1), here.to(dy=3)),
            (by_z, here.to(dz=1), here.to(dz=3)),
        ):
            self.early.append(copy(block[0], block[0], up))
            self.early.append(copy(block[1], block[1], down))
        for block, up, down in (
            (by_y, here.to(dy=1), here.to(dy=3)),
            (by_z, here.to(dz=1), here.to(dz=3)),
        ):
            self.late.append(copy(block[1], block[1], up))
            self.late.append(copy(block[0], block[0], down))

    def relay(self):
        here, copy = self.here, self.lines.copy
        left_y, left_z = self.blocks(3, 3)
        right_y, right_z = self.blocks(1, 1)
        for made, block, to in zip(
            self.early,
            (left_y[0], right_y[1], left_z[0], right_z[1]),
            (here.to(dy=1), here.to(dy=3), here.to(dz=1), here.to(dz=3)),
        ):
            made.wait_recv()
            self.late.append(copy(block, block, to))

    def wait(self):
        for made in self.late:
            made.wait_recv()


def head_forward(pre, scale, cosine, sine, factor):
    r = lax.rsqrt(jnp.mean(pre * pre, axis=-1, keepdims=True) + EPS)
    v = pre * r * (1.0 + scale)
    half = v.shape[1] // 2
    a, b = v[:, :half], v[:, half:]
    turned = jnp.concatenate([a * cosine - b * sine, b * cosine + a * sine], axis=1)
    return (turned * factor).astype(BF16)


def head_backward(grad, pre, scale, cosine, sine, factor):
    grad = grad * factor
    half = grad.shape[1] // 2
    a, b = grad[:, :half], grad[:, half:]
    dy = jnp.concatenate([a * cosine + b * sine, b * cosine - a * sine], axis=1)
    r, out = norm_back(pre, dy * (1.0 + scale), pre.shape[1])
    return out.astype(BF16), jnp.sum(dy * pre * r, axis=0, keepdims=True)


def attend_kernel(
    tokens, cosine, sine, tail, w_query, w_key, w_value, own_out, w_gate, w_up, w_down,
    *refs,
):
    kept = refs[:14]
    gains = refs[14]
    held = refs[15:29]
    (
        xs, gate_full, up_full, down_full, w_qkv, w_out, normed, queries, kv, probs, context,
        attended, qkv_pre, middle,
    ) = held
    mlp_in, own_qkv, own_in, own_down, full_qkv, full_in, full_down, chip_in = refs[29:37]
    send, recv, local, moved = refs[37:]
    moves = Moves(moved)
    place = {id(a): b for a, b in zip(held, kept)}
    keep = lambda ref: moves.store(ref, place[id(ref)])
    here = Place()
    x_at, c, yl = here.x, here.c, here.yl
    n, width = tokens.shape
    rows, units = w_gate.shape
    block = units // 16
    head_dim = w_key.shape[1]
    at = w_query.shape[1]
    heads = at // head_dim
    wide = own_qkv.shape[-1]
    lines = Lines(send, recv)
    gather = [
        PlaneGather(here, lines, local.at[k], own, full)
        for k, (own, full) in enumerate(
            (
                (own_qkv, full_qkv.at[:, :, c]),
                (own_out, w_out.at[:, :, c]),
                (chip_in, full_in),
                (own_down, full_down),
            )
        )
    ]

    sides = [(w_query, 0), (w_key, at), (w_value, at + head_dim)]
    for p in range(4):
        for side, start in sides:
            lo, hi = max(p * wide, start), min((p + 1) * wide, start + side.shape[1])
            if lo < hi:
                own_qkv[p // 2, p % 2, :rows, lo - p * wide : hi - p * wide] = side[
                    :, lo - start : hi - start
                ]
        own_qkv[p // 2, p % 2, rows:] = tail[:, p * wide : (p + 1) * wide]
    greet([here.mate()] + plane_peers(here) + [here.to(dx=d) for d in (1, 2, 3)])
    gather[0].first()
    gather[1].first()
    lane = lax.broadcasted_iota(jnp.int32, (rows, PART), 1)
    inside = lane < block - x_at * PART
    for mat, weight in ((0, w_gate), (1, w_up)):
        turned = pltpu.roll(weight[...].astype(F32), lax.rem(units - PART * x_at, units), 1)
        for core in range(2):
            parts = [
                jnp.where(inside, turned[:, block * f : block * f + PART], 0.0)
                for f in range(core, 16, 2)
            ]
            own_in[core, mat] = jnp.concatenate(parts, axis=1).astype(BF16)
    across = lines.copy(own_in.at[1 - c], chip_in.at[:, c], here.mate())
    chip_in[:, c] = own_in[c]
    gather[0].second()
    for p in range(3):
        start = pl.multiple_of(PART * x_at + 32 * p, 16)
        own_down[p // 2, p % 2] = w_down[pl.ds(start, 32)]
    start = pl.multiple_of(jnp.minimum(PART * x_at + 96, block - 16), 16)
    last = w_down[pl.ds(start, 16)].astype(F32)
    own_down[1, 1, :16] = jnp.where(x_at < 3, last, 0.0).astype(BF16)
    own_down[1, 1, 16:] = jnp.zeros((16, width), BF16)
    x = tokens[...].astype(F32)
    lean = x * lax.rsqrt(jnp.mean(x * x, axis=-1, keepdims=True) + EPS)
    gather[0].relay()
    gather[1].second()
    across.wait_recv()
    gather[2].first()
    gather[3].first()
    gather[0].wait()
    core_qkv = lines.copy(full_qkv.at[:, :, c], full_qkv.at[:, :, c], here.mate())
    core_qkv.wait_recv()
    for p in range(4):
        total = jnp.zeros((8, wide), F32)
        cols = slice(p * wide, (p + 1) * wide)
        for f in range(16):
            part = full_qkv[f // 4, (f // 2) % 2, f % 2, p // 2, p % 2]
            w_qkv[rows * f : rows * f + rows, cols] = part[:rows]
            total = total + part.astype(F32)[rows : rows + 8]
        gains[:, cols] = total
    gather[1].relay()
    gather[2].second()
    keep(w_qkv)
    normed[...] = (lean * (1.0 + gains[0:1, :width])).astype(BF16)
    qkv_pre[...] = dot(normed[...], w_qkv[...])
    cos_v, sin_v = cosine[...], sine[...]
    q_scale, k_scale = (gains[k : k + 1, width : width + head_dim] for k in (0, 1))
    key = head_forward(qkv_pre[:, at : at + head_dim], k_scale, cos_v, sin_v, 1.0)
    kv[yl, :, :head_dim] = key
    kv[yl, :, head_dim:] = qkv_pre[:, at + head_dim :].astype(BF16)
    kv_sent = lines.copy(kv.at[yl], kv.at[yl], here.pair())
    keep(normed)
    keep(qkv_pre)
    for h in range(heads):
        cols = slice(h * head_dim, (h + 1) * head_dim)
        queries[:, cols] = head_forward(qkv_pre[:, cols], q_scale, cos_v, sin_v, head_dim**-0.5)
    gather[1].wait()
    core_out = lines.copy(w_out.at[:, :, c], w_out.at[:, :, c], here.mate())
    kv_sent.wait_recv()
    keep(queries)
    keep(kv)
    keys = kv[:, :, :head_dim].reshape(2 * n, head_dim)
    values = kv[:, :, head_dim:].reshape(2 * n, head_dim)
    row = lax.broadcasted_iota(jnp.int32, (n, 2 * n), 0) + yl * n
    allowed = lax.broadcasted_iota(jnp.int32, (n, 2 * n), 1) <= row
    for h in range(heads):
        cols = slice(h * head_dim, (h + 1) * head_dim)
        scores = jnp.where(allowed, dot(queries[:, cols], keys, NT), -1e30)
        terms = jnp.exp(scores - jnp.max(scores, axis=-1, keepdims=True))
        low = (terms * (1.0 / jnp.sum(terms, axis=-1, keepdims=True))).astype(BF16)
        probs[h] = low
        context[:, cols] = dot(low, values).astype(BF16)
    core_out.wait_recv()
    att = dot(context[...], w_out[...].reshape(at, width))
    attended[...] = att
    r = lax.rsqrt(jnp.mean(att * att, axis=-1, keepdims=True) + EPS)
    mid = x + att * r * (1.0 + gains[1:2, :width])
    middle[...] = mid
    r = lax.rsqrt(jnp.mean(mid * mid, axis=-1, keepdims=True) + EPS)
    mlp_in[...] = (mid * r * (1.0 + gains[2:3, :width])).astype(BF16)
    ring = RingGather(here, lines, mlp_in, xs)
    ring.start()
    for ref in (probs, context, w_out, attended, middle):
        keep(ref)
    gather[2].relay()
    gather[3].second()
    gather[2].wait()
    for f in range(16):
        for mat, whole in ((0, gate_full), (1, up_full)):
            whole[rows * f : rows * f + rows] = full_in[f // 4, (f // 2) % 2, mat, f % 2]
    keep(gate_full)
    keep(up_full)
    gather[3].relay()
    ring.ready0()
    ring.relay()
    gather[3].wait()
    for k in range(8):
        for p in range(4):
            count = min(32, PART - 32 * p)
            down_full[PART * k + 32 * p : PART * k + 32 * p + count] = full_down[
                k // 2, k % 2, p // 2, p % 2, :count
            ]
    keep(down_full)
    ring.ready3()
    ring.ready1()
    ring.ready2()
    keep(xs)
    lines.drain()
    moves.drain()


def attend_block(tokens, cosine, sine, tail, w_query, w_key, w_value, own_out, w_gate, w_up, w_down):
    n, width = tokens.shape
    vmem = pl.BlockSpec(memory_space=pltpu.VMEM)
    shape = jax.ShapeDtypeStruct
    low = lambda *s: shape(s, BF16)
    rows, out_width = w_query.shape
    head_dim, cols = w_key.shape[1], tail.shape[1]
    p_qkv, p_out = (rows + 8, cols // 4), own_out.shape[2:]
    p_in, p_down = (rows, CORE_UNITS), (32, width)
    vm = lambda *s: pltpu.VMEM(s, BF16)
    held = (
        low(4, 2 * n, width),
        low(width, CORE_UNITS),
        low(width, CORE_UNITS),
        low(CORE_UNITS, width),
        low(width, cols),
        low(4, 2, 2, 2, 2, *p_out),
        low(n, width),
        low(n, out_width),
        low(2, n, 2 * head_dim),
        low(out_width // head_dim, n, 2 * n),
        low(n, out_width),
        shape((n, width), F32),
        shape((n, cols), F32),
        shape((n, width), F32),
    )
    return pl.pallas_call(
        attend_kernel,
        out_shape=held + (shape((8, cols), F32),),
        in_specs=[vmem] * 11,
        out_specs=(pl.BlockSpec(memory_space=pl.ANY),) * 14 + (vmem,),
        scratch_shapes=[pltpu.VMEM(a.shape, a.dtype) for a in held]
        + [
            vm(n, width),
            vm(2, 2, *p_qkv),
            vm(2, 2, *p_in),
            vm(2, 2, *p_down),
            vm(4, 2, 2, 2, 2, *p_qkv),
            vm(4, 2, 2, 2, *p_in),
            vm(4, 2, 2, 2, *p_down),
            vm(2, 2, *p_in),
            pltpu.SemaphoreType.DMA((86,)),
            pltpu.SemaphoreType.DMA((86,)),
            pltpu.SemaphoreType.DMA((4,)),
            pltpu.SemaphoreType.DMA((14,)),
        ],
        compiler_params=pltpu.CompilerParams(
            collective_id=0, has_side_effects=True, vmem_limit_bytes=62 * MIB
        ),
        name="attend",
    )(tokens, cosine, sine, tail, w_query, w_key, w_value, own_out, w_gate, w_up, w_down)


class PlaneSum:
    def __init__(
        self, here, lines, grads, landed_a, sums_a, landed_b, sums_b, last_a, last_b, held=None
    ):
        self.here, self.lines, self.grads, self.held = here, lines, grads, held
        self.landed_a, self.sums_a, self.last_a = landed_a, sums_a, last_a
        self.landed_b, self.sums_b, self.last_b = landed_b, sums_b, last_b

    @staticmethod
    def scratch(piece):
        vm = lambda *lead: pltpu.VMEM((*lead, *piece), BF16)
        return [vm(3, 4), vm(4), vm(3, 2, 2), vm(2, 2), vm(3), vm(3)]

    def first(self):
        here, g, copy = self.here, self.grads, self.lines.copy
        self.a, self.b = [], []
        for d in (1, 3, 2):
            _, shard, yl = here.to(dy=d)
            yh = lax.rem(shard // 2, 2)
            self.a.append(copy(g.at[:, yh, yl, 0], self.landed_a.at[d - 1], here.to(dy=d)))
            z = here.to(dz=d)[1] // 4
            self.b.append(copy(g.at[z, :, :, 1], self.landed_b.at[d - 1], here.to(dz=d)))

    def second(self):
        here, g, copy = self.here, self.grads, self.lines.copy
        for made in self.a:
            made.wait_recv()
        for k in range(4):
            own = self.held[0][k] if self.held else g[k, here.yh, here.yl, 0]
            total = own.astype(F32)
            for j in range(3):
                total = total + self.landed_a[j, k].astype(F32)
            self.sums_a[k] = total.astype(BF16)
        self.a = []
        for d in (1, 3, 2):
            z = here.to(dz=d)[1] // 4
            self.a.append(copy(self.sums_a.at[z], self.last_a.at[d - 1], here.to(dz=d)))
        for made in self.b:
            made.wait_recv()
        for k in range(4):
            own = self.held[1][k // 2, k % 2] if self.held else g[here.z, k // 2, k % 2, 1]
            total = own.astype(F32)
            for j in range(3):
                total = total + self.landed_b[j, k // 2, k % 2].astype(F32)
            self.sums_b[k // 2, k % 2] = total.astype(BF16)
        self.b = []
        for d in (1, 3, 2):
            _, shard, yl = here.to(dy=d)
            yh = lax.rem(shard // 2, 2)
            self.b.append(copy(self.sums_b.at[yh, yl], self.last_b.at[d - 1], here.to(dy=d)))

    def result(self, path):
        here = self.here
        for made in (self.a, self.b)[path]:
            made.wait_recv()
        own = self.sums_a[here.z] if path == 0 else self.sums_b[here.yh, here.yl]
        last = (self.last_a, self.last_b)[path]
        total = own.astype(F32)
        for j in range(3):
            total = total + last[j].astype(F32)
        return total


def retreat_kernel(
    middle_grad_h, attended_h, context_h, probs_h, kv_h, queries_h, qkv_pre_h, normed_h, tokens_h,
    w_qkv_h, w_out_h, g_in, cosine, sine, gains, d_gain_in, d_gain_out, half_down,
    grad_tokens, o_in, o_down, o_qkv, o_out,
    middle_grad, attended, context, probs, kv, queries, qkv_pre, normed, tokens, w_qkv, w_out,
    held_a, held_b,
    context_grad, attn_side, kv_part, kv_give, kv_land, g_qkv, g_out, d_gains,
    chip_qkv, chip_out, cross_qkv, cross_out, swap, half_qkv, half_out, land_qkv, land_out, *rest,
):
    here = Place()
    send, recv, moved = rest[-3:]
    x, yl, c = here.x, here.yl, here.c
    moves = Moves(moved)
    loads = {
        name: moves.start(a, b)
        for name, a, b in (
            ("attended", attended_h, attended),
            ("middle_grad", middle_grad_h, middle_grad),
            ("w_out", w_out_h, w_out),
            ("context", context_h, context),
            ("probs", probs_h, probs),
            ("kv", kv_h, kv),
            ("queries", queries_h, queries),
            ("qkv_pre", qkv_pre_h, qkv_pre),
            ("w_qkv", w_qkv_h, w_qkv),
            ("normed", normed_h, normed),
            ("tokens", tokens_h, tokens),
            ("held_a", g_in.at[:, here.yh, yl, 0], held_a),
            ("held_b", g_in.at[here.z, :, :, 1], held_b),
        )
    }

    def ready(*names):
        for name in names:
            loads[name].wait()

    greet([here.mate()] + plane_peers(here) + [here.to(dx=d) for d in (1, 2, 3)])
    lines = Lines(send, recv)
    copy = lines.copy
    n, width = middle_grad.shape
    head_dim = 2 * cosine.shape[1]
    heads = queries.shape[1] // head_dim
    rows = width // 16
    at = heads * head_dim
    sums = [
        PlaneSum(here, lines, g, *rest[6 * k : 6 * k + 6], held)
        for k, (g, held) in enumerate(((g_in, (held_a, held_b)), (chip_qkv, None), (chip_out, None)))
    ]
    sums[0].first()
    o_down[x, yl] = half_down[...]
    down_pair = copy(half_down, o_down.at[x, yl], here.pair())
    ready("attended", "middle_grad", "w_out", "context")

    att, dy = attended[...], middle_grad[...]
    r, grad = norm_back(att, dy * (1.0 + gains[1:2, :width]), width)
    d_gains[...] = jnp.zeros_like(d_gains)
    d_gains[1:2, :width] = jnp.sum(dy * att * r, axis=0, keepdims=True)
    d_gains[2:3, :width] = d_gain_in[...]
    d_gains[3:4, :width] = d_gain_out[...]
    attended_grad = grad.astype(BF16)
    out_full = w_out[...].reshape(at, width)
    context_grad[...] = dot(attended_grad, out_full, NT).astype(BF16)
    grad_out = dot(context[...], attended_grad, TN)
    g_out[...] = grad_out.astype(BF16).reshape(g_out.shape)
    give_out = copy(g_out.at[:, :, 1 - c], cross_out, here.mate())
    down_pair.wait_recv()
    down_x = [copy(o_down.at[x], o_down.at[x], here.to(dx=d)) for d in (1, 3, 2)]

    ready("probs", "kv", "queries", "qkv_pre")
    keys = kv[:, :, :head_dim].reshape(2 * n, head_dim)
    values = kv[:, :, head_dim:].reshape(2 * n, head_dim)
    cos_v, sin_v = cosine[...], sine[...]
    q_scale, k_scale = (gains[k : k + 1, width : width + head_dim] for k in (0, 1))
    d_query = jnp.zeros((1, head_dim), F32)
    for h in range(heads):
        cols = slice(h * head_dim, (h + 1) * head_dim)
        low = probs[h]
        high = low.astype(F32)
        prob_grad = dot(context_grad[:, cols], values, NT)
        inner = jnp.sum(high * prob_grad, axis=-1, keepdims=True)
        score_grad = (high * (prob_grad - inner)).astype(BF16)
        key_part = dot(score_grad, queries[:, cols], TN)
        value_part = dot(low, context_grad[:, cols], TN)
        if h == 0:
            kv_part[:, :, :head_dim] = key_part.reshape(2, n, head_dim)
            kv_part[:, :, head_dim:] = value_part.reshape(2, n, head_dim)
        else:
            kv_part[:, :, :head_dim] += key_part.reshape(2, n, head_dim)
            kv_part[:, :, head_dim:] += value_part.reshape(2, n, head_dim)
        query_grad = dot(score_grad, keys).astype(BF16).astype(F32)
        side, d_scale = head_backward(
            query_grad, qkv_pre[:, cols], q_scale, cos_v, sin_v, head_dim**-0.5
        )
        attn_side[:, cols] = side
        d_query = d_query + d_scale
    kv_give[...] = kv_part[1 - yl].astype(BF16)
    kv_sent = copy(kv_give, kv_land, here.pair())
    give_out.wait_recv()
    for z in range(4):
        for yh in range(2):
            chip_out[z, yh] = (g_out[z, yh, c].astype(F32) + cross_out[z, yh].astype(F32)).astype(BF16)
    sums[2].first()
    kv_sent.wait_recv()
    kv_grad = (kv_part[yl] + kv_land[...].astype(F32)).astype(BF16)
    side, d_key = head_backward(
        kv_grad[:, :head_dim].astype(F32), qkv_pre[:, at : at + head_dim], k_scale, cos_v, sin_v, 1.0
    )
    attn_side[:, at : at + head_dim] = side
    attn_side[:, at + head_dim :] = kv_grad[:, head_dim:]
    d_gains[0:1, width : width + head_dim] = d_query
    d_gains[1:2, width : width + head_dim] = d_key

    ready("w_qkv", "normed", "tokens", "held_a", "held_b")
    normed_grad = dot(attn_side[...], w_qkv[...], NT)
    tok = tokens[...].astype(F32)
    r, grad = norm_back(tok, normed_grad * (1.0 + gains[0:1, :width]), width)
    grad_tokens[...] = (middle_grad[...] + grad).astype(BF16)
    d_gains[0:1, :width] = jnp.sum(normed_grad * tok * r, axis=0, keepdims=True)
    grad_qkv = dot(normed[...], attn_side[...], TN)
    for p in range(4):
        cols = slice(p * g_qkv.shape[-1], (p + 1) * g_qkv.shape[-1])
        tail = d_gains[:, cols].astype(BF16)
        for f in range(16):
            spot = (f // 4, (f // 2) % 2, f % 2, p // 2, p % 2)
            block = jnp.concatenate(
                [grad_qkv[rows * f : rows * f + rows, cols], d_gains[:, cols]], axis=0
            )
            g_qkv[spot] = block.astype(BF16)
    give_qkv = copy(g_qkv.at[:, :, 1 - c], cross_qkv, here.mate())

    sums[0].second()
    give_qkv.wait_recv()
    for z in range(4):
        for yh in range(2):
            chip_qkv[z, yh] = (g_qkv[z, yh, c].astype(F32) + cross_qkv[z, yh].astype(F32)).astype(BF16)
    sums[1].first()
    sums[2].second()
    swap[0] = sums[0].result(0).astype(BF16)
    swap[1] = sums[0].result(1).astype(BF16)
    across = copy(swap.at[1 - c], o_in.at[x, yl, c], here.mate())
    o_in[x, yl, c] = swap[c]
    across.wait_recv()
    in_pair = copy(o_in.at[x, yl], o_in.at[x, yl], here.pair())
    for path in (0, 1):
        half_out[path] = sums[2].result(path).astype(BF16)
    by_x = [copy(half_out, land_out.at[d - 1], here.to(dx=d)) for d in (1, 3, 2)]
    in_pair.wait_recv()
    right, left = here.to(dx=1), here.to(dx=3)
    own = [o_in.at[x, m] for m in (0, 1)]
    early = [copy(own[0], own[0], right), copy(own[1], own[1], left)]
    late = [copy(own[1], own[1], right), copy(own[0], own[0], left)]
    sums[1].second()
    for made, at_x, m, to in ((early[0], left[0], 0, right), (early[1], right[0], 1, left)):
        made.wait_recv()
        late.append(copy(o_in.at[at_x, m], o_in.at[at_x, m], to))
    for path in (0, 1):
        half_qkv[path] = sums[1].result(path).astype(BF16)
    by_x += [copy(half_qkv, land_qkv.at[d - 1], here.to(dx=d)) for d in (1, 3, 2)]
    for made in by_x:
        made.wait_recv()
    for half, land, out in ((half_qkv, land_qkv, o_qkv), (half_out, land_out, o_out)):
        for path in (0, 1):
            total = half[path].astype(F32)
            for j in range(3):
                total = total + land[j, path].astype(F32)
            out[yl, path] = total.astype(BF16)
    ends = [copy(o.at[yl], o.at[yl], here.pair()) for o in (o_qkv, o_out)]
    for made in down_x + late + ends:
        made.wait_recv()
    lines.drain()


def retreat_block(*args):
    (
        middle_grad, attended, context, probs, kv, queries, qkv_pre, normed, tokens, w_qkv, w_out,
        g_in, cosine, _, _, _, _, half_down,
    ) = args
    vmem, hbm = pl.BlockSpec(memory_space=pltpu.VMEM), pl.BlockSpec(memory_space=pl.ANY)
    shape = jax.ShapeDtypeStruct
    n, width = middle_grad.shape
    out_width, head_dim = queries.shape[1], 2 * cosine.shape[1]
    cols = qkv_pre.shape[1]
    p_in, p_down, p_out = g_in.shape[4:], half_down.shape[1:], w_out.shape[5:]
    p_qkv = (width // 16 + 8, cols // 4)
    vm = lambda *s: pltpu.VMEM(s, BF16)
    scratch = [pltpu.VMEM(a.shape, a.dtype) for a in args[:11]]
    scratch += [vm(4, *p_in), vm(2, 2, *p_in)]
    scratch += [vm(n, out_width), vm(n, cols), pltpu.VMEM((2, n, 2 * head_dim), F32)]
    scratch += [vm(n, 2 * head_dim)] * 2
    scratch += [vm(4, 2, 2, 2, 2, *p_qkv), vm(4, 2, 2, 2, 2, *p_out), pltpu.VMEM((8, cols), F32)]
    scratch += [vm(4, 2, 2, 2, *p_qkv), vm(4, 2, 2, 2, *p_out)] * 2
    scratch += [vm(2, *p_in), vm(2, *p_qkv), vm(2, *p_out), vm(3, 2, *p_qkv), vm(3, 2, *p_out)]
    for piece in (p_in, p_qkv, p_out):
        scratch += PlaneSum.scratch(piece)
    scratch += [pltpu.SemaphoreType.DMA((60,))] * 2 + [pltpu.SemaphoreType.DMA((13,))]
    low = lambda *s: shape(s, BF16)
    return pl.pallas_call(
        retreat_kernel,
        out_shape=(
            low(n, width),
            low(4, 2, 2, *p_in),
            low(4, 2, 2, *p_down),
            low(2, 2, *p_qkv),
            low(2, 2, *p_out),
        ),
        in_specs=[hbm] * 12 + [vmem] * 6,
        out_specs=(vmem,) * 5,
        scratch_shapes=scratch,
        compiler_params=pltpu.CompilerParams(
            collective_id=2, has_side_effects=True, vmem_limit_bytes=63 * MIB
        ),
        name="retreat",
    )(*args)


def finish_kernel(
    o_in, o_down, o_qkv, o_out, shown, taken,
    layer_out, grad_tokens, out_query, out_key, out_value, out_out, out_gate, out_up, out_down,
    *out_gains,
):
    rows, units = out_gate.shape
    block = units // 16
    wide = o_qkv.shape[-1]
    at, head_dim = out_query.shape[1], out_key.shape[1]
    for m, out in ((0, out_gate), (1, out_up)):
        for k in range(4):
            count = min(PART, block - PART * k)
            for f in range(16):
                piece = o_in[k, m, f % 2].astype(F32)[:, PART * (f // 2) : PART * (f // 2) + count]
                out[:, block * f + PART * k : block * f + PART * k + count] = piece
    for k in range(4):
        for p in range(4):
            start = PART * k + 32 * p
            count = min(32, PART - 32 * p, block - start)
            if count > 0:
                out_down[start : start + count] = o_down[k, p // 2, p % 2, :count].astype(F32)
    tail = []
    for p in range(4):
        piece = o_qkv[p // 2, p % 2].astype(F32)
        for out, start in ((out_query, 0), (out_key, at), (out_value, at + head_dim)):
            lo, hi = max(p * wide, start), min((p + 1) * wide, start + out.shape[1])
            if lo < hi:
                out[:, lo - start : hi - start] = piece[:rows, lo - p * wide : hi - p * wide]
        tail.append(piece[rows:])
        height = o_out.shape[2]
        out_out[p * height : (p + 1) * height] = o_out[p // 2, p % 2].astype(F32)
    tail = jnp.concatenate(tail, axis=1)
    width = layer_out.shape[1]
    shard = lax.axis_index("fsdp")
    turned = pltpu.roll(tail[:, :width], lax.rem(width - rows * shard, width), 1)
    for k in range(4):
        out_gains[k][...] = turned[k, :rows]
    piece = head_dim // 16
    turned = pltpu.roll(tail[:, width : width + head_dim], lax.rem(head_dim - piece * shard, head_dim), 1)
    for k in range(2):
        out_gains[4 + k][...] = turned[k, :piece]
    layer_out[...] = shown[...]
    grad_tokens[...] = taken[...]


def finish_block(o_in, o_down, o_qkv, o_out, layer_out, grad_tokens, out_shape):
    vmem = pl.BlockSpec(memory_space=pltpu.VMEM)
    return pl.pallas_call(
        finish_kernel,
        out_shape=out_shape,
        in_specs=[vmem] * 6,
        out_specs=(vmem,) * len(out_shape),
        compiler_params=pltpu.CompilerParams(vmem_limit_bytes=48 * MIB),
        name="finish",
    )(o_in, o_down, o_qkv, o_out, layer_out, grad_tokens)


def body(
    tokens,
    w_query,
    w_key,
    w_value,
    w_out,
    w_gate,
    w_up,
    w_down,
    pre_attn_gain,
    post_attn_gain,
    pre_mlp_gain,
    post_mlp_gain,
    query_gain,
    key_gain,
    cotangent,
):
    n, width = tokens.shape
    rows = w_query.shape[0]
    head_dim = w_key.shape[1]
    out_width = w_query.shape[1]
    shard = lax.axis_index("fsdp")

    mine = jnp.arange(16) == shard
    spread = lambda g: jnp.where(mine[:, None], g[None, :], 0).reshape(1, -1)
    gains_d = [spread(g) for g in (pre_attn_gain, post_attn_gain, pre_mlp_gain, post_mlp_gain)]
    gains_h = jnp.concatenate([spread(query_gain), spread(key_gain)], axis=0)
    tail = jnp.concatenate(
        [
            jnp.pad(jnp.concatenate(gains_d, axis=0), ((0, 4), (0, 0))),
            jnp.pad(gains_h, ((0, 6), (0, out_width + head_dim - width))),
        ],
        axis=1,
    )
    own_out = w_out.reshape(2, 2, -1, width)
    positions = (lax.axis_index("seq") * n + jnp.arange(n, dtype=jnp.int32)).astype(F32)
    frequency = jnp.exp(
        jnp.arange(head_dim // 2, dtype=F32) * (-2.0 * math.log(1000000.0) / head_dim)
    )
    angles = positions[:, None] * frequency[None, :]
    cosine, sine = jnp.cos(angles), jnp.sin(angles)

    (
        xs, gate_full, up_full, down_full, w_qkv, w_out_full, normed, queries, kv, probs, context,
        attended, qkv_pre, middle, gains,
    ) = attend_block(
        tokens, cosine, sine, tail, w_query, w_key, w_value, own_out, w_gate, w_up, w_down
    )
    layer_out, middle_grad, d_gain_in, d_gain_out, g_in, half_down = mlp_block(
        xs, middle, cotangent, gains, gate_full, up_full, down_full
    )
    grad_tokens, o_in, o_down, o_qkv, o_out = retreat_block(
        middle_grad, attended, context, probs, kv, queries, qkv_pre, normed, tokens, w_qkv,
        w_out_full, g_in, cosine, sine, gains, d_gain_in, d_gain_out, half_down,
    )
    like = lambda a, kind: jax.ShapeDtypeStruct(a.shape, kind)
    weights = (w_query, w_key, w_value, w_out, w_gate, w_up, w_down)
    gain_args = (pre_attn_gain, post_attn_gain, pre_mlp_gain, post_mlp_gain, query_gain, key_gain)
    shapes = [like(tokens, BF16)] * 2 + [like(a, F32) for a in weights + gain_args]
    return tuple(finish_block(o_in, o_down, o_qkv, o_out, layer_out, grad_tokens, shapes))


def solution(mesh):
    tokens = P(("dp", "fsdp", "seq"), None)
    weight, gain = P("fsdp", None), P("fsdp")
    return jax.shard_map(
        body,
        mesh=mesh,
        in_specs=(tokens,) + (weight,) * 7 + (gain,) * 6 + (tokens,),
        out_specs=(tokens,) * 2 + (weight,) * 7 + (gain,) * 6,
        check_vma=False,
    )
```

```python
import functools
import math

import jax
import jax.numpy as jnp
from jax import lax
from jax.experimental import pallas as pl
from jax.experimental.pallas import tpu as pltpu
from jax.sharding import PartitionSpec as P

F32, BF16 = jnp.float32, jnp.bfloat16
MESH = pl.DeviceIdType.MESH
NN = (((1,), (0,)), ((), ()))
NT = (((1,), (1,)), ((), ()))
TN = (((0,), (0,)), ((), ()))
EPS = 1e-06
MIB = 2**20
PART = 112
CORE_UNITS = 8 * PART


def dot(a, b, dims=NN):
    return lax.dot_general(a, b, dims, preferred_element_type=F32)


class Place:
    def __init__(self):
        shard = lax.axis_index("fsdp")
        self.x = lax.axis_index("dp")
        self.z = shard // 4
        self.yh = lax.rem(shard // 2, 2)
        self.c = lax.rem(shard, 2)
        self.yl = lax.axis_index("seq")

    def to(self, dx=0, dy=0, dz=0, dc=0):
        x, z, yh, yl, c = self.x, self.z, self.yh, self.yl, self.c
        if dx:
            x = lax.rem(x + dx, 4)
        if dz:
            z = lax.rem(z + dz, 4)
        if dy:
            y = lax.rem(yh * 2 + yl + dy, 4)
            yh, yl = y // 2, lax.rem(y, 2)
        if dc:
            c = 1 - c
        return (x, (z * 2 + yh) * 2 + c, yl)

    def mate(self):
        return self.to(dc=1)

    def pair(self):
        return (self.x, (self.z * 2 + self.yh) * 2 + self.c, 1 - self.yl)


def greet(peers):
    barrier = pltpu.get_barrier_semaphore()
    for peer in peers:
        pl.semaphore_signal(barrier, inc=1, device_id=peer, device_id_type=MESH)
    pl.semaphore_wait(barrier, len(peers))


class Moves:
    def __init__(self, sems):
        self.sems, self.used, self.open = sems, 0, []

    def start(self, src, dst):
        made = pltpu.make_async_copy(src, dst, self.sems.at[self.used])
        self.used += 1
        made.start()
        return made

    def store(self, src, dst):
        self.open.append(self.start(src, dst))

    def drain(self):
        for made in self.open:
            made.wait()
        self.open = []


class Lines:
    def __init__(self, send, recv):
        self.send, self.recv, self.used, self.open = send, recv, 0, []

    def copy(self, src, dst, device):
        k = self.used
        self.used += 1
        made = pltpu.make_async_remote_copy(
            src_ref=src,
            dst_ref=dst,
            send_sem=self.send.at[k],
            recv_sem=self.recv.at[k],
            device_id=device,
            device_id_type=MESH,
        )
        made.start()
        self.open.append(made)
        return made

    def drain(self):
        for made in self.open:
            made.wait_send()
        self.open = []


def gate_terms(gate, up):
    k, c = math.sqrt(2.0 / math.pi), 0.044715
    square = gate * gate
    t = jnp.tanh(gate * (k + (k * c) * square))
    half = 0.5 + 0.5 * t
    act = gate * half
    slope = half + 0.5 * gate * (1.0 - t * t) * (k + (3.0 * k * c) * square)
    return act, slope * up, act * up


class RingGather:
    def __init__(self, here, lines, own, full):
        self.here, self.lines, self.own, self.full = here, lines, own, full

    def start(self):
        here, own, full, copy = self.here, self.own, self.full, self.lines.copy
        n = own.shape[0]
        h = n // 2
        right, left = here.to(dx=1), here.to(dx=3)
        lo, hi = pl.ds(0, h), pl.ds(h, h)
        self.core = copy(own, full.at[0, pl.ds(n, n)], here.mate())
        self.a0 = copy(own.at[lo], full.at[3, lo], right)
        self.b0 = copy(own.at[hi], full.at[1, hi], left)
        self.a1 = copy(own.at[hi], full.at[3, hi], right)
        self.b1 = copy(own.at[lo], full.at[1, lo], left)
        full[0, :n] = own[...]

    def ready0(self):
        self.core.wait_recv()

    def relay(self):
        here, full, copy = self.here, self.full, self.lines.copy
        n = self.own.shape[0]
        h = n // 2
        lo, hi = pl.ds(0, h), pl.ds(h, h)
        right, left = here.to(dx=1), here.to(dx=3)
        self.a0.wait_recv()
        self.a2 = copy(full.at[3, lo], full.at[2, lo], right)
        self.b0.wait_recv()
        self.b2 = copy(full.at[1, hi], full.at[2, hi], left)

    def forward(self):
        full, copy = self.full, self.lines.copy
        n = self.own.shape[0]
        both, other = pl.ds(0, n), pl.ds(n, n)
        mate = self.here.mate()
        self.a1.wait_recv()
        self.f3 = copy(full.at[3, both], full.at[3, other], mate)
        self.b1.wait_recv()
        self.f1 = copy(full.at[1, both], full.at[1, other], mate)

    def ready3(self):
        self.f3.wait_recv()

    def ready1(self):
        self.f1.wait_recv()

    def ready2(self):
        n = self.own.shape[0]
        self.a2.wait_recv()
        self.b2.wait_recv()
        f2 = self.lines.copy(
            self.full.at[2, pl.ds(0, n)], self.full.at[2, pl.ds(n, n)], self.here.mate()
        )
        f2.wait_recv()


class RingSum:
    def __init__(self, here, lines, mine, landed, cross, stage_core, stage_ring):
        self.here, self.lines, self.mine = here, lines, mine
        self.landed, self.cross = landed, cross
        self.stage_core, self.stage_ring = stage_core, stage_ring
        self.pending = []

    def add(self, r, term):
        here = self.here
        self.stage_core[r] = term(1).astype(BF16)
        made = self.lines.copy(self.stage_core.at[r], self.cross.at[r], here.mate())
        near = term(0)
        made.wait_recv()
        near = near + self.cross[r].astype(F32)
        if r == 0:
            self.mine[...] = near
        else:
            self.stage_ring[r - 1] = near.astype(BF16)
            self.pending.append(
                self.lines.copy(
                    self.stage_ring.at[r - 1], self.landed.at[3 - r], here.to(dx=r)
                )
            )

    def total(self):
        for made in self.pending:
            made.wait_recv()
        out = self.mine[...]
        for j in range(3):
            out = out + self.landed[j].astype(F32)
        return out


def norm_back(v, u, n):
    r = lax.rsqrt(jnp.sum(v * v, axis=-1, keepdims=True) * (1.0 / n) + EPS)
    inner = jnp.sum(u * v, axis=-1, keepdims=True) * (1.0 / n)
    return r, r * u - v * (r * r * r * inner)


def mlp_kernel(
    xs_h, middle_h, cot_h, gains, w_gate_h, w_up_h, w_down_h,
    layer_out, middle_grad, d_gain_in, d_gain_out, half_in, d_down_h,
    xs, middle, cot, w_gate, w_up, w_down, d_in, gs, act, slope, hidden, cross_f, cross_b, landed_f, landed_b, stage_core, stage_ring,
    mine, mixed_grad, d_down, swap, *rest,
):
    here = Place()
    moves = Moves(rest[-1])
    load_first = [
        moves.start(a, b)
        for a, b in ((xs_h.at[2], xs.at[2]), (w_gate_h, w_gate), (w_up_h, w_up), (w_down_h, w_down))
    ]
    load_xs = {r: moves.start(xs_h.at[r], xs.at[r]) for r in (3, 1, 0)}
    load_last = [moves.start(a, b) for a, b in ((middle_h, middle), (cot_h, cot))]
    greet([here.mate()] + [here.to(dx=d) for d in (1, 2, 3)] + plane_peers(here))
    lines = Lines(*rest[-3:-1])
    n, width = middle.shape
    gain_in, gain_out = gains[2:3, :width], gains[3:4, :width]

    sums = RingSum(here, lines, mine, landed_f, cross_f, stage_core, stage_ring)
    in_sum = PlaneSum(here, lines, d_in, *rest[:8])

    def forward(r):
        x = xs[r]
        a, s, h = gate_terms(dot(x, w_gate[...]), dot(x, w_up[...]))
        act[r] = a.astype(BF16)
        slope[r] = s.astype(BF16)
        hidden[r] = h.astype(BF16)
        sums.add(r, lambda q: dot(hidden[r, q * n : (q + 1) * n], w_down[...]))

    for made in load_first:
        made.wait()
    forward(2)
    for r in (3, 1, 0):
        load_xs[r].wait()
        forward(r)
    for made in load_last:
        made.wait()
    mixed = sums.total()
    lines.drain()

    cot_f = cot[...].astype(F32)
    u = cot_f * (1.0 + gain_out)
    factor, grad = norm_back(mixed, u, width)
    layer_out[...] = (middle[...] + mixed * factor * (1.0 + gain_out)).astype(BF16)
    d_gain_out[...] = jnp.sum(cot_f * mixed * factor, axis=0, keepdims=True)
    mixed_grad[...] = grad.astype(BF16)

    ring = RingGather(here, lines, mixed_grad, gs)
    sums = RingSum(here, lines, mine, landed_b, cross_b, stage_core, stage_ring)
    ring.start()

    def backward(r):
        hidden_grad = dot(gs[r], w_down[...], NT)
        act[r] = (hidden_grad * act[r].astype(F32)).astype(BF16)
        slope[r] = (hidden_grad * slope[r].astype(F32)).astype(BF16)

        def term(q):
            rows = slice(q * n, (q + 1) * n)
            return dot(slope[r, rows], w_gate[...], NT) + dot(act[r, rows], w_up[...], NT)

        sums.add(r, term)

    ring.ready0()
    backward(0)
    ring.relay()
    ring.forward()
    ring.ready3()
    backward(3)
    ring.ready1()
    backward(1)
    ring.ready2()
    backward(2)

    flat = lambda ref: ref[...].reshape(ref.shape[0] * ref.shape[1], ref.shape[2])
    for mat, side in ((0, slope), (1, act)):
        grad_side = dot(flat(xs), flat(side), TN)
        for f in range(16):
            d_in[f // 4, (f // 2) % 2, mat, f % 2] = grad_side[72 * f : 72 * f + 72].astype(BF16)
    in_sum.first()
    grad_down = dot(flat(hidden), flat(gs), TN)
    for k in range(8):
        for p in range(4):
            rows = min(32, PART - 32 * p)
            at = PART * k + 32 * p
            d_down[k // 2, k % 2, p // 2, p % 2, :rows] = grad_down[at : at + rows].astype(BF16)
        d_down[k // 2, k % 2, 1, 1, PART - 96 :] = jnp.zeros((128 - PART, width), BF16)
    moves.store(d_down, d_down_h)
    in_sum.middle()

    update = sums.total()
    base = middle[...]
    u = update * (1.0 + gain_in)
    factor, grad = norm_back(base, u, width)
    d_gain_in[...] = jnp.sum(update * base * factor, axis=0, keepdims=True)
    middle_grad[...] = cot[...].astype(F32) + grad
    in_sum.second()
    for path in (0, 1):
        swap[path] = in_sum.result(path).astype(BF16)
    across = lines.copy(swap.at[1 - here.c], half_in.at[here.c], here.mate())
    half_in[here.c] = swap[here.c]
    across.wait_recv()
    lines.drain()
    moves.drain()


def mlp_block(xs, middle, cot, gains, w_gate, w_up, w_down):
    n, width = middle.shape
    units = w_gate.shape[1]
    vmem, hbm = pl.BlockSpec(memory_space=pltpu.VMEM), pl.BlockSpec(memory_space=pl.ANY)
    shape = jax.ShapeDtypeStruct
    d_in = shape((4, 2, 2, 2, width // 16, units), BF16)
    d_down = shape((4, 2, 2, 2, 32, width), BF16)
    scratch = (
        [pltpu.VMEM(a.shape, a.dtype) for a in (xs, middle, cot, w_gate, w_up, w_down, d_in)]
        + [pltpu.VMEM((4, 2 * n, width), BF16)]
        + [pltpu.VMEM((4, 2 * n, units), BF16)] * 3
        + [pltpu.VMEM((4, n, width), BF16)] * 2
        + [pltpu.VMEM((3, n, width), BF16)] * 2
        + [pltpu.VMEM((4, n, width), BF16), pltpu.VMEM((3, n, width), BF16)]
        + [pltpu.VMEM((n, width), F32), pltpu.VMEM((n, width), BF16)]
        + [pltpu.VMEM(d_down.shape, BF16), pltpu.VMEM((2, *d_in.shape[4:]), BF16)]
        + PlaneSum.scratch(d_in.shape[4:])
        + [pltpu.SemaphoreType.DMA((43,))] * 2
        + [pltpu.SemaphoreType.DMA((10,))]
    )
    return pl.pallas_call(
        mlp_kernel,
        out_shape=(
            shape((n, width), BF16),
            shape((n, width), F32),
            shape((1, width), F32),
            shape((1, width), F32),
            shape((2, *d_in.shape[4:]), BF16),
            d_down,
        ),
        in_specs=[hbm] * 3 + [vmem] + [hbm] * 3,
        out_specs=(vmem,) * 5 + (hbm,),
        scratch_shapes=scratch,
        compiler_params=pltpu.CompilerParams(
            collective_id=1, has_side_effects=True, vmem_limit_bytes=63 * MIB
        ),
        name="mlp_block",
    )(xs, middle, cot, gains, w_gate, w_up, w_down)


def plane_peers(here):
    return [here.to(dz=d) for d in (1, 2, 3)] + [here.to(dy=d) for d in (1, 2, 3)]


class PlaneGather:
    def __init__(self, here, lines, local, own, full):
        self.here, self.lines, self.local, self.own, self.full = here, lines, local, own, full

    def first(self):
        here, own, full, copy = self.here, self.own, self.full, self.lines.copy
        z, yh, yl = here.z, here.yh, here.yl
        keep = pltpu.make_async_copy(own.at[yl], full.at[z, yh, yl], self.local)
        keep.start()
        self.a, self.b = [], []
        for d in (1, 3, 2):
            self.a.append(copy(own.at[yl, 0], full.at[z, yh, yl, 0], here.to(dz=d)))
            self.b.append(copy(own.at[yl, 1], full.at[z, yh, yl, 1], here.to(dy=d)))
        keep.wait()

    def blocks(self, dy, dz):
        _, shard, yl = self.here.to(dy=dy)
        yh = lax.rem(shard // 2, 2)
        z = self.here.to(dz=dz)[1] // 4
        full = self.full
        return (
            [full.at[pl.ds(0, 2), yh, yl, 0], full.at[pl.ds(2, 2), yh, yl, 0]],
            [full.at[z, 0, :, 1], full.at[z, 1, :, 1]],
        )

    def second(self):
        here, copy = self.here, self.lines.copy
        for made in self.a + self.b:
            made.wait_recv()
        by_y, by_z = self.blocks(0, 0)
        self.early, self.late = [], []
        for block, up, down in (
            (by_y, here.to(dy=1), here.to(dy=3)),
            (by_z, here.to(dz=1), here.to(dz=3)),
        ):
            self.early.append(copy(block[0], block[0], up))
            self.early.append(copy(block[1], block[1], down))
        for block, up, down in (
            (by_y, here.to(dy=1), here.to(dy=3)),
            (by_z, here.to(dz=1), here.to(dz=3)),
        ):
            self.late.append(copy(block[1], block[1], up))
            self.late.append(copy(block[0], block[0], down))

    def relay(self):
        here, copy = self.here, self.lines.copy
        left_y, left_z = self.blocks(3, 3)
        right_y, right_z = self.blocks(1, 1)
        for made, block, to in zip(
            self.early,
            (left_y[0], right_y[1], left_z[0], right_z[1]),
            (here.to(dy=1), here.to(dy=3), here.to(dz=1), here.to(dz=3)),
        ):
            made.wait_recv()
            self.late.append(copy(block, block, to))

    def wait(self):
        for made in self.late:
            made.wait_recv()


def head_forward(pre, scale, cosine, sine, factor):
    r = lax.rsqrt(jnp.mean(pre * pre, axis=-1, keepdims=True) + EPS)
    v = pre * r * (1.0 + scale)
    half = v.shape[1] // 2
    a, b = v[:, :half], v[:, half:]
    turned = jnp.concatenate([a * cosine - b * sine, b * cosine + a * sine], axis=1)
    return (turned * factor).astype(BF16)


def head_backward(grad, pre, scale, cosine, sine, factor):
    grad = grad * factor
    half = grad.shape[1] // 2
    a, b = grad[:, :half], grad[:, half:]
    dy = jnp.concatenate([a * cosine + b * sine, b * cosine - a * sine], axis=1)
    r, out = norm_back(pre, dy * (1.0 + scale), pre.shape[1])
    return out.astype(BF16), jnp.sum(dy * pre * r, axis=0, keepdims=True)


def attend_kernel(
    tokens, cosine, sine, tail, w_query, w_key, w_value, own_out, w_gate, w_up, w_down,
    *refs,
):
    kept = refs[:14]
    gains = refs[14]
    held = refs[15:29]
    (
        xs, gate_full, up_full, down_full, w_qkv, w_out, normed, queries, kv, probs, context,
        attended, qkv_pre, middle,
    ) = held
    mlp_in, own_qkv, own_in, own_down, full_qkv, full_in, full_down, chip_in = refs[29:37]
    send, recv, local, moved = refs[37:]
    moves = Moves(moved)
    place = {id(a): b for a, b in zip(held, kept)}
    keep = lambda ref: moves.store(ref, place[id(ref)])
    here = Place()
    x_at, c, yl = here.x, here.c, here.yl
    n, width = tokens.shape
    rows, units = w_gate.shape
    block = units // 16
    head_dim = w_key.shape[1]
    at = w_query.shape[1]
    heads = at // head_dim
    wide = own_qkv.shape[-1]
    lines = Lines(send, recv)
    gather = [
        PlaneGather(here, lines, local.at[k], own, full)
        for k, (own, full) in enumerate(
            (
                (own_qkv, full_qkv.at[:, :, c]),
                (own_out, w_out.at[:, :, c]),
                (chip_in, full_in),
                (own_down, full_down),
            )
        )
    ]

    sides = [(w_query, 0), (w_key, at), (w_value, at + head_dim)]
    for p in range(4):
        for side, start in sides:
            lo, hi = max(p * wide, start), min((p + 1) * wide, start + side.shape[1])
            if lo < hi:
                own_qkv[p // 2, p % 2, :rows, lo - p * wide : hi - p * wide] = side[
                    :, lo - start : hi - start
                ]
        own_qkv[p // 2, p % 2, rows:] = tail[:, p * wide : (p + 1) * wide]
    greet([here.mate()] + plane_peers(here) + [here.to(dx=d) for d in (1, 2, 3)])
    gather[0].first()
    gather[1].first()
    lane = lax.broadcasted_iota(jnp.int32, (rows, PART), 1)
    inside = lane < block - x_at * PART
    for mat, weight in ((0, w_gate), (1, w_up)):
        turned = pltpu.roll(weight[...].astype(F32), lax.rem(units - PART * x_at, units), 1)
        for core in range(2):
            parts = [
                jnp.where(inside, turned[:, block * f : block * f + PART], 0.0)
                for f in range(core, 16, 2)
            ]
            own_in[core, mat] = jnp.concatenate(parts, axis=1).astype(BF16)
    across = lines.copy(own_in.at[1 - c], chip_in.at[:, c], here.mate())
    chip_in[:, c] = own_in[c]
    gather[0].second()
    for p in range(3):
        start = pl.multiple_of(PART * x_at + 32 * p, 16)
        own_down[p // 2, p % 2] = w_down[pl.ds(start, 32)]
    start = pl.multiple_of(jnp.minimum(PART * x_at + 96, block - 16), 16)
    last = w_down[pl.ds(start, 16)].astype(F32)
    own_down[1, 1, :16] = jnp.where(x_at < 3, last, 0.0).astype(BF16)
    own_down[1, 1, 16:] = jnp.zeros((16, width), BF16)
    x = tokens[...].astype(F32)
    lean = x * lax.rsqrt(jnp.mean(x * x, axis=-1, keepdims=True) + EPS)
    gather[0].relay()
    gather[1].second()
    across.wait_recv()
    gather[2].first()
    gather[0].wait()
    core_qkv = [
        lines.copy(full_qkv.at[:, :, c, k], full_qkv.at[:, :, c, k], here.mate()) for k in (0, 1)
    ]
    for p in range(4):
        if p % 2 == 0:
            core_qkv[p // 2].wait_recv()
        if p == 1:
            gather[1].relay()
            gather[2].second()
        total = jnp.zeros((8, wide), F32)
        cols = slice(p * wide, (p + 1) * wide)
        for f in range(16):
            part = full_qkv[f // 4, (f // 2) % 2, f % 2, p // 2, p % 2]
            w_qkv[rows * f : rows * f + rows, cols] = part[:rows]
            total = total + part.astype(F32)[rows : rows + 8]
        gains[:, cols] = total
    keep(w_qkv)
    normed[...] = (lean * (1.0 + gains[0:1, :width])).astype(BF16)
    qkv_pre[...] = dot(normed[...], w_qkv[...])
    cos_v, sin_v = cosine[...], sine[...]
    q_scale, k_scale = (gains[k : k + 1, width : width + head_dim] for k in (0, 1))
    key = head_forward(qkv_pre[:, at : at + head_dim], k_scale, cos_v, sin_v, 1.0)
    kv[yl, :, :head_dim] = key
    kv[yl, :, head_dim:] = qkv_pre[:, at + head_dim :].astype(BF16)
    kv_sent = lines.copy(kv.at[yl], kv.at[yl], here.pair())
    keep(normed)
    keep(qkv_pre)
    for h in range(heads):
        cols = slice(h * head_dim, (h + 1) * head_dim)
        queries[:, cols] = head_forward(qkv_pre[:, cols], q_scale, cos_v, sin_v, head_dim**-0.5)
    gather[1].wait()
    core_out = lines.copy(w_out.at[:, :, c], w_out.at[:, :, c], here.mate())
    kv_sent.wait_recv()
    keep(queries)
    keep(kv)
    keys = kv[:, :, :head_dim].reshape(2 * n, head_dim)
    values = kv[:, :, head_dim:].reshape(2 * n, head_dim)
    row = lax.broadcasted_iota(jnp.int32, (n, 2 * n), 0) + yl * n
    allowed = lax.broadcasted_iota(jnp.int32, (n, 2 * n), 1) <= row
    for h in range(heads):
        if h == 1:
            gather[3].first()
        cols = slice(h * head_dim, (h + 1) * head_dim)
        scores = jnp.where(allowed, dot(queries[:, cols], keys, NT), -1e30)
        terms = jnp.exp(scores - jnp.max(scores, axis=-1, keepdims=True))
        low = (terms * (1.0 / jnp.sum(terms, axis=-1, keepdims=True))).astype(BF16)
        probs[h] = low
        context[:, cols] = dot(low, values).astype(BF16)
    core_out.wait_recv()
    att = dot(context[...], w_out[...].reshape(at, width))
    attended[...] = att
    r = lax.rsqrt(jnp.mean(att * att, axis=-1, keepdims=True) + EPS)
    mid = x + att * r * (1.0 + gains[1:2, :width])
    middle[...] = mid
    r = lax.rsqrt(jnp.mean(mid * mid, axis=-1, keepdims=True) + EPS)
    mlp_in[...] = (mid * r * (1.0 + gains[2:3, :width])).astype(BF16)
    ring = RingGather(here, lines, mlp_in, xs)
    ring.start()
    gather[2].relay()
    gather[3].second()
    for ref in (probs, context, w_out, attended, middle):
        keep(ref)
    ring.relay()
    gather[2].wait()
    for f in range(16):
        for mat, whole in ((0, gate_full), (1, up_full)):
            whole[rows * f : rows * f + rows] = full_in[f // 4, (f // 2) % 2, mat, f % 2]
    keep(gate_full)
    keep(up_full)
    ring.forward()
    gather[3].relay()
    ring.ready0()
    gather[3].wait()
    for k in range(8):
        for p in range(4):
            count = min(32, PART - 32 * p)
            down_full[PART * k + 32 * p : PART * k + 32 * p + count] = full_down[
                k // 2, k % 2, p // 2, p % 2, :count
            ]
    keep(down_full)
    ring.ready3()
    ring.ready1()
    ring.ready2()
    keep(xs)
    lines.drain()
    moves.drain()


def attend_block(tokens, cosine, sine, tail, w_query, w_key, w_value, own_out, w_gate, w_up, w_down):
    n, width = tokens.shape
    vmem = pl.BlockSpec(memory_space=pltpu.VMEM)
    shape = jax.ShapeDtypeStruct
    low = lambda *s: shape(s, BF16)
    rows, out_width = w_query.shape
    head_dim, cols = w_key.shape[1], tail.shape[1]
    p_qkv, p_out = (rows + 8, cols // 4), own_out.shape[2:]
    p_in, p_down = (rows, CORE_UNITS), (32, width)
    vm = lambda *s: pltpu.VMEM(s, BF16)
    held = (
        low(4, 2 * n, width),
        low(width, CORE_UNITS),
        low(width, CORE_UNITS),
        low(CORE_UNITS, width),
        low(width, cols),
        low(4, 2, 2, 2, 2, *p_out),
        low(n, width),
        low(n, out_width),
        low(2, n, 2 * head_dim),
        low(out_width // head_dim, n, 2 * n),
        low(n, out_width),
        shape((n, width), F32),
        shape((n, cols), F32),
        shape((n, width), F32),
    )
    return pl.pallas_call(
        attend_kernel,
        out_shape=held + (shape((8, cols), F32),),
        in_specs=[vmem] * 11,
        out_specs=(pl.BlockSpec(memory_space=pl.ANY),) * 14 + (vmem,),
        scratch_shapes=[pltpu.VMEM(a.shape, a.dtype) for a in held]
        + [
            vm(n, width),
            vm(2, 2, *p_qkv),
            vm(2, 2, *p_in),
            vm(2, 2, *p_down),
            vm(4, 2, 2, 2, 2, *p_qkv),
            vm(4, 2, 2, 2, *p_in),
            vm(4, 2, 2, 2, *p_down),
            vm(2, 2, *p_in),
            pltpu.SemaphoreType.DMA((87,)),
            pltpu.SemaphoreType.DMA((87,)),
            pltpu.SemaphoreType.DMA((4,)),
            pltpu.SemaphoreType.DMA((14,)),
        ],
        compiler_params=pltpu.CompilerParams(
            collective_id=0, has_side_effects=True, vmem_limit_bytes=62 * MIB
        ),
        name="attend",
    )(tokens, cosine, sine, tail, w_query, w_key, w_value, own_out, w_gate, w_up, w_down)


class PlaneSum:
    def __init__(
        self, here, lines, grads, landed_a, half_a, sums_a, landed_b, half_b, sums_b, last_a, last_b
    ):
        self.here, self.lines, self.grads = here, lines, grads
        self.landed_a, self.half_a, self.sums_a, self.last_a = landed_a, half_a, sums_a, last_a
        self.landed_b, self.half_b, self.sums_b, self.last_b = landed_b, half_b, sums_b, last_b

    @staticmethod
    def scratch(piece):
        vm = lambda *lead: pltpu.VMEM((*lead, *piece), BF16)
        return [vm(2, 4), vm(2, 2), vm(4), vm(2, 2, 2), vm(2, 2), vm(2, 2), vm(3), vm(3)]

    def spots(self, d):
        _, shard, yl = self.here.to(dy=d)
        yh = lax.rem(shard // 2, 2)
        z = self.here.to(dz=d)[1] // 4
        low, high = pl.ds(0, 2), pl.ds(2, 2)
        return ((low, yh, yl, 0), (high, yh, yl, 0)), ((z, 0, slice(None), 1), (z, 1, slice(None), 1))

    def first(self):
        here, g, copy = self.here, self.grads, self.lines.copy
        up_y, down_y, up_z, down_z = here.to(dy=1), here.to(dy=3), here.to(dz=1), here.to(dz=3)
        low, high = pl.ds(0, 2), pl.ds(2, 2)
        a, b = self.spots(2)
        self.half = [
            copy(g.at[a[0]], self.half_a.at[0], up_y),
            copy(g.at[a[1]], self.half_a.at[1], down_y),
            copy(g.at[b[0]], self.half_b.at[0], up_z),
            copy(g.at[b[1]], self.half_b.at[1], down_z),
        ]
        (a1, b1), (a3, b3) = self.spots(1), self.spots(3)
        self.a = [
            copy(g.at[a1[1]], self.landed_a.at[0, high], up_y),
            copy(g.at[a3[0]], self.landed_a.at[1, low], down_y),
        ]
        self.b = [
            copy(g.at[b1[1]], self.landed_b.at[0, 1], up_z),
            copy(g.at[b3[0]], self.landed_b.at[1, 0], down_z),
        ]

    def middle(self):
        here, g, copy = self.here, self.grads, self.lines.copy
        low, high = pl.ds(0, 2), pl.ds(2, 2)
        (a1, b1), (a3, b3) = self.spots(1), self.spots(3)
        for made, spot, half in zip(
            self.half,
            (a1[0], a3[1], b1[0], b3[1]),
            (self.half_a.at[0], self.half_a.at[1], self.half_b.at[0], self.half_b.at[1]),
        ):
            made.wait_recv()
            g[spot] = (g[spot].astype(F32) + half[...].astype(F32)).astype(BF16)
        self.a += [
            copy(g.at[a1[0]], self.landed_a.at[0, low], here.to(dy=1)),
            copy(g.at[a3[1]], self.landed_a.at[1, high], here.to(dy=3)),
        ]
        self.b += [
            copy(g.at[b1[0]], self.landed_b.at[0, 0], here.to(dz=1)),
            copy(g.at[b3[1]], self.landed_b.at[1, 1], here.to(dz=3)),
        ]

    def second(self):
        here, g, copy = self.here, self.grads, self.lines.copy
        for made in self.a:
            made.wait_recv()
        for k in range(4):
            total = g[k, here.yh, here.yl, 0].astype(F32)
            for j in range(2):
                total = total + self.landed_a[j, k].astype(F32)
            self.sums_a[k] = total.astype(BF16)
        self.a = []
        for d in (1, 3, 2):
            z = here.to(dz=d)[1] // 4
            self.a.append(copy(self.sums_a.at[z], self.last_a.at[d - 1], here.to(dz=d)))
        for made in self.b:
            made.wait_recv()
        for k in range(4):
            total = g[here.z, k // 2, k % 2, 1].astype(F32)
            for j in range(2):
                total = total + self.landed_b[j, k // 2, k % 2].astype(F32)
            self.sums_b[k // 2, k % 2] = total.astype(BF16)
        self.b = []
        for d in (1, 3, 2):
            _, shard, yl = here.to(dy=d)
            yh = lax.rem(shard // 2, 2)
            self.b.append(copy(self.sums_b.at[yh, yl], self.last_b.at[d - 1], here.to(dy=d)))

    def result(self, path):
        here = self.here
        for made in (self.a, self.b)[path]:
            made.wait_recv()
        own = self.sums_a[here.z] if path == 0 else self.sums_b[here.yh, here.yl]
        last = (self.last_a, self.last_b)[path]
        total = own.astype(F32)
        for j in range(3):
            total = total + last[j].astype(F32)
        return total


def retreat_kernel(
    middle_grad_h, attended_h, context_h, probs_h, kv_h, queries_h, qkv_pre_h, normed_h, tokens_h,
    w_qkv_h, w_out_h, g_down_h, cosine, sine, gains, d_gain_in, d_gain_out, half_in,
    grad_tokens, o_in, o_down, o_qkv, o_out,
    middle_grad, attended, context, probs, kv, queries, qkv_pre, normed, tokens, w_qkv, w_out,
    g_down,
    context_grad, attn_side, kv_part, kv_give, kv_land, g_qkv, g_out, d_gains,
    chip_qkv, chip_out, cross_qkv, cross_out, half_qkv, half_out, land_qkv, land_out, *rest,
):
    here = Place()
    send, recv, moved = rest[-3:]
    x, yl, c = here.x, here.yl, here.c
    moves = Moves(moved)
    loads = {
        name: moves.start(a, b)
        for name, a, b in (
            ("g_down", g_down_h, g_down),
            ("attended", attended_h, attended),
            ("middle_grad", middle_grad_h, middle_grad),
            ("w_out", w_out_h, w_out),
            ("context", context_h, context),
            ("probs", probs_h, probs),
            ("kv", kv_h, kv),
            ("queries", queries_h, queries),
            ("qkv_pre", qkv_pre_h, qkv_pre),
            ("w_qkv", w_qkv_h, w_qkv),
            ("normed", normed_h, normed),
            ("tokens", tokens_h, tokens),
        )
    }

    def ready(*names):
        for name in names:
            loads[name].wait()

    greet([here.mate()] + plane_peers(here) + [here.to(dx=d) for d in (1, 2, 3)])
    lines = Lines(send, recv)
    copy = lines.copy
    n, width = middle_grad.shape
    head_dim = 2 * cosine.shape[1]
    heads = queries.shape[1] // head_dim
    rows = width // 16
    at = heads * head_dim
    sums = [
        PlaneSum(here, lines, g, *rest[8 * k : 8 * k + 8])
        for k, g in enumerate((g_down, chip_qkv, chip_out))
    ]
    o_in[x, yl] = half_in[...]
    in_pair = copy(half_in, o_in.at[x, yl], here.pair())
    ready("g_down")
    sums[0].first()
    ready("attended", "middle_grad", "w_out", "context")

    att, dy = attended[...], middle_grad[...]
    r, grad = norm_back(att, dy * (1.0 + gains[1:2, :width]), width)
    d_gains[...] = jnp.zeros_like(d_gains)
    d_gains[1:2, :width] = jnp.sum(dy * att * r, axis=0, keepdims=True)
    d_gains[2:3, :width] = d_gain_in[...]
    d_gains[3:4, :width] = d_gain_out[...]
    attended_grad = grad.astype(BF16)
    out_full = w_out[...].reshape(at, width)
    context_grad[...] = dot(attended_grad, out_full, NT).astype(BF16)
    grad_out = dot(context[...], attended_grad, TN)
    g_out[...] = grad_out.astype(BF16).reshape(g_out.shape)
    give_out = copy(g_out.at[:, :, 1 - c], cross_out, here.mate())
    in_pair.wait_recv()
    right, left = here.to(dx=1), here.to(dx=3)
    own = [o_in.at[x, m] for m in (0, 1)]
    early = [copy(own[0], own[0], right), copy(own[1], own[1], left)]
    late = [copy(own[1], own[1], right), copy(own[0], own[0], left)]
    sums[0].middle()

    ready("probs", "kv", "queries", "qkv_pre")
    keys = kv[:, :, :head_dim].reshape(2 * n, head_dim)
    values = kv[:, :, head_dim:].reshape(2 * n, head_dim)
    cos_v, sin_v = cosine[...], sine[...]
    q_scale, k_scale = (gains[k : k + 1, width : width + head_dim] for k in (0, 1))
    d_query = jnp.zeros((1, head_dim), F32)
    for h in range(heads):
        cols = slice(h * head_dim, (h + 1) * head_dim)
        low = probs[h]
        high = low.astype(F32)
        prob_grad = dot(context_grad[:, cols], values, NT)
        inner = jnp.sum(high * prob_grad, axis=-1, keepdims=True)
        score_grad = (high * (prob_grad - inner)).astype(BF16)
        key_part = dot(score_grad, queries[:, cols], TN)
        value_part = dot(low, context_grad[:, cols], TN)
        if h == 0:
            kv_part[:, :, :head_dim] = key_part.reshape(2, n, head_dim)
            kv_part[:, :, head_dim:] = value_part.reshape(2, n, head_dim)
        else:
            kv_part[:, :, :head_dim] += key_part.reshape(2, n, head_dim)
            kv_part[:, :, head_dim:] += value_part.reshape(2, n, head_dim)
        query_grad = dot(score_grad, keys).astype(BF16).astype(F32)
        side, d_scale = head_backward(
            query_grad, qkv_pre[:, cols], q_scale, cos_v, sin_v, head_dim**-0.5
        )
        attn_side[:, cols] = side
        d_query = d_query + d_scale
    kv_give[...] = kv_part[1 - yl].astype(BF16)
    kv_sent = copy(kv_give, kv_land, here.pair())
    give_out.wait_recv()
    for z in range(4):
        for yh in range(2):
            chip_out[z, yh] = (g_out[z, yh, c].astype(F32) + cross_out[z, yh].astype(F32)).astype(BF16)
    sums[2].first()
    sums[0].second()
    kv_sent.wait_recv()
    kv_grad = (kv_part[yl] + kv_land[...].astype(F32)).astype(BF16)
    side, d_key = head_backward(
        kv_grad[:, :head_dim].astype(F32), qkv_pre[:, at : at + head_dim], k_scale, cos_v, sin_v, 1.0
    )
    attn_side[:, at : at + head_dim] = side
    attn_side[:, at + head_dim :] = kv_grad[:, head_dim:]
    d_gains[0:1, width : width + head_dim] = d_query
    d_gains[1:2, width : width + head_dim] = d_key

    ready("w_qkv", "normed", "tokens")
    normed_grad = dot(attn_side[...], w_qkv[...], NT)
    tok = tokens[...].astype(F32)
    r, grad = norm_back(tok, normed_grad * (1.0 + gains[0:1, :width]), width)
    grad_tokens[...] = (middle_grad[...] + grad).astype(BF16)
    d_gains[0:1, :width] = jnp.sum(normed_grad * tok * r, axis=0, keepdims=True)
    grad_qkv = dot(normed[...], attn_side[...], TN)
    for p in range(4):
        cols = slice(p * g_qkv.shape[-1], (p + 1) * g_qkv.shape[-1])
        tail = d_gains[:, cols].astype(BF16)
        for f in range(16):
            spot = (f // 4, (f // 2) % 2, f % 2, p // 2, p % 2)
            block = jnp.concatenate(
                [grad_qkv[rows * f : rows * f + rows, cols], d_gains[:, cols]], axis=0
            )
            g_qkv[spot] = block.astype(BF16)
    give_qkv = copy(g_qkv.at[:, :, 1 - c], cross_qkv, here.mate())

    for made, at_x, m, to in ((early[0], left[0], 0, right), (early[1], right[0], 1, left)):
        made.wait_recv()
        late.append(copy(o_in.at[at_x, m], o_in.at[at_x, m], to))
    give_qkv.wait_recv()
    for z in range(4):
        for yh in range(2):
            chip_qkv[z, yh] = (g_qkv[z, yh, c].astype(F32) + cross_qkv[z, yh].astype(F32)).astype(BF16)
    sums[1].first()
    for path in (0, 1):
        o_down[x, yl, path] = sums[0].result(path).astype(BF16)
    down_pair = copy(o_down.at[x, yl], o_down.at[x, yl], here.pair())
    sums[2].middle()
    sums[1].middle()
    down_pair.wait_recv()
    down_x = [copy(o_down.at[x], o_down.at[x], here.to(dx=d)) for d in (1, 3, 2)]
    sums[2].second()
    for path in (0, 1):
        half_out[path] = sums[2].result(path).astype(BF16)
    by_x = [copy(half_out, land_out.at[d - 1], here.to(dx=d)) for d in (1, 3, 2)]
    sums[1].second()
    for path in (0, 1):
        half_qkv[path] = sums[1].result(path).astype(BF16)
    by_x += [copy(half_qkv, land_qkv.at[d - 1], here.to(dx=d)) for d in (1, 3, 2)]
    for made in by_x:
        made.wait_recv()
    for half, land, out in ((half_qkv, land_qkv, o_qkv), (half_out, land_out, o_out)):
        for path in (0, 1):
            total = half[path].astype(F32)
            for j in range(3):
                total = total + land[j, path].astype(F32)
            out[yl, path] = total.astype(BF16)
    ends = [copy(o.at[yl], o.at[yl], here.pair()) for o in (o_qkv, o_out)]
    for made in down_x + late + ends:
        made.wait_recv()
    lines.drain()


def retreat_block(*args):
    (
        middle_grad, attended, context, probs, kv, queries, qkv_pre, normed, tokens, w_qkv, w_out,
        g_down, cosine, _, _, _, _, half_in,
    ) = args
    vmem, hbm = pl.BlockSpec(memory_space=pltpu.VMEM), pl.BlockSpec(memory_space=pl.ANY)
    shape = jax.ShapeDtypeStruct
    n, width = middle_grad.shape
    out_width, head_dim = queries.shape[1], 2 * cosine.shape[1]
    cols = qkv_pre.shape[1]
    p_in, p_down, p_out = half_in.shape[1:], g_down.shape[4:], w_out.shape[5:]
    p_qkv = (width // 16 + 8, cols // 4)
    vm = lambda *s: pltpu.VMEM(s, BF16)
    scratch = [pltpu.VMEM(a.shape, a.dtype) for a in args[:11]]
    scratch += [vm(*g_down.shape)]
    scratch += [vm(n, out_width), vm(n, cols), pltpu.VMEM((2, n, 2 * head_dim), F32)]
    scratch += [vm(n, 2 * head_dim)] * 2
    scratch += [vm(4, 2, 2, 2, 2, *p_qkv), vm(4, 2, 2, 2, 2, *p_out), pltpu.VMEM((8, cols), F32)]
    scratch += [vm(4, 2, 2, 2, *p_qkv), vm(4, 2, 2, 2, *p_out)] * 2
    scratch += [vm(2, *p_qkv), vm(2, *p_out), vm(3, 2, *p_qkv), vm(3, 2, *p_out)]
    for piece in (p_down, p_qkv, p_out):
        scratch += PlaneSum.scratch(piece)
    scratch += [pltpu.SemaphoreType.DMA((76,))] * 2 + [pltpu.SemaphoreType.DMA((12,))]
    low = lambda *s: shape(s, BF16)
    return pl.pallas_call(
        retreat_kernel,
        out_shape=(
            low(n, width),
            low(4, 2, 2, *p_in),
            low(4, 2, 2, *p_down),
            low(2, 2, *p_qkv),
            low(2, 2, *p_out),
        ),
        in_specs=[hbm] * 12 + [vmem] * 6,
        out_specs=(vmem,) * 5,
        scratch_shapes=scratch,
        compiler_params=pltpu.CompilerParams(
            collective_id=2, has_side_effects=True, vmem_limit_bytes=63 * MIB
        ),
        name="retreat",
    )(*args)


def finish_kernel(
    o_in_h, o_down_h, o_qkv_h, o_out_h, shown_h, taken_h,
    layer_out_h, grad_tokens_h, out_query, out_key, out_value, out_out, out_gate_h, out_up_h, out_down_h,
    *rest,
):
    out_gains = rest[:6]
    o_in, o_down, o_qkv, o_out, out_gate, out_up, out_down, shown, taken, moved = rest[6:]
    moves = Moves(moved)
    load_in = [moves.start(o_in_h.at[:, m], o_in.at[:, m]) for m in (0, 1)]
    load_tokens = [moves.start(shown_h, shown), moves.start(taken_h, taken)]
    load_down = moves.start(o_down_h, o_down)
    load_rest = [moves.start(o_qkv_h, o_qkv), moves.start(o_out_h, o_out)]
    rows, units = out_gate.shape
    block = units // 16
    wide = o_qkv.shape[-1]
    at, head_dim = out_query.shape[1], out_key.shape[1]
    for m, out, out_h in ((0, out_gate, out_gate_h), (1, out_up, out_up_h)):
        load_in[m].wait()
        for k in range(4):
            count = min(PART, block - PART * k)
            for f in range(16):
                piece = o_in[k, m, f % 2].astype(F32)[:, PART * (f // 2) : PART * (f // 2) + count]
                out[:, block * f + PART * k : block * f + PART * k + count] = piece
        moves.store(out, out_h)
    for made, held, out_h in zip(load_tokens, (shown, taken), (layer_out_h, grad_tokens_h)):
        made.wait()
        moves.store(held, out_h)
    load_down.wait()
    for k in range(4):
        for p in range(4):
            start = PART * k + 32 * p
            count = min(32, PART - 32 * p, block - start)
            if count > 0:
                out_down[start : start + count] = o_down[k, p // 2, p % 2, :count].astype(F32)
    moves.store(out_down, out_down_h)
    for made in load_rest:
        made.wait()
    tail = []
    for p in range(4):
        piece = o_qkv[p // 2, p % 2].astype(F32)
        for out, start in ((out_query, 0), (out_key, at), (out_value, at + head_dim)):
            lo, hi = max(p * wide, start), min((p + 1) * wide, start + out.shape[1])
            if lo < hi:
                out[:, lo - start : hi - start] = piece[:rows, lo - p * wide : hi - p * wide]
        tail.append(piece[rows:])
        height = o_out.shape[2]
        out_out[p * height : (p + 1) * height] = o_out[p // 2, p % 2].astype(F32)
    tail = jnp.concatenate(tail, axis=1)
    width = out_out.shape[1]
    shard = lax.axis_index("fsdp")
    turned = pltpu.roll(tail[:, :width], lax.rem(width - rows * shard, width), 1)
    for k in range(4):
        out_gains[k][...] = turned[k, :rows]
    piece = head_dim // 16
    turned = pltpu.roll(tail[:, width : width + head_dim], lax.rem(head_dim - piece * shard, head_dim), 1)
    for k in range(2):
        out_gains[4 + k][...] = turned[k, :piece]
    moves.drain()


def finish_block(o_in, o_down, o_qkv, o_out, layer_out, grad_tokens, out_shape):
    vmem, hbm = pl.BlockSpec(memory_space=pltpu.VMEM), pl.BlockSpec(memory_space=pl.ANY)
    big = out_shape[6:9]
    return pl.pallas_call(
        finish_kernel,
        out_shape=out_shape,
        in_specs=[hbm] * 6,
        out_specs=(hbm,) * 2 + (vmem,) * 4 + (hbm,) * 3 + (vmem,) * 6,
        scratch_shapes=[pltpu.VMEM(a.shape, a.dtype) for a in (o_in, o_down, o_qkv, o_out, *big, layer_out, grad_tokens)]
        + [pltpu.SemaphoreType.DMA((12,))],
        compiler_params=pltpu.CompilerParams(vmem_limit_bytes=62 * MIB),
        name="finish",
    )(o_in, o_down, o_qkv, o_out, layer_out, grad_tokens)


def body(
    tokens,
    w_query,
    w_key,
    w_value,
    w_out,
    w_gate,
    w_up,
    w_down,
    pre_attn_gain,
    post_attn_gain,
    pre_mlp_gain,
    post_mlp_gain,
    query_gain,
    key_gain,
    cotangent,
):
    n, width = tokens.shape
    rows = w_query.shape[0]
    head_dim = w_key.shape[1]
    out_width = w_query.shape[1]
    shard = lax.axis_index("fsdp")

    mine = jnp.arange(16) == shard
    spread = lambda g: jnp.where(mine[:, None], g[None, :], 0).reshape(1, -1)
    gains_d = [spread(g) for g in (pre_attn_gain, post_attn_gain, pre_mlp_gain, post_mlp_gain)]
    gains_h = jnp.concatenate([spread(query_gain), spread(key_gain)], axis=0)
    tail = jnp.concatenate(
        [
            jnp.pad(jnp.concatenate(gains_d, axis=0), ((0, 4), (0, 0))),
            jnp.pad(gains_h, ((0, 6), (0, out_width + head_dim - width))),
        ],
        axis=1,
    )
    own_out = w_out.reshape(2, 2, -1, width)
    positions = (lax.axis_index("seq") * n + jnp.arange(n, dtype=jnp.int32)).astype(F32)
    frequency = jnp.exp(
        jnp.arange(head_dim // 2, dtype=F32) * (-2.0 * math.log(1000000.0) / head_dim)
    )
    angles = positions[:, None] * frequency[None, :]
    cosine, sine = jnp.cos(angles), jnp.sin(angles)

    (
        xs, gate_full, up_full, down_full, w_qkv, w_out_full, normed, queries, kv, probs, context,
        attended, qkv_pre, middle, gains,
    ) = attend_block(
        tokens, cosine, sine, tail, w_query, w_key, w_value, own_out, w_gate, w_up, w_down
    )
    layer_out, middle_grad, d_gain_in, d_gain_out, half_in, g_down = mlp_block(
        xs, middle, cotangent, gains, gate_full, up_full, down_full
    )
    grad_tokens, o_in, o_down, o_qkv, o_out = retreat_block(
        middle_grad, attended, context, probs, kv, queries, qkv_pre, normed, tokens, w_qkv,
        w_out_full, g_down, cosine, sine, gains, d_gain_in, d_gain_out, half_in,
    )
    like = lambda a, kind: jax.ShapeDtypeStruct(a.shape, kind)
    weights = (w_query, w_key, w_value, w_out, w_gate, w_up, w_down)
    gain_args = (pre_attn_gain, post_attn_gain, pre_mlp_gain, post_mlp_gain, query_gain, key_gain)
    shapes = [like(tokens, BF16)] * 2 + [like(a, F32) for a in weights + gain_args]
    return tuple(finish_block(o_in, o_down, o_qkv, o_out, layer_out, grad_tokens, shapes))


def solution(mesh):
    tokens = P(("dp", "fsdp", "seq"), None)
    weight, gain = P("fsdp", None), P("fsdp")
    return jax.shard_map(
        body,
        mesh=mesh,
        in_specs=(tokens,) + (weight,) * 7 + (gain,) * 6 + (tokens,),
        out_specs=(tokens,) * 2 + (weight,) * 7 + (gain,) * 6,
        check_vma=False,
    )
```

```python
import functools
import math

import jax
import jax.numpy as jnp
from jax import lax
from jax.experimental import pallas as pl
from jax.experimental.pallas import tpu as pltpu
from jax.sharding import PartitionSpec as P

F32, BF16 = jnp.float32, jnp.bfloat16
MESH = pl.DeviceIdType.MESH
NN = (((1,), (0,)), ((), ()))
NT = (((1,), (1,)), ((), ()))
TN = (((0,), (0,)), ((), ()))
EPS = 1e-06
MIB = 2**20
PART = 112
CORE_UNITS = 8 * PART


def dot(a, b, dims=NN):
    return lax.dot_general(a, b, dims, preferred_element_type=F32)


class Place:
    def __init__(self):
        shard = lax.axis_index("fsdp")
        self.x = lax.axis_index("dp")
        self.z = shard // 4
        self.yh = lax.rem(shard // 2, 2)
        self.c = lax.rem(shard, 2)
        self.yl = lax.axis_index("seq")

    def to(self, dx=0, dy=0, dz=0, dc=0):
        x, z, yh, yl, c = self.x, self.z, self.yh, self.yl, self.c
        if dx:
            x = lax.rem(x + dx, 4)
        if dz:
            z = lax.rem(z + dz, 4)
        if dy:
            y = lax.rem(yh * 2 + yl + dy, 4)
            yh, yl = y // 2, lax.rem(y, 2)
        if dc:
            c = 1 - c
        return (x, (z * 2 + yh) * 2 + c, yl)

    def mate(self):
        return self.to(dc=1)

    def pair(self):
        return (self.x, (self.z * 2 + self.yh) * 2 + self.c, 1 - self.yl)


def greet(peers):
    barrier = pltpu.get_barrier_semaphore()
    for peer in peers:
        pl.semaphore_signal(barrier, inc=1, device_id=peer, device_id_type=MESH)
    pl.semaphore_wait(barrier, len(peers))


class Moves:
    def __init__(self, sems):
        self.sems, self.used, self.open = sems, 0, []

    def start(self, src, dst):
        made = pltpu.make_async_copy(src, dst, self.sems.at[self.used])
        self.used += 1
        made.start()
        return made

    def store(self, src, dst):
        self.open.append(self.start(src, dst))

    def drain(self):
        for made in self.open:
            made.wait()
        self.open = []


class Lines:
    def __init__(self, send, recv):
        self.send, self.recv, self.used, self.open = send, recv, 0, []

    def copy(self, src, dst, device):
        k = self.used
        self.used += 1
        made = pltpu.make_async_remote_copy(
            src_ref=src,
            dst_ref=dst,
            send_sem=self.send.at[k],
            recv_sem=self.recv.at[k],
            device_id=device,
            device_id_type=MESH,
        )
        made.start()
        self.open.append(made)
        return made

    def drain(self):
        for made in self.open:
            made.wait_send()
        self.open = []


def gate_terms(gate, up):
    k, c = math.sqrt(2.0 / math.pi), 0.044715
    square = gate * gate
    t = jnp.tanh(gate * (k + (k * c) * square))
    half = 0.5 + 0.5 * t
    act = gate * half
    slope = half + 0.5 * gate * (1.0 - t * t) * (k + (3.0 * k * c) * square)
    return act, slope * up, act * up


class RingGather:
    def __init__(self, here, lines, own, full):
        self.here, self.lines, self.own, self.full = here, lines, own, full

    def start(self):
        here, own, full, copy = self.here, self.own, self.full, self.lines.copy
        n = own.shape[0]
        h = n // 2
        right, left = here.to(dx=1), here.to(dx=3)
        lo, hi = pl.ds(0, h), pl.ds(h, h)
        self.core = copy(own, full.at[0, pl.ds(n, n)], here.mate())
        self.a0 = copy(own.at[lo], full.at[3, lo], right)
        self.b0 = copy(own.at[hi], full.at[1, hi], left)
        self.a1 = copy(own.at[hi], full.at[3, hi], right)
        self.b1 = copy(own.at[lo], full.at[1, lo], left)
        full[0, :n] = own[...]

    def start_low(self):
        here, own, full, copy = self.here, self.own, self.full, self.lines.copy
        lo = pl.ds(0, own.shape[0] // 2)
        self.a0 = copy(own.at[lo], full.at[3, lo], here.to(dx=1))
        self.b1 = copy(own.at[lo], full.at[1, lo], here.to(dx=3))

    def start_high(self):
        here, own, full, copy = self.here, self.own, self.full, self.lines.copy
        n = own.shape[0]
        hi = pl.ds(n // 2, n // 2)
        self.b0 = copy(own.at[hi], full.at[1, hi], here.to(dx=3))
        self.a1 = copy(own.at[hi], full.at[3, hi], here.to(dx=1))
        self.core = copy(own, full.at[0, pl.ds(n, n)], here.mate())
        full[0, :n] = own[...]

    def ready0(self):
        self.core.wait_recv()

    def relay(self):
        here, full, copy = self.here, self.full, self.lines.copy
        n = self.own.shape[0]
        h = n // 2
        lo, hi = pl.ds(0, h), pl.ds(h, h)
        right, left = here.to(dx=1), here.to(dx=3)
        self.a0.wait_recv()
        self.a2 = copy(full.at[3, lo], full.at[2, lo], right)
        self.b0.wait_recv()
        self.b2 = copy(full.at[1, hi], full.at[2, hi], left)

    def forward(self):
        full, copy = self.full, self.lines.copy
        n = self.own.shape[0]
        both, other = pl.ds(0, n), pl.ds(n, n)
        mate = self.here.mate()
        self.a1.wait_recv()
        self.f3 = copy(full.at[3, both], full.at[3, other], mate)
        self.b1.wait_recv()
        self.f1 = copy(full.at[1, both], full.at[1, other], mate)

    def ready3(self):
        self.f3.wait_recv()

    def ready1(self):
        self.f1.wait_recv()

    def ready2(self):
        n = self.own.shape[0]
        self.a2.wait_recv()
        self.b2.wait_recv()
        f2 = self.lines.copy(
            self.full.at[2, pl.ds(0, n)], self.full.at[2, pl.ds(n, n)], self.here.mate()
        )
        f2.wait_recv()


class RingSum:
    def __init__(self, here, lines, mine, landed, cross, stage_core, stage_ring):
        self.here, self.lines, self.mine = here, lines, mine
        self.landed, self.cross = landed, cross
        self.stage_core, self.stage_ring = stage_core, stage_ring
        self.pending = []

    def add(self, r, term):
        here = self.here
        self.stage_core[r] = term(1).astype(BF16)
        made = self.lines.copy(self.stage_core.at[r], self.cross.at[r], here.mate())
        near = term(0)
        made.wait_recv()
        near = near + self.cross[r].astype(F32)
        if r == 0:
            self.mine[...] = near
        else:
            self.stage_ring[r - 1] = near.astype(BF16)
            self.pending.append(
                self.lines.copy(
                    self.stage_ring.at[r - 1], self.landed.at[3 - r], here.to(dx=r)
                )
            )

    def total(self):
        for made in self.pending:
            made.wait_recv()
        out = self.mine[...]
        for j in range(3):
            out = out + self.landed[j].astype(F32)
        return out


def norm_back(v, u, n):
    r = lax.rsqrt(jnp.sum(v * v, axis=-1, keepdims=True) * (1.0 / n) + EPS)
    inner = jnp.sum(u * v, axis=-1, keepdims=True) * (1.0 / n)
    return r, r * u - v * (r * r * r * inner)


def mlp_kernel(
    xs_h, middle_h, cot_h, gains, w_gate_h, w_up_h, w_down_h,
    layer_out, middle_grad, d_gain_in, d_gain_out, half_a, half_b, near_a, near_b,
    down_half_a, down_half_b, down_near_a, down_near_b, d_in_h, d_down_h,
    xs, middle, cot, w_gate, w_up, w_down, d_in, gs, act, slope, hidden, cross_f, cross_b, landed_f, landed_b, stage_core, stage_ring,
    mine, mixed_grad, d_down, *rest,
):
    here = Place()
    moves = Moves(rest[-1])
    load_first = [
        moves.start(a, b)
        for a, b in ((xs_h.at[2], xs.at[2]), (w_gate_h, w_gate), (w_up_h, w_up), (w_down_h, w_down))
    ]
    load_xs = {r: moves.start(xs_h.at[r], xs.at[r]) for r in (3, 1, 0)}
    load_last = [moves.start(a, b) for a, b in ((middle_h, middle), (cot_h, cot))]
    greet([here.mate()] + [here.to(dx=d) for d in (1, 2, 3)] + plane_peers(here))
    lines = Lines(*rest[-3:-1])
    n, width = middle.shape
    gain_in, gain_out = gains[2:3, :width], gains[3:4, :width]

    sums = RingSum(here, lines, mine, landed_f, cross_f, stage_core, stage_ring)
    in_sum = PlaneSum(here, lines, d_in, *[None] * 8)
    down_sum = PlaneSum(here, lines, d_down, *[None] * 8)

    def forward(r):
        x = xs[r]
        a, s, h = gate_terms(dot(x, w_gate[...]), dot(x, w_up[...]))
        act[r] = a.astype(BF16)
        slope[r] = s.astype(BF16)
        hidden[r] = h.astype(BF16)
        sums.add(r, lambda q: dot(hidden[r, q * n : (q + 1) * n], w_down[...]))

    for made in load_first:
        made.wait()
    forward(2)
    for r in (3, 1, 0):
        load_xs[r].wait()
        forward(r)
    for made in load_last:
        made.wait()
    mixed = sums.total()
    lines.drain()

    cot_f = cot[...].astype(F32)
    u = cot_f * (1.0 + gain_out)
    factor, grad = norm_back(mixed, u, width)
    layer_out[...] = (middle[...] + mixed * factor * (1.0 + gain_out)).astype(BF16)
    d_gain_out[...] = jnp.sum(cot_f * mixed * factor, axis=0, keepdims=True)
    mixed_grad[...] = grad.astype(BF16)

    ring = RingGather(here, lines, mixed_grad, gs)
    sums = RingSum(here, lines, mine, landed_b, cross_b, stage_core, stage_ring)
    ring.start()

    def backward(r):
        hidden_grad = dot(gs[r], w_down[...], NT)
        act[r] = (hidden_grad * act[r].astype(F32)).astype(BF16)
        slope[r] = (hidden_grad * slope[r].astype(F32)).astype(BF16)

        def term(q):
            rows = slice(q * n, (q + 1) * n)
            return dot(slope[r, rows], w_gate[...], NT) + dot(act[r, rows], w_up[...], NT)

        sums.add(r, term)

    ring.ready0()
    backward(0)
    ring.relay()
    ring.forward()
    ring.ready3()
    backward(3)
    ring.ready1()
    backward(1)
    ring.ready2()
    backward(2)

    flat = lambda ref: ref[...].reshape(ref.shape[0] * ref.shape[1], ref.shape[2])
    grad_down = dot(flat(hidden), flat(gs), TN)
    for k in range(8):
        for p in range(4):
            rows = min(32, PART - 32 * p)
            at = PART * k + 32 * p
            d_down[k // 2, k % 2, p // 2, p % 2, :rows] = grad_down[at : at + rows].astype(BF16)
        d_down[k // 2, k % 2, 1, 1, PART - 96 :] = jnp.zeros((128 - PART, width), BF16)
    down_sum.begin(
        down_half_a, down_half_b, [down_near_a.at[0], down_near_a.at[1]],
        [down_near_b.at[0], down_near_b.at[1]],
    )
    moves.store(d_down, d_down_h)
    for mat, side in ((0, slope), (1, act)):
        grad_side = dot(flat(xs), flat(side), TN)
        for f in range(16):
            d_in[f // 4, (f // 2) % 2, mat, f % 2] = grad_side[72 * f : 72 * f + 72].astype(BF16)
    in_sum.begin(
        half_a, half_b, [near_a.at[0], near_a.at[1]], [near_b.at[0], near_b.at[1]]
    )
    moves.store(d_in, d_in_h)

    update = sums.total()
    base = middle[...]
    u = update * (1.0 + gain_in)
    factor, grad = norm_back(base, u, width)
    d_gain_in[...] = jnp.sum(update * base * factor, axis=0, keepdims=True)
    middle_grad[...] = cot[...].astype(F32) + grad
    down_sum.begun()
    in_sum.begun()
    lines.drain()
    moves.drain()


def mlp_block(xs, middle, cot, gains, w_gate, w_up, w_down):
    n, width = middle.shape
    units = w_gate.shape[1]
    vmem, hbm = pl.BlockSpec(memory_space=pltpu.VMEM), pl.BlockSpec(memory_space=pl.ANY)
    shape = jax.ShapeDtypeStruct
    d_in = shape((4, 2, 2, 2, width // 16, units), BF16)
    d_down = shape((4, 2, 2, 2, 32, width), BF16)
    scratch = (
        [pltpu.VMEM(a.shape, a.dtype) for a in (xs, middle, cot, w_gate, w_up, w_down, d_in)]
        + [pltpu.VMEM((4, 2 * n, width), BF16)]
        + [pltpu.VMEM((4, 2 * n, units), BF16)] * 3
        + [pltpu.VMEM((4, n, width), BF16)] * 2
        + [pltpu.VMEM((3, n, width), BF16)] * 2
        + [pltpu.VMEM((4, n, width), BF16), pltpu.VMEM((3, n, width), BF16)]
        + [pltpu.VMEM((n, width), F32), pltpu.VMEM((n, width), BF16)]
        + [pltpu.VMEM(d_down.shape, BF16)]
        + [pltpu.SemaphoreType.DMA((40,))] * 2
        + [pltpu.SemaphoreType.DMA((11,))]
    )
    return pl.pallas_call(
        mlp_kernel,
        out_shape=(
            shape((n, width), BF16),
            shape((n, width), F32),
            shape((1, width), F32),
            shape((1, width), F32),
            *[shape((2, 2, *d_in.shape[4:]), BF16)] * 4,
            *[shape((2, 2, *d_down.shape[4:]), BF16)] * 4,
            d_in,
            d_down,
        ),
        in_specs=[hbm] * 3 + [vmem] + [hbm] * 3,
        out_specs=(vmem,) * 12 + (hbm,) * 2,
        scratch_shapes=scratch,
        compiler_params=pltpu.CompilerParams(
            collective_id=1, has_side_effects=True, vmem_limit_bytes=63 * MIB
        ),
        name="mlp_block",
    )(xs, middle, cot, gains, w_gate, w_up, w_down)


def plane_peers(here):
    return [here.to(dz=d) for d in (1, 2, 3)] + [here.to(dy=d) for d in (1, 2, 3)]


class PlaneGather:
    def __init__(self, here, lines, local, own, full):
        self.here, self.lines, self.local, self.own, self.full = here, lines, local, own, full

    def first(self):
        here, own, full, copy = self.here, self.own, self.full, self.lines.copy
        z, yh, yl = here.z, here.yh, here.yl
        keep = pltpu.make_async_copy(own.at[yl], full.at[z, yh, yl], self.local)
        keep.start()
        self.a, self.b = [], []
        for d in (1, 3, 2):
            self.a.append(copy(own.at[yl, 0], full.at[z, yh, yl, 0], here.to(dz=d)))
            self.b.append(copy(own.at[yl, 1], full.at[z, yh, yl, 1], here.to(dy=d)))
        keep.wait()

    def blocks(self, dy, dz):
        _, shard, yl = self.here.to(dy=dy)
        yh = lax.rem(shard // 2, 2)
        z = self.here.to(dz=dz)[1] // 4
        full = self.full
        return (
            [full.at[pl.ds(0, 2), yh, yl, 0], full.at[pl.ds(2, 2), yh, yl, 0]],
            [full.at[z, 0, :, 1], full.at[z, 1, :, 1]],
        )

    def second(self):
        here, copy = self.here, self.lines.copy
        for made in self.a + self.b:
            made.wait_recv()
        by_y, by_z = self.blocks(0, 0)
        self.early, self.late = [], []
        for block, up, down in (
            (by_y, here.to(dy=1), here.to(dy=3)),
            (by_z, here.to(dz=1), here.to(dz=3)),
        ):
            self.early.append(copy(block[0], block[0], up))
            self.early.append(copy(block[1], block[1], down))
        for block, up, down in (
            (by_y, here.to(dy=1), here.to(dy=3)),
            (by_z, here.to(dz=1), here.to(dz=3)),
        ):
            self.late.append(copy(block[1], block[1], up))
            self.late.append(copy(block[0], block[0], down))

    def relay(self):
        here, copy = self.here, self.lines.copy
        left_y, left_z = self.blocks(3, 3)
        right_y, right_z = self.blocks(1, 1)
        for made, block, to in zip(
            self.early,
            (left_y[0], right_y[1], left_z[0], right_z[1]),
            (here.to(dy=1), here.to(dy=3), here.to(dz=1), here.to(dz=3)),
        ):
            made.wait_recv()
            self.late.append(copy(block, block, to))

    def wait(self):
        for made in self.late:
            made.wait_recv()


def head_forward(pre, scale, cosine, sine, factor):
    r = lax.rsqrt(jnp.mean(pre * pre, axis=-1, keepdims=True) + EPS)
    v = pre * r * (1.0 + scale)
    half = v.shape[1] // 2
    a, b = v[:, :half], v[:, half:]
    turned = jnp.concatenate([a * cosine - b * sine, b * cosine + a * sine], axis=1)
    return (turned * factor).astype(BF16)


def head_backward(grad, pre, scale, cosine, sine, factor):
    grad = grad * factor
    half = grad.shape[1] // 2
    a, b = grad[:, :half], grad[:, half:]
    dy = jnp.concatenate([a * cosine + b * sine, b * cosine - a * sine], axis=1)
    r, out = norm_back(pre, dy * (1.0 + scale), pre.shape[1])
    return out.astype(BF16), jnp.sum(dy * pre * r, axis=0, keepdims=True)


def attend_kernel(
    tokens, cosine, sine, tail, w_query, w_key, w_value, own_out, w_gate, w_up, w_down,
    *refs,
):
    kept = refs[:14]
    gains = refs[14]
    held = refs[15:29]
    (
        xs, gate_full, up_full, down_full, w_qkv, w_out, normed, queries, kv, probs, context,
        attended, qkv_pre, middle,
    ) = held
    mlp_in, own_qkv, own_in, own_down, full_qkv, full_in, full_down, chip_in = refs[29:37]
    send, recv, local, moved = refs[37:]
    moves = Moves(moved)
    place = {id(a): b for a, b in zip(held, kept)}
    keep = lambda ref: moves.store(ref, place[id(ref)])
    here = Place()
    x_at, c, yl = here.x, here.c, here.yl
    n, width = tokens.shape
    rows, units = w_gate.shape
    block = units // 16
    head_dim = w_key.shape[1]
    at = w_query.shape[1]
    heads = at // head_dim
    wide = own_qkv.shape[-1]
    lines = Lines(send, recv)
    gather = [
        PlaneGather(here, lines, local.at[k], own, full)
        for k, (own, full) in enumerate(
            (
                (own_qkv, full_qkv.at[:, :, c]),
                (own_out, w_out.at[:, :, c]),
                (chip_in, full_in),
                (own_down, full_down),
            )
        )
    ]

    sides = [(w_query, 0), (w_key, at), (w_value, at + head_dim)]
    for p in range(4):
        for side, start in sides:
            lo, hi = max(p * wide, start), min((p + 1) * wide, start + side.shape[1])
            if lo < hi:
                own_qkv[p // 2, p % 2, :rows, lo - p * wide : hi - p * wide] = side[
                    :, lo - start : hi - start
                ]
        own_qkv[p // 2, p % 2, rows:] = tail[:, p * wide : (p + 1) * wide]
    greet([here.mate()] + plane_peers(here) + [here.to(dx=d) for d in (1, 2, 3)])
    gather[0].first()
    gather[1].first()
    lane = lax.broadcasted_iota(jnp.int32, (rows, PART), 1)
    inside = lane < block - x_at * PART
    for mat, weight in ((0, w_gate), (1, w_up)):
        turned = pltpu.roll(weight[...].astype(F32), lax.rem(units - PART * x_at, units), 1)
        for core in range(2):
            parts = [
                jnp.where(inside, turned[:, block * f : block * f + PART], 0.0)
                for f in range(core, 16, 2)
            ]
            own_in[core, mat] = jnp.concatenate(parts, axis=1).astype(BF16)
    across = lines.copy(own_in.at[1 - c], chip_in.at[:, c], here.mate())
    chip_in[:, c] = own_in[c]
    gather[0].second()
    for p in range(3):
        start = pl.multiple_of(PART * x_at + 32 * p, 16)
        own_down[p // 2, p % 2] = w_down[pl.ds(start, 32)]
    start = pl.multiple_of(jnp.minimum(PART * x_at + 96, block - 16), 16)
    last = w_down[pl.ds(start, 16)].astype(F32)
    own_down[1, 1, :16] = jnp.where(x_at < 3, last, 0.0).astype(BF16)
    own_down[1, 1, 16:] = jnp.zeros((16, width), BF16)
    x = tokens[...].astype(F32)
    lean = x * lax.rsqrt(jnp.mean(x * x, axis=-1, keepdims=True) + EPS)
    gather[0].relay()
    gather[1].second()
    across.wait_recv()
    gather[2].first()
    gather[0].wait()
    core_qkv = [
        lines.copy(full_qkv.at[:, :, c, k], full_qkv.at[:, :, c, k], here.mate()) for k in (0, 1)
    ]
    for p in range(4):
        if p % 2 == 0:
            core_qkv[p // 2].wait_recv()
        if p == 1:
            gather[1].relay()
        total = jnp.zeros((8, wide), F32)
        cols = slice(p * wide, (p + 1) * wide)
        for f in range(16):
            part = full_qkv[f // 4, (f // 2) % 2, f % 2, p // 2, p % 2]
            w_qkv[rows * f : rows * f + rows, cols] = part[:rows]
            total = total + part.astype(F32)[rows : rows + 8]
        gains[:, cols] = total
    keep(w_qkv)
    normed[...] = (lean * (1.0 + gains[0:1, :width])).astype(BF16)
    qkv_pre[...] = dot(normed[...], w_qkv[...])
    cos_v, sin_v = cosine[...], sine[...]
    q_scale, k_scale = (gains[k : k + 1, width : width + head_dim] for k in (0, 1))
    key = head_forward(qkv_pre[:, at : at + head_dim], k_scale, cos_v, sin_v, 1.0)
    kv[yl, :, :head_dim] = key
    kv[yl, :, head_dim:] = qkv_pre[:, at + head_dim :].astype(BF16)
    kv_sent = lines.copy(kv.at[yl], kv.at[yl], here.pair())
    gather[2].second()
    keep(normed)
    keep(qkv_pre)
    for h in range(heads):
        cols = slice(h * head_dim, (h + 1) * head_dim)
        queries[:, cols] = head_forward(qkv_pre[:, cols], q_scale, cos_v, sin_v, head_dim**-0.5)
    gather[1].wait()
    core_out = lines.copy(w_out.at[:, :, c], w_out.at[:, :, c], here.mate())
    kv_sent.wait_recv()
    keep(queries)
    keep(kv)
    keys = kv[:, :, :head_dim].reshape(2 * n, head_dim)
    values = kv[:, :, head_dim:].reshape(2 * n, head_dim)
    ring = RingGather(here, lines, mlp_in, xs)
    half = n // 2
    for part in range(2):
        spot = slice(part * half, (part + 1) * half)
        row = lax.broadcasted_iota(jnp.int32, (half, 2 * n), 0) + (yl * n + part * half)
        allowed = lax.broadcasted_iota(jnp.int32, (half, 2 * n), 1) <= row
        for h in range(heads):
            if part == 0 and h == 2:
                gather[3].first()
            cols = slice(h * head_dim, (h + 1) * head_dim)
            scores = jnp.where(allowed, dot(queries[spot, cols], keys, NT), -1e30)
            terms = jnp.exp(scores - jnp.max(scores, axis=-1, keepdims=True))
            low = (terms * (1.0 / jnp.sum(terms, axis=-1, keepdims=True))).astype(BF16)
            probs[h, spot] = low
            context[spot, cols] = dot(low, values).astype(BF16)
        if part == 0:
            core_out.wait_recv()
        att = dot(context[spot, :], w_out[...].reshape(at, width))
        attended[spot, :] = att
        r = lax.rsqrt(jnp.mean(att * att, axis=-1, keepdims=True) + EPS)
        mid = x[spot] + att * r * (1.0 + gains[1:2, :width])
        middle[spot, :] = mid
        r = lax.rsqrt(jnp.mean(mid * mid, axis=-1, keepdims=True) + EPS)
        mlp_in[spot, :] = (mid * r * (1.0 + gains[2:3, :width])).astype(BF16)
        if part == 0:
            ring.start_low()
        else:
            ring.start_high()
    gather[2].relay()
    gather[3].second()
    for ref in (probs, context, w_out, attended, middle):
        keep(ref)
    ring.relay()
    gather[2].wait()
    for f in range(16):
        for mat, whole in ((0, gate_full), (1, up_full)):
            whole[rows * f : rows * f + rows] = full_in[f // 4, (f // 2) % 2, mat, f % 2]
    keep(gate_full)
    keep(up_full)
    ring.forward()
    gather[3].relay()
    ring.ready0()
    gather[3].wait()
    for k in range(8):
        for p in range(4):
            count = min(32, PART - 32 * p)
            down_full[PART * k + 32 * p : PART * k + 32 * p + count] = full_down[
                k // 2, k % 2, p // 2, p % 2, :count
            ]
    keep(down_full)
    ring.ready3()
    ring.ready1()
    ring.ready2()
    keep(xs)
    lines.drain()
    moves.drain()


def attend_block(tokens, cosine, sine, tail, w_query, w_key, w_value, own_out, w_gate, w_up, w_down):
    n, width = tokens.shape
    vmem = pl.BlockSpec(memory_space=pltpu.VMEM)
    shape = jax.ShapeDtypeStruct
    low = lambda *s: shape(s, BF16)
    rows, out_width = w_query.shape
    head_dim, cols = w_key.shape[1], tail.shape[1]
    p_qkv, p_out = (rows + 8, cols // 4), own_out.shape[2:]
    p_in, p_down = (rows, CORE_UNITS), (32, width)
    vm = lambda *s: pltpu.VMEM(s, BF16)
    held = (
        low(4, 2 * n, width),
        low(width, CORE_UNITS),
        low(width, CORE_UNITS),
        low(CORE_UNITS, width),
        low(width, cols),
        low(4, 2, 2, 2, 2, *p_out),
        low(n, width),
        low(n, out_width),
        low(2, n, 2 * head_dim),
        low(out_width // head_dim, n, 2 * n),
        low(n, out_width),
        shape((n, width), F32),
        shape((n, cols), F32),
        shape((n, width), F32),
    )
    return pl.pallas_call(
        attend_kernel,
        out_shape=held + (shape((8, cols), F32),),
        in_specs=[vmem] * 11,
        out_specs=(pl.BlockSpec(memory_space=pl.ANY),) * 14 + (vmem,),
        scratch_shapes=[pltpu.VMEM(a.shape, a.dtype) for a in held]
        + [
            vm(n, width),
            vm(2, 2, *p_qkv),
            vm(2, 2, *p_in),
            vm(2, 2, *p_down),
            vm(4, 2, 2, 2, 2, *p_qkv),
            vm(4, 2, 2, 2, *p_in),
            vm(4, 2, 2, 2, *p_down),
            vm(2, 2, *p_in),
            pltpu.SemaphoreType.DMA((87,)),
            pltpu.SemaphoreType.DMA((87,)),
            pltpu.SemaphoreType.DMA((4,)),
            pltpu.SemaphoreType.DMA((14,)),
        ],
        compiler_params=pltpu.CompilerParams(
            collective_id=0, has_side_effects=True, vmem_limit_bytes=62 * MIB
        ),
        name="attend",
    )(tokens, cosine, sine, tail, w_query, w_key, w_value, own_out, w_gate, w_up, w_down)


class PlaneSum:
    def __init__(
        self, here, lines, grads, landed_a, half_a, sums_a, landed_b, half_b, sums_b, last_a, last_b
    ):
        self.here, self.lines, self.grads = here, lines, grads
        self.landed_a, self.half_a, self.sums_a, self.last_a = landed_a, half_a, sums_a, last_a
        self.landed_b, self.half_b, self.sums_b, self.last_b = landed_b, half_b, sums_b, last_b

    @staticmethod
    def scratch(piece):
        vm = lambda *lead: pltpu.VMEM((*lead, *piece), BF16)
        return [vm(2, 4), vm(2, 2), vm(4), vm(2, 2, 2), vm(2, 2), vm(2, 2), vm(3), vm(3)]

    def spots(self, d):
        _, shard, yl = self.here.to(dy=d)
        yh = lax.rem(shard // 2, 2)
        z = self.here.to(dz=d)[1] // 4
        low, high = pl.ds(0, 2), pl.ds(2, 2)
        return ((low, yh, yl, 0), (high, yh, yl, 0)), ((z, 0, slice(None), 1), (z, 1, slice(None), 1))

    def first(self):
        low, high = pl.ds(0, 2), pl.ds(2, 2)
        self.begin(
            self.half_a,
            self.half_b,
            [self.landed_a.at[0, high], self.landed_a.at[1, low]],
            [self.landed_b.at[0, 1], self.landed_b.at[1, 0]],
        )

    def begin(self, half_a, half_b, near_a, near_b):
        here, g, copy = self.here, self.grads, self.lines.copy
        up_y, down_y, up_z, down_z = here.to(dy=1), here.to(dy=3), here.to(dz=1), here.to(dz=3)
        a, b = self.spots(2)
        self.half = [
            copy(g.at[a[0]], half_a.at[0], up_y),
            copy(g.at[a[1]], half_a.at[1], down_y),
            copy(g.at[b[0]], half_b.at[0], up_z),
            copy(g.at[b[1]], half_b.at[1], down_z),
        ]
        (a1, b1), (a3, b3) = self.spots(1), self.spots(3)
        self.a = [copy(g.at[a1[1]], near_a[0], up_y), copy(g.at[a3[0]], near_a[1], down_y)]
        self.b = [copy(g.at[b1[1]], near_b[0], up_z), copy(g.at[b3[0]], near_b[1], down_z)]

    def begun(self):
        for made in self.half + self.a + self.b:
            made.wait_recv()

    def resume(self, moves, half_a, half_b, near_a, near_b):
        low, high = pl.ds(0, 2), pl.ds(2, 2)
        self.half = [moves.start(half_a, self.half_a), moves.start(half_b, self.half_b)]
        self.a = [
            moves.start(near_a.at[0], self.landed_a.at[0, high]),
            moves.start(near_a.at[1], self.landed_a.at[1, low]),
        ]
        self.b = [
            moves.start(near_b.at[0], self.landed_b.at[0, 1]),
            moves.start(near_b.at[1], self.landed_b.at[1, 0]),
        ]

    def resumed(self):
        for made in self.half + self.a + self.b:
            made.wait()
        self.half, self.a, self.b = [], [], []

    def middle(self):
        here, g, copy = self.here, self.grads, self.lines.copy
        low, high = pl.ds(0, 2), pl.ds(2, 2)
        (a1, b1), (a3, b3) = self.spots(1), self.spots(3)
        for made in self.half:
            made.wait_recv()
        for spot, half in zip(
            (a1[0], a3[1], b1[0], b3[1]),
            (self.half_a.at[0], self.half_a.at[1], self.half_b.at[0], self.half_b.at[1]),
        ):
            g[spot] = (g[spot].astype(F32) + half[...].astype(F32)).astype(BF16)
        self.a += [
            copy(g.at[a1[0]], self.landed_a.at[0, low], here.to(dy=1)),
            copy(g.at[a3[1]], self.landed_a.at[1, high], here.to(dy=3)),
        ]
        self.b += [
            copy(g.at[b1[0]], self.landed_b.at[0, 0], here.to(dz=1)),
            copy(g.at[b3[1]], self.landed_b.at[1, 1], here.to(dz=3)),
        ]

    def second(self):
        here, g, copy = self.here, self.grads, self.lines.copy
        for made in self.a:
            made.wait_recv()
        for k in range(4):
            total = g[k, here.yh, here.yl, 0].astype(F32)
            for j in range(2):
                total = total + self.landed_a[j, k].astype(F32)
            self.sums_a[k] = total.astype(BF16)
        self.a = []
        for d in (1, 3, 2):
            z = here.to(dz=d)[1] // 4
            self.a.append(copy(self.sums_a.at[z], self.last_a.at[d - 1], here.to(dz=d)))
        for made in self.b:
            made.wait_recv()
        for k in range(4):
            total = g[here.z, k // 2, k % 2, 1].astype(F32)
            for j in range(2):
                total = total + self.landed_b[j, k // 2, k % 2].astype(F32)
            self.sums_b[k // 2, k % 2] = total.astype(BF16)
        self.b = []
        for d in (1, 3, 2):
            _, shard, yl = here.to(dy=d)
            yh = lax.rem(shard // 2, 2)
            self.b.append(copy(self.sums_b.at[yh, yl], self.last_b.at[d - 1], here.to(dy=d)))

    def result(self, path):
        here = self.here
        for made in (self.a, self.b)[path]:
            made.wait_recv()
        own = self.sums_a[here.z] if path == 0 else self.sums_b[here.yh, here.yl]
        last = (self.last_a, self.last_b)[path]
        total = own.astype(F32)
        for j in range(3):
            total = total + last[j].astype(F32)
        return total


def retreat_kernel(
    middle_grad_h, attended_h, context_h, probs_h, kv_h, queries_h, qkv_pre_h, normed_h, tokens_h,
    w_qkv_h, w_out_h, g_down_h, g_in_h, half_a, half_b, near_a, near_b,
    down_half_a, down_half_b, down_near_a, down_near_b,
    cosine, sine, gains, d_gain_in, d_gain_out,
    grad_tokens, o_in, o_down, o_qkv, o_out,
    middle_grad, attended, context, probs, kv, queries, qkv_pre, normed, tokens, w_qkv, w_out,
    g_down, g_in,
    context_grad, attn_side, kv_part, kv_give, kv_land, g_qkv, g_out, d_gains,
    chip_qkv, chip_out, cross_qkv, cross_out, swap, half_qkv, half_out, land_qkv, land_out, *rest,
):
    here = Place()
    send, recv, moved = rest[-3:]
    x, yl, c = here.x, here.yl, here.c
    moves = Moves(moved)
    lines = Lines(send, recv)
    copy = lines.copy
    sums = [
        PlaneSum(here, lines, g, *rest[8 * k : 8 * k + 8])
        for k, g in enumerate((g_down, chip_qkv, chip_out, g_in))
    ]
    loads = {"g_in": moves.start(g_in_h, g_in)}
    sums[3].resume(moves, half_a, half_b, near_a, near_b)
    loads["g_down"] = moves.start(g_down_h, g_down)
    sums[0].resume(moves, down_half_a, down_half_b, down_near_a, down_near_b)
    loads |= {
        name: moves.start(a, b)
        for name, a, b in (
            ("attended", attended_h, attended),
            ("middle_grad", middle_grad_h, middle_grad),
            ("w_out", w_out_h, w_out),
            ("context", context_h, context),
            ("probs", probs_h, probs),
            ("kv", kv_h, kv),
            ("queries", queries_h, queries),
            ("qkv_pre", qkv_pre_h, qkv_pre),
            ("w_qkv", w_qkv_h, w_qkv),
            ("normed", normed_h, normed),
            ("tokens", tokens_h, tokens),
        )
    }

    def ready(*names):
        for name in names:
            loads[name].wait()

    greet([here.mate()] + plane_peers(here) + [here.to(dx=d) for d in (1, 2, 3)])
    n, width = middle_grad.shape
    head_dim = 2 * cosine.shape[1]
    heads = queries.shape[1] // head_dim
    rows = width // 16
    at = heads * head_dim
    ready("g_in")
    sums[3].resumed()
    sums[3].middle()
    ready("g_down")
    sums[0].resumed()
    sums[0].middle()
    ready("attended", "middle_grad", "w_out", "context")

    att, dy = attended[...], middle_grad[...]
    r, grad = norm_back(att, dy * (1.0 + gains[1:2, :width]), width)
    d_gains[...] = jnp.zeros_like(d_gains)
    d_gains[1:2, :width] = jnp.sum(dy * att * r, axis=0, keepdims=True)
    d_gains[2:3, :width] = d_gain_in[...]
    d_gains[3:4, :width] = d_gain_out[...]
    attended_grad = grad.astype(BF16)
    out_full = w_out[...].reshape(at, width)
    context_grad[...] = dot(attended_grad, out_full, NT).astype(BF16)
    grad_out = dot(context[...], attended_grad, TN)
    g_out[...] = grad_out.astype(BF16).reshape(g_out.shape)
    give_out = copy(g_out.at[:, :, 1 - c], cross_out, here.mate())
    ready("probs", "kv", "queries", "qkv_pre")
    keys = kv[:, :, :head_dim].reshape(2 * n, head_dim)
    values = kv[:, :, head_dim:].reshape(2 * n, head_dim)
    cos_v, sin_v = cosine[...], sine[...]
    q_scale, k_scale = (gains[k : k + 1, width : width + head_dim] for k in (0, 1))
    d_query = jnp.zeros((1, head_dim), F32)
    for h in range(heads):
        cols = slice(h * head_dim, (h + 1) * head_dim)
        low = probs[h]
        high = low.astype(F32)
        prob_grad = dot(context_grad[:, cols], values, NT)
        inner = jnp.sum(high * prob_grad, axis=-1, keepdims=True)
        score_grad = (high * (prob_grad - inner)).astype(BF16)
        key_part = dot(score_grad, queries[:, cols], TN)
        value_part = dot(low, context_grad[:, cols], TN)
        if h == 0:
            kv_part[:, :, :head_dim] = key_part.reshape(2, n, head_dim)
            kv_part[:, :, head_dim:] = value_part.reshape(2, n, head_dim)
        else:
            kv_part[:, :, :head_dim] += key_part.reshape(2, n, head_dim)
            kv_part[:, :, head_dim:] += value_part.reshape(2, n, head_dim)
        query_grad = dot(score_grad, keys).astype(BF16).astype(F32)
        side, d_scale = head_backward(
            query_grad, qkv_pre[:, cols], q_scale, cos_v, sin_v, head_dim**-0.5
        )
        attn_side[:, cols] = side
        d_query = d_query + d_scale
        if h == 1:
            sums[3].second()
        if h == 2:
            sums[0].second()
    kv_give[...] = kv_part[1 - yl].astype(BF16)
    kv_sent = copy(kv_give, kv_land, here.pair())
    ready("w_qkv", "normed", "tokens")
    normed_grad = dot(attn_side[:, :at], w_qkv[:, :at], NT)
    grad_query = dot(normed[...], attn_side[:, :at], TN)
    for path in (0, 1):
        swap[path] = sums[3].result(path).astype(BF16)
    across = copy(swap.at[1 - c], o_in.at[x, yl, c], here.mate())
    o_in[x, yl, c] = swap[c]
    for path in (0, 1):
        o_down[x, yl, path] = sums[0].result(path).astype(BF16)
    down_pair = copy(o_down.at[x, yl], o_down.at[x, yl], here.pair())
    give_out.wait_recv()
    across.wait_recv()
    in_pair = copy(o_in.at[x, yl], o_in.at[x, yl], here.pair())
    for z in range(4):
        for yh in range(2):
            chip_out[z, yh] = (g_out[z, yh, c].astype(F32) + cross_out[z, yh].astype(F32)).astype(BF16)
    kv_sent.wait_recv()
    kv_grad = (kv_part[yl] + kv_land[...].astype(F32)).astype(BF16)
    side, d_key = head_backward(
        kv_grad[:, :head_dim].astype(F32), qkv_pre[:, at : at + head_dim], k_scale, cos_v, sin_v, 1.0
    )
    attn_side[:, at : at + head_dim] = side
    attn_side[:, at + head_dim :] = kv_grad[:, head_dim:]
    d_gains[0:1, width : width + head_dim] = d_query
    d_gains[1:2, width : width + head_dim] = d_key
    down_pair.wait_recv()
    down_x = [copy(o_down.at[x], o_down.at[x], here.to(dx=d)) for d in (1, 3, 2)]

    normed_grad = normed_grad + dot(attn_side[:, at:], w_qkv[:, at:], NT)
    tok = tokens[...].astype(F32)
    r, grad = norm_back(tok, normed_grad * (1.0 + gains[0:1, :width]), width)
    grad_tokens[...] = (middle_grad[...] + grad).astype(BF16)
    d_gains[0:1, :width] = jnp.sum(normed_grad * tok * r, axis=0, keepdims=True)
    grad_kv = dot(normed[...], attn_side[:, at:], TN)
    wide = g_qkv.shape[-1]
    for p in range(4):
        cols = slice(p * wide, (p + 1) * wide)
        for f in range(16):
            spot = (f // 4, (f // 2) % 2, f % 2, p // 2, p % 2)
            span = slice(rows * f, rows * f + rows)
            parts = []
            if p * wide < at:
                parts.append(grad_query[span, p * wide : min((p + 1) * wide, at)])
            if (p + 1) * wide > at:
                parts.append(grad_kv[span, max(p * wide - at, 0) : (p + 1) * wide - at])
            block = parts[0] if len(parts) == 1 else jnp.concatenate(parts, axis=1)
            g_qkv[spot] = jnp.concatenate([block, d_gains[:, cols]], axis=0).astype(BF16)
    give_qkv = copy(g_qkv.at[:, :, 1 - c], cross_qkv, here.mate())
    sums[2].first()
    in_pair.wait_recv()
    right, left = here.to(dx=1), here.to(dx=3)
    own = [o_in.at[x, m] for m in (0, 1)]
    early = [copy(own[0], own[0], right), copy(own[1], own[1], left)]
    late = [copy(own[1], own[1], right), copy(own[0], own[0], left)]
    give_qkv.wait_recv()
    for z in range(4):
        for yh in range(2):
            chip_qkv[z, yh] = (g_qkv[z, yh, c].astype(F32) + cross_qkv[z, yh].astype(F32)).astype(BF16)
    sums[1].first()
    sums[2].middle()
    sums[1].middle()
    for made, at_x, m, to in ((early[0], left[0], 0, right), (early[1], right[0], 1, left)):
        made.wait_recv()
        late.append(copy(o_in.at[at_x, m], o_in.at[at_x, m], to))
    sums[2].second()
    sums[1].second()
    for path in (0, 1):
        half_out[path] = sums[2].result(path).astype(BF16)
        half_qkv[path] = sums[1].result(path).astype(BF16)
    by_x = []
    for d in (1, 3, 2):
        by_x.append(copy(half_qkv, land_qkv.at[d - 1], here.to(dx=d)))
        by_x.append(copy(half_out, land_out.at[d - 1], here.to(dx=d)))
    for made in by_x:
        made.wait_recv()
    for half, land, out in ((half_qkv, land_qkv, o_qkv), (half_out, land_out, o_out)):
        for path in (0, 1):
            total = half[path].astype(F32)
            for j in range(3):
                total = total + land[j, path].astype(F32)
            out[yl, path] = total.astype(BF16)
    ends = [copy(o.at[yl], o.at[yl], here.pair()) for o in (o_qkv, o_out)]
    for made in down_x + late + ends:
        made.wait_recv()
    lines.drain()


def retreat_block(*args):
    (
        middle_grad, attended, context, probs, kv, queries, qkv_pre, normed, tokens, w_qkv, w_out,
        g_down, g_in, *_, cosine, _, _, _, _,
    ) = args
    vmem, hbm = pl.BlockSpec(memory_space=pltpu.VMEM), pl.BlockSpec(memory_space=pl.ANY)
    shape = jax.ShapeDtypeStruct
    n, width = middle_grad.shape
    out_width, head_dim = queries.shape[1], 2 * cosine.shape[1]
    cols = qkv_pre.shape[1]
    p_in, p_down, p_out = g_in.shape[4:], g_down.shape[4:], w_out.shape[5:]
    p_qkv = (width // 16 + 8, cols // 4)
    vm = lambda *s: pltpu.VMEM(s, BF16)
    scratch = [pltpu.VMEM(a.shape, a.dtype) for a in args[:11]]
    scratch += [vm(*g_down.shape), vm(*g_in.shape)]
    scratch += [vm(n, out_width), vm(n, cols), pltpu.VMEM((2, n, 2 * head_dim), F32)]
    scratch += [vm(n, 2 * head_dim)] * 2
    scratch += [vm(4, 2, 2, 2, 2, *p_qkv), vm(4, 2, 2, 2, 2, *p_out), pltpu.VMEM((8, cols), F32)]
    scratch += [vm(4, 2, 2, 2, *p_qkv), vm(4, 2, 2, 2, *p_out)] * 2
    scratch += [vm(2, *p_in), vm(2, *p_qkv), vm(2, *p_out), vm(3, 2, *p_qkv), vm(3, 2, *p_out)]
    for piece in (p_down, p_qkv, p_out, p_in):
        scratch += PlaneSum.scratch(piece)
    scratch += [pltpu.SemaphoreType.DMA((79,))] * 2 + [pltpu.SemaphoreType.DMA((25,))]
    low = lambda *s: shape(s, BF16)
    return pl.pallas_call(
        retreat_kernel,
        out_shape=(
            low(n, width),
            low(4, 2, 2, *p_in),
            low(4, 2, 2, *p_down),
            low(2, 2, *p_qkv),
            low(2, 2, *p_out),
        ),
        in_specs=[hbm] * 21 + [vmem] * 5,
        out_specs=(vmem,) * 5,
        scratch_shapes=scratch,
        compiler_params=pltpu.CompilerParams(
            collective_id=2, has_side_effects=True, vmem_limit_bytes=63 * MIB
        ),
        name="retreat",
    )(*args)


def finish_kernel(
    o_in_h, o_down_h, o_qkv_h, o_out_h, shown_h, taken_h,
    layer_out_h, grad_tokens_h, out_query, out_key, out_value, out_out, out_gate_h, out_up_h, out_down_h,
    *rest,
):
    out_gains = rest[:6]
    o_in, o_down, o_qkv, o_out, out_gate, out_up, out_down, shown, taken, moved = rest[6:]
    moves = Moves(moved)
    load_in = [moves.start(o_in_h.at[:, m], o_in.at[:, m]) for m in (0, 1)]
    load_tokens = [moves.start(shown_h, shown), moves.start(taken_h, taken)]
    load_down = moves.start(o_down_h, o_down)
    load_rest = [moves.start(o_qkv_h, o_qkv), moves.start(o_out_h, o_out)]
    rows, units = out_gate.shape
    block = units // 16
    wide = o_qkv.shape[-1]
    at, head_dim = out_query.shape[1], out_key.shape[1]
    for m, out, out_h in ((0, out_gate, out_gate_h), (1, out_up, out_up_h)):
        load_in[m].wait()
        for k in range(4):
            count = min(PART, block - PART * k)
            for f in range(16):
                piece = o_in[k, m, f % 2].astype(F32)[:, PART * (f // 2) : PART * (f // 2) + count]
                out[:, block * f + PART * k : block * f + PART * k + count] = piece
        moves.store(out, out_h)
    for made, held, out_h in zip(load_tokens, (shown, taken), (layer_out_h, grad_tokens_h)):
        made.wait()
        moves.store(held, out_h)
    load_down.wait()
    for k in range(4):
        for p in range(4):
            start = PART * k + 32 * p
            count = min(32, PART - 32 * p, block - start)
            if count > 0:
                out_down[start : start + count] = o_down[k, p // 2, p % 2, :count].astype(F32)
    moves.store(out_down, out_down_h)
    for made in load_rest:
        made.wait()
    tail = []
    for p in range(4):
        piece = o_qkv[p // 2, p % 2].astype(F32)
        for out, start in ((out_query, 0), (out_key, at), (out_value, at + head_dim)):
            lo, hi = max(p * wide, start), min((p + 1) * wide, start + out.shape[1])
            if lo < hi:
                out[:, lo - start : hi - start] = piece[:rows, lo - p * wide : hi - p * wide]
        tail.append(piece[rows:])
        height = o_out.shape[2]
        out_out[p * height : (p + 1) * height] = o_out[p // 2, p % 2].astype(F32)
    tail = jnp.concatenate(tail, axis=1)
    width = out_out.shape[1]
    shard = lax.axis_index("fsdp")
    turned = pltpu.roll(tail[:, :width], lax.rem(width - rows * shard, width), 1)
    for k in range(4):
        out_gains[k][...] = turned[k, :rows]
    piece = head_dim // 16
    turned = pltpu.roll(tail[:, width : width + head_dim], lax.rem(head_dim - piece * shard, head_dim), 1)
    for k in range(2):
        out_gains[4 + k][...] = turned[k, :piece]
    moves.drain()


def finish_block(o_in, o_down, o_qkv, o_out, layer_out, grad_tokens, out_shape):
    vmem, hbm = pl.BlockSpec(memory_space=pltpu.VMEM), pl.BlockSpec(memory_space=pl.ANY)
    big = out_shape[6:9]
    return pl.pallas_call(
        finish_kernel,
        out_shape=out_shape,
        in_specs=[hbm] * 6,
        out_specs=(hbm,) * 2 + (vmem,) * 4 + (hbm,) * 3 + (vmem,) * 6,
        scratch_shapes=[pltpu.VMEM(a.shape, a.dtype) for a in (o_in, o_down, o_qkv, o_out, *big, layer_out, grad_tokens)]
        + [pltpu.SemaphoreType.DMA((12,))],
        compiler_params=pltpu.CompilerParams(vmem_limit_bytes=62 * MIB),
        name="finish",
    )(o_in, o_down, o_qkv, o_out, layer_out, grad_tokens)


def body(
    tokens,
    w_query,
    w_key,
    w_value,
    w_out,
    w_gate,
    w_up,
    w_down,
    pre_attn_gain,
    post_attn_gain,
    pre_mlp_gain,
    post_mlp_gain,
    query_gain,
    key_gain,
    cotangent,
):
    n, width = tokens.shape
    rows = w_query.shape[0]
    head_dim = w_key.shape[1]
    out_width = w_query.shape[1]
    shard = lax.axis_index("fsdp")

    mine = jnp.arange(16) == shard
    spread = lambda g: jnp.where(mine[:, None], g[None, :], 0).reshape(1, -1)
    gains_d = [spread(g) for g in (pre_attn_gain, post_attn_gain, pre_mlp_gain, post_mlp_gain)]
    gains_h = jnp.concatenate([spread(query_gain), spread(key_gain)], axis=0)
    tail = jnp.concatenate(
        [
            jnp.pad(jnp.concatenate(gains_d, axis=0), ((0, 4), (0, 0))),
            jnp.pad(gains_h, ((0, 6), (0, out_width + head_dim - width))),
        ],
        axis=1,
    )
    own_out = w_out.reshape(2, 2, -1, width)
    positions = (lax.axis_index("seq") * n + jnp.arange(n, dtype=jnp.int32)).astype(F32)
    frequency = jnp.exp(
        jnp.arange(head_dim // 2, dtype=F32) * (-2.0 * math.log(1000000.0) / head_dim)
    )
    angles = positions[:, None] * frequency[None, :]
    cosine, sine = jnp.cos(angles), jnp.sin(angles)

    (
        xs, gate_full, up_full, down_full, w_qkv, w_out_full, normed, queries, kv, probs, context,
        attended, qkv_pre, middle, gains,
    ) = attend_block(
        tokens, cosine, sine, tail, w_query, w_key, w_value, own_out, w_gate, w_up, w_down
    )
    layer_out, middle_grad, d_gain_in, d_gain_out, *begun, g_in, g_down = mlp_block(
        xs, middle, cotangent, gains, gate_full, up_full, down_full
    )
    grad_tokens, o_in, o_down, o_qkv, o_out = retreat_block(
        middle_grad, attended, context, probs, kv, queries, qkv_pre, normed, tokens, w_qkv,
        w_out_full, g_down, g_in, *begun, cosine, sine, gains, d_gain_in, d_gain_out,
    )
    like = lambda a, kind: jax.ShapeDtypeStruct(a.shape, kind)
    weights = (w_query, w_key, w_value, w_out, w_gate, w_up, w_down)
    gain_args = (pre_attn_gain, post_attn_gain, pre_mlp_gain, post_mlp_gain, query_gain, key_gain)
    shapes = [like(tokens, BF16)] * 2 + [like(a, F32) for a in weights + gain_args]
    return tuple(finish_block(o_in, o_down, o_qkv, o_out, layer_out, grad_tokens, shapes))


def solution(mesh):
    tokens = P(("dp", "fsdp", "seq"), None)
    weight, gain = P("fsdp", None), P("fsdp")
    return jax.shard_map(
        body,
        mesh=mesh,
        in_specs=(tokens,) + (weight,) * 7 + (gain,) * 6 + (tokens,),
        out_specs=(tokens,) * 2 + (weight,) * 7 + (gain,) * 6,
        check_vma=False,
    )
```

```python
import functools
import math

import jax
import jax.numpy as jnp
from jax import lax
from jax.experimental import pallas as pl
from jax.experimental.pallas import tpu as pltpu
from jax.sharding import PartitionSpec as P

F32, BF16 = jnp.float32, jnp.bfloat16
MESH = pl.DeviceIdType.MESH
NN = (((1,), (0,)), ((), ()))
NT = (((1,), (1,)), ((), ()))
TN = (((0,), (0,)), ((), ()))
EPS = 1e-06
MIB = 2**20
PART = 112
CORE_UNITS = 8 * PART
UNITS_OF_SHARD = 432


def dot(a, b, dims=NN):
    return lax.dot_general(a, b, dims, preferred_element_type=F32)


class Place:
    def __init__(self):
        shard = lax.axis_index("fsdp")
        self.x = lax.axis_index("dp")
        self.z = shard // 4
        self.yh = lax.rem(shard // 2, 2)
        self.c = lax.rem(shard, 2)
        self.yl = lax.axis_index("seq")

    def to(self, dx=0, dy=0, dz=0, dc=0):
        x, z, yh, yl, c = self.x, self.z, self.yh, self.yl, self.c
        if dx:
            x = lax.rem(x + dx, 4)
        if dz:
            z = lax.rem(z + dz, 4)
        if dy:
            y = lax.rem(yh * 2 + yl + dy, 4)
            yh, yl = y // 2, lax.rem(y, 2)
        if dc:
            c = 1 - c
        return (x, (z * 2 + yh) * 2 + c, yl)

    def mate(self):
        return self.to(dc=1)

    def pair(self):
        return (self.x, (self.z * 2 + self.yh) * 2 + self.c, 1 - self.yl)


def greet(peers):
    barrier = pltpu.get_barrier_semaphore()
    for peer in peers:
        pl.semaphore_signal(barrier, inc=1, device_id=peer, device_id_type=MESH)
    pl.semaphore_wait(barrier, len(peers))


class Moves:
    def __init__(self, sems):
        self.sems, self.used, self.open = sems, 0, []

    def start(self, src, dst):
        made = pltpu.make_async_copy(src, dst, self.sems.at[self.used])
        self.used += 1
        made.start()
        return made

    def store(self, src, dst):
        self.open.append(self.start(src, dst))

    def drain(self):
        for made in self.open:
            made.wait()
        self.open = []


class Lines:
    def __init__(self, send, recv):
        self.send, self.recv, self.used, self.open = send, recv, 0, []

    def copy(self, src, dst, device):
        made = self.plan(src, dst, device)
        made.start()
        return made

    def plan(self, src, dst, device):
        k = self.used
        self.used += 1
        made = pltpu.make_async_remote_copy(
            src_ref=src,
            dst_ref=dst,
            send_sem=self.send.at[k],
            recv_sem=self.recv.at[k],
            device_id=device,
            device_id_type=MESH,
        )
        self.open.append(made)
        return made

    def drain(self):
        for made in self.open:
            made.wait_send()
        self.open = []


def gate_terms(gate, up):
    k, c = math.sqrt(2.0 / math.pi), 0.044715
    square = gate * gate
    t = jnp.tanh(gate * (k + (k * c) * square))
    half = 0.5 + 0.5 * t
    act = gate * half
    slope = half + 0.5 * gate * (1.0 - t * t) * (k + (3.0 * k * c) * square)
    return act, slope * up, act * up


class RingGather:
    def __init__(self, here, lines, own, full):
        self.here, self.lines, self.own, self.full = here, lines, own, full

    def start(self):
        here, own, full, copy = self.here, self.own, self.full, self.lines.copy
        n = own.shape[0]
        h = n // 2
        right, left = here.to(dx=1), here.to(dx=3)
        lo, hi = pl.ds(0, h), pl.ds(h, h)
        self.core = copy(own, full.at[0, pl.ds(n, n)], here.mate())
        self.a0 = copy(own.at[lo], full.at[3, lo], right)
        self.b0 = copy(own.at[hi], full.at[1, hi], left)
        self.a1 = copy(own.at[hi], full.at[3, hi], right)
        self.b1 = copy(own.at[lo], full.at[1, lo], left)
        full[0, :n] = own[...]

    def start_low(self):
        here, own, full, copy = self.here, self.own, self.full, self.lines.copy
        lo = pl.ds(0, own.shape[0] // 2)
        self.a0 = copy(own.at[lo], full.at[3, lo], here.to(dx=1))
        self.b1 = copy(own.at[lo], full.at[1, lo], here.to(dx=3))

    def start_high(self):
        here, own, full, copy = self.here, self.own, self.full, self.lines.copy
        n = own.shape[0]
        hi = pl.ds(n // 2, n // 2)
        self.b0 = copy(own.at[hi], full.at[1, hi], here.to(dx=3))
        self.a1 = copy(own.at[hi], full.at[3, hi], here.to(dx=1))
        self.core = copy(own, full.at[0, pl.ds(n, n)], here.mate())
        full[0, :n] = own[...]

    def ready0(self):
        self.core.wait_recv()

    def relay(self):
        here, full, copy = self.here, self.full, self.lines.copy
        n = self.own.shape[0]
        h = n // 2
        lo, hi = pl.ds(0, h), pl.ds(h, h)
        right, left = here.to(dx=1), here.to(dx=3)
        self.a0.wait_recv()
        self.a2 = copy(full.at[3, lo], full.at[2, lo], right)
        self.b0.wait_recv()
        self.b2 = copy(full.at[1, hi], full.at[2, hi], left)

    def forward(self):
        full, copy = self.full, self.lines.copy
        n = self.own.shape[0]
        both, other = pl.ds(0, n), pl.ds(n, n)
        mate = self.here.mate()
        self.a1.wait_recv()
        self.f3 = copy(full.at[3, both], full.at[3, other], mate)
        self.b1.wait_recv()
        self.f1 = copy(full.at[1, both], full.at[1, other], mate)

    def ready3(self):
        self.f3.wait_recv()

    def ready1(self):
        self.f1.wait_recv()

    def ready2(self):
        n = self.own.shape[0]
        self.a2.wait_recv()
        self.b2.wait_recv()
        f2 = self.lines.copy(
            self.full.at[2, pl.ds(0, n)], self.full.at[2, pl.ds(n, n)], self.here.mate()
        )
        f2.wait_recv()


class RingSum:
    def __init__(self, here, lines, mine, landed, cross, stage_core, stage_ring):
        self.here, self.lines, self.mine = here, lines, mine
        self.landed, self.cross = landed, cross
        self.stage_core, self.stage_ring = stage_core, stage_ring
        self.pending = []

    def add(self, r, term):
        here = self.here
        self.stage_core[r] = term(1).astype(BF16)
        made = self.lines.copy(self.stage_core.at[r], self.cross.at[r], here.mate())
        near = term(0)
        made.wait_recv()
        near = near + self.cross[r].astype(F32)
        if r == 0:
            self.mine[...] = near
        else:
            self.stage_ring[r - 1] = near.astype(BF16)
            self.pending.append(
                self.lines.copy(
                    self.stage_ring.at[r - 1], self.landed.at[3 - r], here.to(dx=r)
                )
            )

    def total(self):
        for made in self.pending:
            made.wait_recv()
        out = self.mine[...]
        for j in range(3):
            out = out + self.landed[j].astype(F32)
        return out


def norm_back(v, u, n):
    r = lax.rsqrt(jnp.sum(v * v, axis=-1, keepdims=True) * (1.0 / n) + EPS)
    inner = jnp.sum(u * v, axis=-1, keepdims=True) * (1.0 / n)
    return r, r * u - v * (r * r * r * inner)


def mlp_kernel(
    xs_h, middle_h, cot_h, gains, w_gate_h, w_up_h, w_down_h,
    layer_out, middle_grad, d_gain_in, d_gain_out, half_a, half_b, near_a, near_b,
    down_half_a, down_half_b, down_near_a, down_near_b, d_in_h, d_down_h,
    xs, middle, cot, w_gate, w_up, w_down, d_in, gs, act, slope, hidden, cross_f, cross_b, landed_f, landed_b, stage_core, stage_ring,
    mine, mixed_grad, d_down, *rest,
):
    here = Place()
    moves = Moves(rest[-1])
    load_first = [
        moves.start(a, b)
        for a, b in ((xs_h.at[2], xs.at[2]), (w_gate_h, w_gate), (w_up_h, w_up), (w_down_h, w_down))
    ]
    load_xs = {r: moves.start(xs_h.at[r], xs.at[r]) for r in (3, 1, 0)}
    load_last = [moves.start(a, b) for a, b in ((middle_h, middle), (cot_h, cot))]
    greet([here.mate()] + [here.to(dx=d) for d in (1, 2, 3)] + plane_peers(here))
    lines = Lines(*rest[-3:-1])
    n, width = middle.shape
    gain_in, gain_out = gains[2:3, :width], gains[3:4, :width]

    sums = RingSum(here, lines, mine, landed_f, cross_f, stage_core, stage_ring)
    in_sum = PlaneSum(here, lines, d_in, *[None] * 8)
    down_sum = PlaneSum(here, lines, d_down, *[None] * 8)

    def forward(r):
        x = xs[r]
        a, s, h = gate_terms(dot(x, w_gate[...]), dot(x, w_up[...]))
        act[r] = a.astype(BF16)
        slope[r] = s.astype(BF16)
        hidden[r] = h.astype(BF16)
        sums.add(r, lambda q: dot(hidden[r, q * n : (q + 1) * n], w_down[...]))

    for made in load_first:
        made.wait()
    forward(2)
    for r in (3, 1, 0):
        load_xs[r].wait()
        forward(r)
    for made in load_last:
        made.wait()
    mixed = sums.total()
    lines.drain()

    cot_f = cot[...].astype(F32)
    u = cot_f * (1.0 + gain_out)
    factor, grad = norm_back(mixed, u, width)
    layer_out[...] = (middle[...] + mixed * factor * (1.0 + gain_out)).astype(BF16)
    d_gain_out[...] = jnp.sum(cot_f * mixed * factor, axis=0, keepdims=True)
    mixed_grad[...] = grad.astype(BF16)

    ring = RingGather(here, lines, mixed_grad, gs)
    sums = RingSum(here, lines, mine, landed_b, cross_b, stage_core, stage_ring)
    ring.start()

    def backward(r):
        hidden_grad = dot(gs[r], w_down[...], NT)
        act[r] = (hidden_grad * act[r].astype(F32)).astype(BF16)
        slope[r] = (hidden_grad * slope[r].astype(F32)).astype(BF16)

        def term(q):
            rows = slice(q * n, (q + 1) * n)
            return dot(slope[r, rows], w_gate[...], NT) + dot(act[r, rows], w_up[...], NT)

        sums.add(r, term)

    ring.ready0()
    backward(0)
    ring.relay()
    ring.forward()
    ring.ready3()
    backward(3)
    ring.ready1()
    backward(1)
    ring.ready2()
    backward(2)

    flat = lambda ref: ref[...].reshape(ref.shape[0] * ref.shape[1], ref.shape[2])
    send_in = in_sum.begin_by_owner(half_a, half_b, near_a, near_b)
    for mat, side in ((0, slope), (1, act)):
        grad_side = dot(flat(xs), flat(side), TN)
        for f in range(16):
            d_in[f // 4, (f // 2) % 2, mat, f % 2] = grad_side[72 * f : 72 * f + 72].astype(BF16)
        send_in(mat)
    moves.store(d_in, d_in_h)
    grad_down = dot(flat(hidden), flat(gs), TN)
    for k in range(8):
        for p in range(4):
            rows = min(32, PART - 32 * p)
            at = PART * k + 32 * p
            d_down[k // 2, k % 2, p // 2, p % 2, :rows] = grad_down[at : at + rows].astype(BF16)
        d_down[k // 2, k % 2, 1, 1, PART - 96 :] = jnp.zeros((128 - PART, width), BF16)
    down_sum.begin(
        down_half_a, down_half_b, [down_near_a.at[0], down_near_a.at[1]],
        [down_near_b.at[0], down_near_b.at[1]],
    )
    moves.store(d_down, d_down_h)

    update = sums.total()
    base = middle[...]
    u = update * (1.0 + gain_in)
    factor, grad = norm_back(base, u, width)
    d_gain_in[...] = jnp.sum(update * base * factor, axis=0, keepdims=True)
    middle_grad[...] = cot[...].astype(F32) + grad
    down_sum.begun()
    in_sum.begun()
    lines.drain()
    moves.drain()


def mlp_block(xs, middle, cot, gains, w_gate, w_up, w_down):
    n, width = middle.shape
    units = w_gate.shape[1]
    vmem, hbm = pl.BlockSpec(memory_space=pltpu.VMEM), pl.BlockSpec(memory_space=pl.ANY)
    shape = jax.ShapeDtypeStruct
    d_in = shape((4, 2, 2, 2, width // 16, units), BF16)
    d_down = shape((4, 2, 2, 2, 32, width), BF16)
    scratch = (
        [pltpu.VMEM(a.shape, a.dtype) for a in (xs, middle, cot, w_gate, w_up, w_down, d_in)]
        + [pltpu.VMEM((4, 2 * n, width), BF16)]
        + [pltpu.VMEM((4, 2 * n, units), BF16)] * 3
        + [pltpu.VMEM((4, n, width), BF16)] * 2
        + [pltpu.VMEM((3, n, width), BF16)] * 2
        + [pltpu.VMEM((4, n, width), BF16), pltpu.VMEM((3, n, width), BF16)]
        + [pltpu.VMEM((n, width), F32), pltpu.VMEM((n, width), BF16)]
        + [pltpu.VMEM(d_down.shape, BF16)]
        + [pltpu.SemaphoreType.DMA((44,))] * 2
        + [pltpu.SemaphoreType.DMA((11,))]
    )
    return pl.pallas_call(
        mlp_kernel,
        out_shape=(
            shape((n, width), BF16),
            shape((n, width), F32),
            shape((1, width), F32),
            shape((1, width), F32),
            *[shape((2, 2, *d_in.shape[4:]), BF16)] * 4,
            *[shape((2, 2, *d_down.shape[4:]), BF16)] * 4,
            d_in,
            d_down,
        ),
        in_specs=[hbm] * 3 + [vmem] + [hbm] * 3,
        out_specs=(vmem,) * 12 + (hbm,) * 2,
        scratch_shapes=scratch,
        compiler_params=pltpu.CompilerParams(
            collective_id=1, has_side_effects=True, vmem_limit_bytes=63 * MIB
        ),
        name="mlp_block",
    )(xs, middle, cot, gains, w_gate, w_up, w_down)


def plane_peers(here):
    return [here.to(dz=d) for d in (1, 2, 3)] + [here.to(dy=d) for d in (1, 2, 3)]


class PlaneGather:
    def __init__(self, here, lines, local, own, full):
        self.here, self.lines, self.local, self.own, self.full = here, lines, local, own, full

    def first(self):
        here, own, full, copy = self.here, self.own, self.full, self.lines.copy
        z, yh, yl = here.z, here.yh, here.yl
        keep = pltpu.make_async_copy(own.at[yl], full.at[z, yh, yl], self.local)
        keep.start()
        self.a, self.b = [], []
        for d in (1, 3, 2):
            self.a.append(copy(own.at[yl, 0], full.at[z, yh, yl, 0], here.to(dz=d)))
            self.b.append(copy(own.at[yl, 1], full.at[z, yh, yl, 1], here.to(dy=d)))
        keep.wait()

    def blocks(self, dy, dz):
        _, shard, yl = self.here.to(dy=dy)
        yh = lax.rem(shard // 2, 2)
        z = self.here.to(dz=dz)[1] // 4
        full = self.full
        return (
            [full.at[pl.ds(0, 2), yh, yl, 0], full.at[pl.ds(2, 2), yh, yl, 0]],
            [full.at[z, 0, :, 1], full.at[z, 1, :, 1]],
        )

    def second(self):
        here, copy = self.here, self.lines.copy
        for made in self.a + self.b:
            made.wait_recv()
        by_y, by_z = self.blocks(0, 0)
        self.early, self.late = [], []
        for block, up, down in (
            (by_y, here.to(dy=1), here.to(dy=3)),
            (by_z, here.to(dz=1), here.to(dz=3)),
        ):
            self.early.append(copy(block[0], block[0], up))
            self.early.append(copy(block[1], block[1], down))
        for block, up, down in (
            (by_y, here.to(dy=1), here.to(dy=3)),
            (by_z, here.to(dz=1), here.to(dz=3)),
        ):
            self.late.append(copy(block[1], block[1], up))
            self.late.append(copy(block[0], block[0], down))

    def relay(self):
        here, copy = self.here, self.lines.copy
        left_y, left_z = self.blocks(3, 3)
        right_y, right_z = self.blocks(1, 1)
        for made, block, to in zip(
            self.early,
            (left_y[0], right_y[1], left_z[0], right_z[1]),
            (here.to(dy=1), here.to(dy=3), here.to(dz=1), here.to(dz=3)),
        ):
            made.wait_recv()
            self.late.append(copy(block, block, to))

    def wait(self):
        for made in self.late:
            made.wait_recv()


def head_forward(pre, scale, cosine, sine, factor):
    r = lax.rsqrt(jnp.mean(pre * pre, axis=-1, keepdims=True) + EPS)
    v = pre * r * (1.0 + scale)
    half = v.shape[1] // 2
    a, b = v[:, :half], v[:, half:]
    turned = jnp.concatenate([a * cosine - b * sine, b * cosine + a * sine], axis=1)
    return (turned * factor).astype(BF16)


def head_backward(grad, pre, scale, cosine, sine, factor):
    grad = grad * factor
    half = grad.shape[1] // 2
    a, b = grad[:, :half], grad[:, half:]
    dy = jnp.concatenate([a * cosine + b * sine, b * cosine - a * sine], axis=1)
    r, out = norm_back(pre, dy * (1.0 + scale), pre.shape[1])
    return out.astype(BF16), jnp.sum(dy * pre * r, axis=0, keepdims=True)


def attend_kernel(
    tokens, cosine, sine, tail, w_query, w_key, w_value, own_out, w_gate, w_up, w_down,
    *refs,
):
    kept = refs[:14]
    gains = refs[14]
    held = refs[15:29]
    (
        xs, gate_full, up_full, down_full, w_qkv, w_out, normed, queries, kv, probs, context,
        attended, qkv_pre, middle,
    ) = held
    mlp_in, own_qkv, own_in, own_down, full_qkv, full_in, full_down, chip_in = refs[29:37]
    send, recv, local, moved = refs[37:]
    moves = Moves(moved)
    place = {id(a): b for a, b in zip(held, kept)}
    keep = lambda ref: moves.store(ref, place[id(ref)])
    here = Place()
    x_at, c, yl = here.x, here.c, here.yl
    n, width = tokens.shape
    rows, units = w_gate.shape
    block = units // 16
    head_dim = w_key.shape[1]
    at = w_query.shape[1]
    heads = at // head_dim
    wide = own_qkv.shape[-1]
    lines = Lines(send, recv)
    gather = [
        PlaneGather(here, lines, local.at[k], own, full)
        for k, (own, full) in enumerate(
            (
                (own_qkv, full_qkv.at[:, :, c]),
                (own_out, w_out.at[:, :, c]),
                (chip_in, full_in),
                (own_down, full_down),
            )
        )
    ]

    sides = [(w_query, 0), (w_key, at), (w_value, at + head_dim)]
    for p in range(4):
        for side, start in sides:
            lo, hi = max(p * wide, start), min((p + 1) * wide, start + side.shape[1])
            if lo < hi:
                own_qkv[p // 2, p % 2, :rows, lo - p * wide : hi - p * wide] = side[
                    :, lo - start : hi - start
                ]
        own_qkv[p // 2, p % 2, rows:] = tail[:, p * wide : (p + 1) * wide]
    greet([here.mate()] + plane_peers(here) + [here.to(dx=d) for d in (1, 2, 3)])
    gather[0].first()
    gather[1].first()
    lane = lax.broadcasted_iota(jnp.int32, (rows, PART), 1)
    inside = lane < block - x_at * PART
    for mat, weight in ((0, w_gate), (1, w_up)):
        turned = pltpu.roll(weight[...].astype(F32), lax.rem(units - PART * x_at, units), 1)
        for core in range(2):
            parts = [
                jnp.where(inside, turned[:, block * f : block * f + PART], 0.0)
                for f in range(core, 16, 2)
            ]
            own_in[core, mat] = jnp.concatenate(parts, axis=1).astype(BF16)
    across = lines.copy(own_in.at[1 - c], chip_in.at[:, c], here.mate())
    chip_in[:, c] = own_in[c]
    gather[0].second()
    for p in range(3):
        start = pl.multiple_of(PART * x_at + 32 * p, 16)
        own_down[p // 2, p % 2] = w_down[pl.ds(start, 32)]
    start = pl.multiple_of(jnp.minimum(PART * x_at + 96, block - 16), 16)
    last = w_down[pl.ds(start, 16)].astype(F32)
    own_down[1, 1, :16] = jnp.where(x_at < 3, last, 0.0).astype(BF16)
    own_down[1, 1, 16:] = jnp.zeros((16, width), BF16)
    x = tokens[...].astype(F32)
    lean = x * lax.rsqrt(jnp.mean(x * x, axis=-1, keepdims=True) + EPS)
    gather[0].relay()
    gather[1].second()
    across.wait_recv()
    gather[2].first()
    gather[0].wait()
    core_qkv = [
        lines.copy(full_qkv.at[:, :, c, k], full_qkv.at[:, :, c, k], here.mate()) for k in (0, 1)
    ]
    for p in range(4):
        if p % 2 == 0:
            core_qkv[p // 2].wait_recv()
        if p == 1:
            gather[1].relay()
        total = jnp.zeros((8, wide), F32)
        cols = slice(p * wide, (p + 1) * wide)
        for f in range(16):
            part = full_qkv[f // 4, (f // 2) % 2, f % 2, p // 2, p % 2]
            w_qkv[rows * f : rows * f + rows, cols] = part[:rows]
            total = total + part.astype(F32)[rows : rows + 8]
        gains[:, cols] = total
    keep(w_qkv)
    normed[...] = (lean * (1.0 + gains[0:1, :width])).astype(BF16)
    qkv_pre[...] = dot(normed[...], w_qkv[...])
    cos_v, sin_v = cosine[...], sine[...]
    q_scale, k_scale = (gains[k : k + 1, width : width + head_dim] for k in (0, 1))
    key = head_forward(qkv_pre[:, at : at + head_dim], k_scale, cos_v, sin_v, 1.0)
    kv[yl, :, :head_dim] = key
    kv[yl, :, head_dim:] = qkv_pre[:, at + head_dim :].astype(BF16)
    kv_sent = lines.copy(kv.at[yl], kv.at[yl], here.pair())
    gather[2].second()
    keep(normed)
    keep(qkv_pre)
    for h in range(heads):
        cols = slice(h * head_dim, (h + 1) * head_dim)
        queries[:, cols] = head_forward(qkv_pre[:, cols], q_scale, cos_v, sin_v, head_dim**-0.5)
    gather[1].wait()
    core_out = lines.copy(w_out.at[:, :, c], w_out.at[:, :, c], here.mate())
    kv_sent.wait_recv()
    keep(queries)
    keep(kv)
    keys = kv[:, :, :head_dim].reshape(2 * n, head_dim)
    values = kv[:, :, head_dim:].reshape(2 * n, head_dim)
    ring = RingGather(here, lines, mlp_in, xs)
    half = n // 2
    for part in range(2):
        spot = slice(part * half, (part + 1) * half)
        row = lax.broadcasted_iota(jnp.int32, (half, 2 * n), 0) + (yl * n + part * half)
        allowed = lax.broadcasted_iota(jnp.int32, (half, 2 * n), 1) <= row
        for h in range(heads):
            if part == 0 and h == 2:
                gather[3].first()
            cols = slice(h * head_dim, (h + 1) * head_dim)
            scores = jnp.where(allowed, dot(queries[spot, cols], keys, NT), -1e30)
            terms = jnp.exp(scores - jnp.max(scores, axis=-1, keepdims=True))
            low = (terms * (1.0 / jnp.sum(terms, axis=-1, keepdims=True))).astype(BF16)
            probs[h, spot] = low
            context[spot, cols] = dot(low, values).astype(BF16)
        if part == 0:
            core_out.wait_recv()
        att = dot(context[spot, :], w_out[...].reshape(at, width))
        attended[spot, :] = att
        r = lax.rsqrt(jnp.mean(att * att, axis=-1, keepdims=True) + EPS)
        mid = x[spot] + att * r * (1.0 + gains[1:2, :width])
        middle[spot, :] = mid
        r = lax.rsqrt(jnp.mean(mid * mid, axis=-1, keepdims=True) + EPS)
        mlp_in[spot, :] = (mid * r * (1.0 + gains[2:3, :width])).astype(BF16)
        if part == 0:
            ring.start_low()
        else:
            ring.start_high()
    gather[2].relay()
    gather[3].second()
    for ref in (probs, context, w_out, attended, middle):
        keep(ref)
    ring.relay()
    gather[2].wait()
    for f in range(16):
        for mat, whole in ((0, gate_full), (1, up_full)):
            whole[rows * f : rows * f + rows] = full_in[f // 4, (f // 2) % 2, mat, f % 2]
    keep(gate_full)
    keep(up_full)
    ring.forward()
    gather[3].relay()
    ring.ready0()
    gather[3].wait()
    for k in range(8):
        for p in range(4):
            count = min(32, PART - 32 * p)
            down_full[PART * k + 32 * p : PART * k + 32 * p + count] = full_down[
                k // 2, k % 2, p // 2, p % 2, :count
            ]
    keep(down_full)
    ring.ready3()
    ring.ready1()
    ring.ready2()
    keep(xs)
    lines.drain()
    moves.drain()


def attend_block(tokens, cosine, sine, tail, w_query, w_key, w_value, own_out, w_gate, w_up, w_down):
    n, width = tokens.shape
    vmem = pl.BlockSpec(memory_space=pltpu.VMEM)
    shape = jax.ShapeDtypeStruct
    low = lambda *s: shape(s, BF16)
    rows, out_width = w_query.shape
    head_dim, cols = w_key.shape[1], tail.shape[1]
    p_qkv, p_out = (rows + 8, cols // 4), own_out.shape[2:]
    p_in, p_down = (rows, CORE_UNITS), (32, width)
    vm = lambda *s: pltpu.VMEM(s, BF16)
    held = (
        low(4, 2 * n, width),
        low(width, CORE_UNITS),
        low(width, CORE_UNITS),
        low(CORE_UNITS, width),
        low(width, cols),
        low(4, 2, 2, 2, 2, *p_out),
        low(n, width),
        low(n, out_width),
        low(2, n, 2 * head_dim),
        low(out_width // head_dim, n, 2 * n),
        low(n, out_width),
        shape((n, width), F32),
        shape((n, cols), F32),
        shape((n, width), F32),
    )
    return pl.pallas_call(
        attend_kernel,
        out_shape=held + (shape((8, cols), F32),),
        in_specs=[vmem] * 11,
        out_specs=(pl.BlockSpec(memory_space=pl.ANY),) * 14 + (vmem,),
        scratch_shapes=[pltpu.VMEM(a.shape, a.dtype) for a in held]
        + [
            vm(n, width),
            vm(2, 2, *p_qkv),
            vm(2, 2, *p_in),
            vm(2, 2, *p_down),
            vm(4, 2, 2, 2, 2, *p_qkv),
            vm(4, 2, 2, 2, *p_in),
            vm(4, 2, 2, 2, *p_down),
            vm(2, 2, *p_in),
            pltpu.SemaphoreType.DMA((87,)),
            pltpu.SemaphoreType.DMA((87,)),
            pltpu.SemaphoreType.DMA((4,)),
            pltpu.SemaphoreType.DMA((14,)),
        ],
        compiler_params=pltpu.CompilerParams(
            collective_id=0, has_side_effects=True, vmem_limit_bytes=62 * MIB
        ),
        name="attend",
    )(tokens, cosine, sine, tail, w_query, w_key, w_value, own_out, w_gate, w_up, w_down)


class PlaneSum:
    def __init__(
        self, here, lines, grads, landed_a, half_a, sums_a, landed_b, half_b, sums_b, last_a, last_b
    ):
        self.here, self.lines, self.grads = here, lines, grads
        self.landed_a, self.half_a, self.sums_a, self.last_a = landed_a, half_a, sums_a, last_a
        self.landed_b, self.half_b, self.sums_b, self.last_b = landed_b, half_b, sums_b, last_b

    @staticmethod
    def scratch(piece):
        vm = lambda *lead: pltpu.VMEM((*lead, *piece), BF16)
        return [vm(2, 4), vm(2, 2), vm(4), vm(2, 2, 2), vm(2, 2), vm(2, 2), vm(3), vm(3)]

    def spots(self, d):
        _, shard, yl = self.here.to(dy=d)
        yh = lax.rem(shard // 2, 2)
        z = self.here.to(dz=d)[1] // 4
        low, high = pl.ds(0, 2), pl.ds(2, 2)
        return ((low, yh, yl, 0), (high, yh, yl, 0)), ((z, 0, slice(None), 1), (z, 1, slice(None), 1))

    def first(self):
        low, high = pl.ds(0, 2), pl.ds(2, 2)
        self.begin(
            self.half_a,
            self.half_b,
            [self.landed_a.at[0, high], self.landed_a.at[1, low]],
            [self.landed_b.at[0, 1], self.landed_b.at[1, 0]],
        )

    def begin(self, half_a, half_b, near_a, near_b):
        here, g, copy = self.here, self.grads, self.lines.copy
        up_y, down_y, up_z, down_z = here.to(dy=1), here.to(dy=3), here.to(dz=1), here.to(dz=3)
        a, b = self.spots(2)
        self.half = [
            copy(g.at[a[0]], half_a.at[0], up_y),
            copy(g.at[a[1]], half_a.at[1], down_y),
            copy(g.at[b[0]], half_b.at[0], up_z),
            copy(g.at[b[1]], half_b.at[1], down_z),
        ]
        (a1, b1), (a3, b3) = self.spots(1), self.spots(3)
        self.a = [copy(g.at[a1[1]], near_a[0], up_y), copy(g.at[a3[0]], near_a[1], down_y)]
        self.b = [copy(g.at[b1[1]], near_b[0], up_z), copy(g.at[b3[0]], near_b[1], down_z)]

    def begin_by_owner(self, half_a, half_b, near_a, near_b):
        here, g, plan = self.here, self.grads, self.lines.plan
        up_y, down_y, up_z, down_z = here.to(dy=1), here.to(dy=3), here.to(dz=1), here.to(dz=3)
        (a, b), (a1, b1), (a3, b3) = self.spots(2), self.spots(1), self.spots(3)
        same = [plan(g.at[a[0]], half_a.at[0], up_y), plan(g.at[a[1]], half_a.at[1], down_y)]
        other = [plan(g.at[a1[1]], near_a.at[0], up_y), plan(g.at[a3[0]], near_a.at[1], down_y)]
        by_z = [
            [
                plan(g.at[b[0][0], 0, k, 1], half_b.at[0, k], up_z),
                plan(g.at[b[0][0], 1, k, 1], half_b.at[1, k], down_z),
                plan(g.at[b1[0][0], 1, k, 1], near_b.at[0, k], up_z),
                plan(g.at[b3[0][0], 0, k, 1], near_b.at[1, k], down_z),
            ]
            for k in range(2)
        ]
        self.half, self.a, self.b = same, other, by_z[0] + by_z[1]

        def send(k):
            @pl.when(here.yl == k)
            def _():
                for made in same:
                    made.start()

            @pl.when(here.yl != k)
            def _():
                for made in other:
                    made.start()

            for made in by_z[k]:
                made.start()

        return send

    def begun(self):
        for made in self.half + self.a + self.b:
            made.wait_recv()

    def resume(self, moves, half_a, half_b, near_a, near_b):
        low, high = pl.ds(0, 2), pl.ds(2, 2)
        self.half = [moves.start(half_a, self.half_a), moves.start(half_b, self.half_b)]
        self.a = [
            moves.start(near_a.at[0], self.landed_a.at[0, high]),
            moves.start(near_a.at[1], self.landed_a.at[1, low]),
        ]
        self.b = [
            moves.start(near_b.at[0], self.landed_b.at[0, 1]),
            moves.start(near_b.at[1], self.landed_b.at[1, 0]),
        ]

    def resumed(self):
        for made in self.half + self.a + self.b:
            made.wait()
        self.half, self.a, self.b = [], [], []

    def middle(self):
        here, g, copy = self.here, self.grads, self.lines.copy
        low, high = pl.ds(0, 2), pl.ds(2, 2)
        (a1, b1), (a3, b3) = self.spots(1), self.spots(3)
        for made in self.half:
            made.wait_recv()
        for spot, half in zip(
            (a1[0], a3[1], b1[0], b3[1]),
            (self.half_a.at[0], self.half_a.at[1], self.half_b.at[0], self.half_b.at[1]),
        ):
            g[spot] = (g[spot].astype(F32) + half[...].astype(F32)).astype(BF16)
        self.a += [
            copy(g.at[a1[0]], self.landed_a.at[0, low], here.to(dy=1)),
            copy(g.at[a3[1]], self.landed_a.at[1, high], here.to(dy=3)),
        ]
        self.b += [
            copy(g.at[b1[0]], self.landed_b.at[0, 0], here.to(dz=1)),
            copy(g.at[b3[1]], self.landed_b.at[1, 1], here.to(dz=3)),
        ]

    def second(self):
        here, g, copy = self.here, self.grads, self.lines.copy
        for made in self.a:
            made.wait_recv()
        for k in range(4):
            total = g[k, here.yh, here.yl, 0].astype(F32)
            for j in range(2):
                total = total + self.landed_a[j, k].astype(F32)
            self.sums_a[k] = total.astype(BF16)
        self.a = []
        for d in (1, 3, 2):
            z = here.to(dz=d)[1] // 4
            self.a.append(copy(self.sums_a.at[z], self.last_a.at[d - 1], here.to(dz=d)))
        for made in self.b:
            made.wait_recv()
        for k in range(4):
            total = g[here.z, k // 2, k % 2, 1].astype(F32)
            for j in range(2):
                total = total + self.landed_b[j, k // 2, k % 2].astype(F32)
            self.sums_b[k // 2, k % 2] = total.astype(BF16)
        self.b = []
        for d in (1, 3, 2):
            _, shard, yl = here.to(dy=d)
            yh = lax.rem(shard // 2, 2)
            self.b.append(copy(self.sums_b.at[yh, yl], self.last_b.at[d - 1], here.to(dy=d)))

    def result(self, path):
        here = self.here
        for made in (self.a, self.b)[path]:
            made.wait_recv()
        own = self.sums_a[here.z] if path == 0 else self.sums_b[here.yh, here.yl]
        last = (self.last_a, self.last_b)[path]
        total = own.astype(F32)
        for j in range(3):
            total = total + last[j].astype(F32)
        return total


def retreat_kernel(
    middle_grad_h, attended_h, context_h, probs_h, kv_h, queries_h, qkv_pre_h, normed_h, tokens_h,
    w_qkv_h, w_out_h, g_down_h, g_in_h, half_a, half_b, near_a, near_b,
    down_half_a, down_half_b, down_near_a, down_near_b,
    cosine, sine, gains, d_gain_in, d_gain_out,
    grad_tokens, laid_h, o_down, o_qkv, o_out,
    laid, row, o_in, middle_grad, attended, context, probs, kv, queries, qkv_pre, normed, tokens, w_qkv, w_out,
    g_down, g_in,
    context_grad, attn_side, kv_part, kv_give, kv_land, g_qkv, g_out, d_gains,
    chip_qkv, chip_out, cross_qkv, cross_out, swap, half_qkv, half_out, land_qkv, land_out, *rest,
):
    here = Place()
    send, recv, moved = rest[-3:]
    x, yl, c = here.x, here.yl, here.c
    moves = Moves(moved)
    lines = Lines(send, recv)
    copy = lines.copy
    sums = [
        PlaneSum(here, lines, g, *rest[8 * k : 8 * k + 8])
        for k, g in enumerate((g_down, chip_qkv, chip_out, g_in))
    ]
    loads = {"g_in": moves.start(g_in_h, g_in)}
    sums[3].resume(moves, half_a, half_b, near_a, near_b)
    loads["g_down"] = moves.start(g_down_h, g_down)
    sums[0].resume(moves, down_half_a, down_half_b, down_near_a, down_near_b)
    loads |= {
        name: moves.start(a, b)
        for name, a, b in (
            ("attended", attended_h, attended),
            ("middle_grad", middle_grad_h, middle_grad),
            ("w_out", w_out_h, w_out),
            ("context", context_h, context),
            ("probs", probs_h, probs),
            ("kv", kv_h, kv),
            ("queries", queries_h, queries),
            ("qkv_pre", qkv_pre_h, qkv_pre),
            ("w_qkv", w_qkv_h, w_qkv),
            ("normed", normed_h, normed),
            ("tokens", tokens_h, tokens),
        )
    }

    def ready(*names):
        for name in names:
            loads[name].wait()

    greet([here.mate()] + plane_peers(here) + [here.to(dx=d) for d in (1, 2, 3)])
    n, width = middle_grad.shape
    head_dim = 2 * cosine.shape[1]
    heads = queries.shape[1] // head_dim
    rows = width // 16
    at = heads * head_dim
    ready("g_in")
    sums[3].resumed()
    sums[3].middle()
    ready("g_down")
    sums[0].resumed()
    sums[0].middle()
    ready("attended", "middle_grad", "w_out", "context")

    att, dy = attended[...], middle_grad[...]
    r, grad = norm_back(att, dy * (1.0 + gains[1:2, :width]), width)
    d_gains[...] = jnp.zeros_like(d_gains)
    d_gains[1:2, :width] = jnp.sum(dy * att * r, axis=0, keepdims=True)
    d_gains[2:3, :width] = d_gain_in[...]
    d_gains[3:4, :width] = d_gain_out[...]
    attended_grad = grad.astype(BF16)
    out_full = w_out[...].reshape(at, width)
    context_grad[...] = dot(attended_grad, out_full, NT).astype(BF16)
    grad_out = dot(context[...], attended_grad, TN)
    g_out[...] = grad_out.astype(BF16).reshape(g_out.shape)
    give_out = copy(g_out.at[:, :, 1 - c], cross_out, here.mate())
    ready("probs", "kv", "queries", "qkv_pre")
    keys = kv[:, :, :head_dim].reshape(2 * n, head_dim)
    values = kv[:, :, head_dim:].reshape(2 * n, head_dim)
    cos_v, sin_v = cosine[...], sine[...]
    q_scale, k_scale = (gains[k : k + 1, width : width + head_dim] for k in (0, 1))
    d_query = jnp.zeros((1, head_dim), F32)
    for h in range(heads):
        cols = slice(h * head_dim, (h + 1) * head_dim)
        low = probs[h]
        high = low.astype(F32)
        prob_grad = dot(context_grad[:, cols], values, NT)
        inner = jnp.sum(high * prob_grad, axis=-1, keepdims=True)
        score_grad = (high * (prob_grad - inner)).astype(BF16)
        key_part = dot(score_grad, queries[:, cols], TN)
        value_part = dot(low, context_grad[:, cols], TN)
        if h == 0:
            kv_part[:, :, :head_dim] = key_part.reshape(2, n, head_dim)
            kv_part[:, :, head_dim:] = value_part.reshape(2, n, head_dim)
        else:
            kv_part[:, :, :head_dim] += key_part.reshape(2, n, head_dim)
            kv_part[:, :, head_dim:] += value_part.reshape(2, n, head_dim)
        query_grad = dot(score_grad, keys).astype(BF16).astype(F32)
        side, d_scale = head_backward(
            query_grad, qkv_pre[:, cols], q_scale, cos_v, sin_v, head_dim**-0.5
        )
        attn_side[:, cols] = side
        d_query = d_query + d_scale
        if h == 1:
            sums[3].second()
        if h == 2:
            sums[0].second()
    kv_give[...] = kv_part[1 - yl].astype(BF16)
    kv_sent = copy(kv_give, kv_land, here.pair())
    ready("w_qkv", "normed", "tokens")
    normed_grad = dot(attn_side[:, :at], w_qkv[:, :at], NT)
    grad_query = dot(normed[...], attn_side[:, :at], TN)
    for path in (0, 1):
        swap[path] = sums[3].result(path).astype(BF16)
    across = copy(swap.at[1 - c], o_in.at[x, yl, c], here.mate())
    o_in[x, yl, c] = swap[c]
    for path in (0, 1):
        o_down[x, yl, path] = sums[0].result(path).astype(BF16)
    down_pair = copy(o_down.at[x, yl], o_down.at[x, yl], here.pair())
    give_out.wait_recv()
    across.wait_recv()
    in_pair = copy(o_in.at[x, yl], o_in.at[x, yl], here.pair())
    for z in range(4):
        for yh in range(2):
            chip_out[z, yh] = (g_out[z, yh, c].astype(F32) + cross_out[z, yh].astype(F32)).astype(BF16)
    kv_sent.wait_recv()
    kv_grad = (kv_part[yl] + kv_land[...].astype(F32)).astype(BF16)
    side, d_key = head_backward(
        kv_grad[:, :head_dim].astype(F32), qkv_pre[:, at : at + head_dim], k_scale, cos_v, sin_v, 1.0
    )
    attn_side[:, at : at + head_dim] = side
    attn_side[:, at + head_dim :] = kv_grad[:, head_dim:]
    d_gains[0:1, width : width + head_dim] = d_query
    d_gains[1:2, width : width + head_dim] = d_key
    down_pair.wait_recv()
    down_x = [copy(o_down.at[x], o_down.at[x], here.to(dx=d)) for d in (1, 3, 2)]

    normed_grad = normed_grad + dot(attn_side[:, at:], w_qkv[:, at:], NT)
    tok = tokens[...].astype(F32)
    r, grad = norm_back(tok, normed_grad * (1.0 + gains[0:1, :width]), width)
    grad_tokens[...] = (middle_grad[...] + grad).astype(BF16)
    d_gains[0:1, :width] = jnp.sum(normed_grad * tok * r, axis=0, keepdims=True)
    grad_kv = dot(normed[...], attn_side[:, at:], TN)
    wide = g_qkv.shape[-1]
    for p in range(4):
        cols = slice(p * wide, (p + 1) * wide)
        for f in range(16):
            spot = (f // 4, (f // 2) % 2, f % 2, p // 2, p % 2)
            span = slice(rows * f, rows * f + rows)
            parts = []
            if p * wide < at:
                parts.append(grad_query[span, p * wide : min((p + 1) * wide, at)])
            if (p + 1) * wide > at:
                parts.append(grad_kv[span, max(p * wide - at, 0) : (p + 1) * wide - at])
            block = parts[0] if len(parts) == 1 else jnp.concatenate(parts, axis=1)
            g_qkv[spot] = jnp.concatenate([block, d_gains[:, cols]], axis=0).astype(BF16)
    give_qkv = copy(g_qkv.at[:, :, 1 - c], cross_qkv, here.mate())
    sums[2].first()
    in_pair.wait_recv()
    right, left = here.to(dx=1), here.to(dx=3)
    own = [o_in.at[x, m] for m in (0, 1)]
    early = [copy(own[0], own[0], right), copy(own[1], own[1], left)]
    late = [copy(own[1], own[1], right), copy(own[0], own[0], left)]
    give_qkv.wait_recv()
    for z in range(4):
        for yh in range(2):
            chip_qkv[z, yh] = (g_qkv[z, yh, c].astype(F32) + cross_qkv[z, yh].astype(F32)).astype(BF16)
    sums[1].first()
    sums[2].middle()
    sums[1].middle()
    for made, at_x, m, to in ((early[0], left[0], 0, right), (early[1], right[0], 1, left)):
        made.wait_recv()
        late.append(copy(o_in.at[at_x, m], o_in.at[at_x, m], to))
    sums[2].second()
    sums[1].second()
    for path in (0, 1):
        half_out[path] = sums[2].result(path).astype(BF16)
        half_qkv[path] = sums[1].result(path).astype(BF16)
    by_x = []
    for d in (1, 3, 2):
        by_x.append(copy(half_qkv, land_qkv.at[d - 1], here.to(dx=d)))
        by_x.append(copy(half_out, land_out.at[d - 1], here.to(dx=d)))
    for made in late:
        made.wait_recv()
    block = row.shape[1] // 16
    for m in range(2):
        for k in range(4):
            count = min(PART, block - PART * k)
            for f in range(16):
                piece = o_in[k, m, f % 2].astype(F32)[:, PART * (f // 2) : PART * (f // 2) + count]
                row[:, block * f + PART * k : block * f + PART * k + count] = piece
        laid[m] = row[...].astype(BF16)
        moves.store(laid.at[m], laid_h.at[m])
    for made in by_x:
        made.wait_recv()
    for half, land, out in ((half_qkv, land_qkv, o_qkv), (half_out, land_out, o_out)):
        for path in (0, 1):
            total = half[path].astype(F32)
            for j in range(3):
                total = total + land[j, path].astype(F32)
            out[yl, path] = total.astype(BF16)
    ends = [copy(o.at[yl], o.at[yl], here.pair()) for o in (o_qkv, o_out)]
    for made in down_x + ends:
        made.wait_recv()
    lines.drain()
    moves.drain()


def retreat_block(*args):
    (
        middle_grad, attended, context, probs, kv, queries, qkv_pre, normed, tokens, w_qkv, w_out,
        g_down, g_in, *_, cosine, _, _, _, _,
    ) = args
    vmem, hbm = pl.BlockSpec(memory_space=pltpu.VMEM), pl.BlockSpec(memory_space=pl.ANY)
    shape = jax.ShapeDtypeStruct
    n, width = middle_grad.shape
    out_width, head_dim = queries.shape[1], 2 * cosine.shape[1]
    cols = qkv_pre.shape[1]
    p_in, p_down, p_out = g_in.shape[4:], g_down.shape[4:], w_out.shape[5:]
    p_qkv = (width // 16 + 8, cols // 4)
    vm = lambda *s: pltpu.VMEM(s, BF16)
    units = 16 * UNITS_OF_SHARD
    scratch = [vm(2, width // 16, units), pltpu.VMEM((width // 16, units), F32), vm(4, 2, 2, *p_in)]
    scratch += [pltpu.VMEM(a.shape, a.dtype) for a in args[:11]]
    scratch += [vm(*g_down.shape), vm(*g_in.shape)]
    scratch += [vm(n, out_width), vm(n, cols), pltpu.VMEM((2, n, 2 * head_dim), F32)]
    scratch += [vm(n, 2 * head_dim)] * 2
    scratch += [vm(4, 2, 2, 2, 2, *p_qkv), vm(4, 2, 2, 2, 2, *p_out), pltpu.VMEM((8, cols), F32)]
    scratch += [vm(4, 2, 2, 2, *p_qkv), vm(4, 2, 2, 2, *p_out)] * 2
    scratch += [vm(2, *p_in), vm(2, *p_qkv), vm(2, *p_out), vm(3, 2, *p_qkv), vm(3, 2, *p_out)]
    for piece in (p_down, p_qkv, p_out, p_in):
        scratch += PlaneSum.scratch(piece)
    scratch += [pltpu.SemaphoreType.DMA((79,))] * 2 + [pltpu.SemaphoreType.DMA((27,))]
    low = lambda *s: shape(s, BF16)
    return pl.pallas_call(
        retreat_kernel,
        out_shape=(
            low(n, width),
            low(2, width // 16, units),
            low(4, 2, 2, *p_down),
            low(2, 2, *p_qkv),
            low(2, 2, *p_out),
        ),
        in_specs=[hbm] * 21 + [vmem] * 5,
        out_specs=(vmem, hbm) + (vmem,) * 3,
        scratch_shapes=scratch,
        compiler_params=pltpu.CompilerParams(
            collective_id=2, has_side_effects=True, vmem_limit_bytes=63 * MIB
        ),
        name="retreat",
    )(*args)


def finish_kernel(
    o_in_h, o_down_h, o_qkv_h, o_out_h, shown_h, taken_h,
    layer_out_h, grad_tokens_h, out_query, out_key, out_value, out_out, out_gate_h, out_up_h, out_down_h,
    *rest,
):
    out_gains = rest[:6]
    o_in, o_down, o_qkv, o_out, out_gate, out_up, out_down, shown, taken, moved = rest[6:]
    moves = Moves(moved)
    load_in = [moves.start(o_in_h.at[m], o_in.at[m]) for m in (0, 1)]
    load_tokens = [moves.start(shown_h, shown), moves.start(taken_h, taken)]
    load_down = moves.start(o_down_h, o_down)
    load_rest = [moves.start(o_qkv_h, o_qkv), moves.start(o_out_h, o_out)]
    rows, units = out_gate.shape
    block = units // 16
    wide = o_qkv.shape[-1]
    at, head_dim = out_query.shape[1], out_key.shape[1]
    for m, out, out_h in ((0, out_gate, out_gate_h), (1, out_up, out_up_h)):
        load_in[m].wait()
        out[...] = o_in[m].astype(F32)
        moves.store(out, out_h)
    for made, held, out_h in zip(load_tokens, (shown, taken), (layer_out_h, grad_tokens_h)):
        made.wait()
        moves.store(held, out_h)
    load_down.wait()
    for k in range(4):
        for p in range(4):
            start = PART * k + 32 * p
            count = min(32, PART - 32 * p, block - start)
            if count > 0:
                out_down[start : start + count] = o_down[k, p // 2, p % 2, :count].astype(F32)
    moves.store(out_down, out_down_h)
    for made in load_rest:
        made.wait()
    tail = []
    for p in range(4):
        piece = o_qkv[p // 2, p % 2].astype(F32)
        for out, start in ((out_query, 0), (out_key, at), (out_value, at + head_dim)):
            lo, hi = max(p * wide, start), min((p + 1) * wide, start + out.shape[1])
            if lo < hi:
                out[:, lo - start : hi - start] = piece[:rows, lo - p * wide : hi - p * wide]
        tail.append(piece[rows:])
        height = o_out.shape[2]
        out_out[p * height : (p + 1) * height] = o_out[p // 2, p % 2].astype(F32)
    tail = jnp.concatenate(tail, axis=1)
    width = out_out.shape[1]
    shard = lax.axis_index("fsdp")
    turned = pltpu.roll(tail[:, :width], lax.rem(width - rows * shard, width), 1)
    for k in range(4):
        out_gains[k][...] = turned[k, :rows]
    piece = head_dim // 16
    turned = pltpu.roll(tail[:, width : width + head_dim], lax.rem(head_dim - piece * shard, head_dim), 1)
    for k in range(2):
        out_gains[4 + k][...] = turned[k, :piece]
    moves.drain()


def finish_block(o_in, o_down, o_qkv, o_out, layer_out, grad_tokens, out_shape):
    vmem, hbm = pl.BlockSpec(memory_space=pltpu.VMEM), pl.BlockSpec(memory_space=pl.ANY)
    big = out_shape[6:9]
    return pl.pallas_call(
        finish_kernel,
        out_shape=out_shape,
        in_specs=[hbm] * 6,
        out_specs=(hbm,) * 2 + (vmem,) * 4 + (hbm,) * 3 + (vmem,) * 6,
        scratch_shapes=[pltpu.VMEM(a.shape, a.dtype) for a in (o_in, o_down, o_qkv, o_out, *big, layer_out, grad_tokens)]
        + [pltpu.SemaphoreType.DMA((12,))],
        compiler_params=pltpu.CompilerParams(vmem_limit_bytes=62 * MIB),
        name="finish",
    )(o_in, o_down, o_qkv, o_out, layer_out, grad_tokens)


def body(
    tokens,
    w_query,
    w_key,
    w_value,
    w_out,
    w_gate,
    w_up,
    w_down,
    pre_attn_gain,
    post_attn_gain,
    pre_mlp_gain,
    post_mlp_gain,
    query_gain,
    key_gain,
    cotangent,
):
    n, width = tokens.shape
    rows = w_query.shape[0]
    head_dim = w_key.shape[1]
    out_width = w_query.shape[1]
    shard = lax.axis_index("fsdp")

    mine = jnp.arange(16) == shard
    spread = lambda g: jnp.where(mine[:, None], g[None, :], 0).reshape(1, -1)
    gains_d = [spread(g) for g in (pre_attn_gain, post_attn_gain, pre_mlp_gain, post_mlp_gain)]
    gains_h = jnp.concatenate([spread(query_gain), spread(key_gain)], axis=0)
    tail = jnp.concatenate(
        [
            jnp.pad(jnp.concatenate(gains_d, axis=0), ((0, 4), (0, 0))),
            jnp.pad(gains_h, ((0, 6), (0, out_width + head_dim - width))),
        ],
        axis=1,
    )
    own_out = w_out.reshape(2, 2, -1, width)
    positions = (lax.axis_index("seq") * n + jnp.arange(n, dtype=jnp.int32)).astype(F32)
    frequency = jnp.exp(
        jnp.arange(head_dim // 2, dtype=F32) * (-2.0 * math.log(1000000.0) / head_dim)
    )
    angles = positions[:, None] * frequency[None, :]
    cosine, sine = jnp.cos(angles), jnp.sin(angles)

    (
        xs, gate_full, up_full, down_full, w_qkv, w_out_full, normed, queries, kv, probs, context,
        attended, qkv_pre, middle, gains,
    ) = attend_block(
        tokens, cosine, sine, tail, w_query, w_key, w_value, own_out, w_gate, w_up, w_down
    )
    layer_out, middle_grad, d_gain_in, d_gain_out, *begun, g_in, g_down = mlp_block(
        xs, middle, cotangent, gains, gate_full, up_full, down_full
    )
    grad_tokens, o_in, o_down, o_qkv, o_out = retreat_block(
        middle_grad, attended, context, probs, kv, queries, qkv_pre, normed, tokens, w_qkv,
        w_out_full, g_down, g_in, *begun, cosine, sine, gains, d_gain_in, d_gain_out,
    )
    like = lambda a, kind: jax.ShapeDtypeStruct(a.shape, kind)
    weights = (w_query, w_key, w_value, w_out, w_gate, w_up, w_down)
    gain_args = (pre_attn_gain, post_attn_gain, pre_mlp_gain, post_mlp_gain, query_gain, key_gain)
    shapes = [like(tokens, BF16)] * 2 + [like(a, F32) for a in weights + gain_args]
    return tuple(finish_block(o_in, o_down, o_qkv, o_out, layer_out, grad_tokens, shapes))


def solution(mesh):
    tokens = P(("dp", "fsdp", "seq"), None)
    weight, gain = P("fsdp", None), P("fsdp")
    return jax.shard_map(
        body,
        mesh=mesh,
        in_specs=(tokens,) + (weight,) * 7 + (gain,) * 6 + (tokens,),
        out_specs=(tokens,) * 2 + (weight,) * 7 + (gain,) * 6,
        check_vma=False,
    )
```

```python
import functools
import math

import jax
import jax.numpy as jnp
from jax import lax
from jax.experimental import pallas as pl
from jax.experimental.pallas import tpu as pltpu
from jax.sharding import PartitionSpec as P

F32, BF16 = jnp.float32, jnp.bfloat16
MESH = pl.DeviceIdType.MESH
NN = (((1,), (0,)), ((), ()))
NT = (((1,), (1,)), ((), ()))
TN = (((0,), (0,)), ((), ()))
EPS = 1e-06
MIB = 2**20
PART = 112
CORE_UNITS = 8 * PART
UNITS_OF_SHARD = 432


def dot(a, b, dims=NN):
    return lax.dot_general(a, b, dims, preferred_element_type=F32)


class Place:
    def __init__(self):
        shard = lax.axis_index("fsdp")
        self.x = lax.axis_index("dp")
        self.z = shard // 4
        self.yh = lax.rem(shard // 2, 2)
        self.c = lax.rem(shard, 2)
        self.yl = lax.axis_index("seq")

    def to(self, dx=0, dy=0, dz=0, dc=0):
        x, z, yh, yl, c = self.x, self.z, self.yh, self.yl, self.c
        if dx:
            x = lax.rem(x + dx, 4)
        if dz:
            z = lax.rem(z + dz, 4)
        if dy:
            y = lax.rem(yh * 2 + yl + dy, 4)
            yh, yl = y // 2, lax.rem(y, 2)
        if dc:
            c = 1 - c
        return (x, (z * 2 + yh) * 2 + c, yl)

    def mate(self):
        return self.to(dc=1)

    def pair(self):
        return (self.x, (self.z * 2 + self.yh) * 2 + self.c, 1 - self.yl)


def greet(peers):
    barrier = pltpu.get_barrier_semaphore()
    for peer in peers:
        pl.semaphore_signal(barrier, inc=1, device_id=peer, device_id_type=MESH)
    pl.semaphore_wait(barrier, len(peers))


class Moves:
    def __init__(self, sems):
        self.sems, self.used, self.open = sems, 0, []

    def start(self, src, dst):
        made = pltpu.make_async_copy(src, dst, self.sems.at[self.used])
        self.used += 1
        made.start()
        return made

    def store(self, src, dst):
        self.open.append(self.start(src, dst))

    def drain(self):
        for made in self.open:
            made.wait()
        self.open = []


class Lines:
    def __init__(self, send, recv):
        self.send, self.recv, self.used, self.open = send, recv, 0, []

    def copy(self, src, dst, device):
        made = self.plan(src, dst, device)
        made.start()
        return made

    def plan(self, src, dst, device):
        k = self.used
        self.used += 1
        made = pltpu.make_async_remote_copy(
            src_ref=src,
            dst_ref=dst,
            send_sem=self.send.at[k],
            recv_sem=self.recv.at[k],
            device_id=device,
            device_id_type=MESH,
        )
        self.open.append(made)
        return made

    def drain(self):
        for made in self.open:
            made.wait_send()
        self.open = []


def gate_terms(gate, up):
    k, c = math.sqrt(2.0 / math.pi), 0.044715
    square = gate * gate
    t = jnp.tanh(gate * (k + (k * c) * square))
    half = 0.5 + 0.5 * t
    act = gate * half
    slope = half + 0.5 * gate * (1.0 - t * t) * (k + (3.0 * k * c) * square)
    return act, slope * up, act * up


class RingGather:
    def __init__(self, here, lines, own, full):
        self.here, self.lines, self.own, self.full = here, lines, own, full

    def start(self):
        here, own, full, copy = self.here, self.own, self.full, self.lines.copy
        n = own.shape[0]
        h = n // 2
        right, left = here.to(dx=1), here.to(dx=3)
        lo, hi = pl.ds(0, h), pl.ds(h, h)
        self.core = copy(own, full.at[0, pl.ds(n, n)], here.mate())
        self.a0 = copy(own.at[lo], full.at[3, lo], right)
        self.b0 = copy(own.at[hi], full.at[1, hi], left)
        self.a1 = copy(own.at[hi], full.at[3, hi], right)
        self.b1 = copy(own.at[lo], full.at[1, lo], left)
        full[0, :n] = own[...]

    def start_low(self):
        here, own, full, copy = self.here, self.own, self.full, self.lines.copy
        lo = pl.ds(0, own.shape[0] // 2)
        self.a0 = copy(own.at[lo], full.at[3, lo], here.to(dx=1))
        self.b1 = copy(own.at[lo], full.at[1, lo], here.to(dx=3))

    def start_high(self):
        here, own, full, copy = self.here, self.own, self.full, self.lines.copy
        n = own.shape[0]
        hi = pl.ds(n // 2, n // 2)
        self.b0 = copy(own.at[hi], full.at[1, hi], here.to(dx=3))
        self.a1 = copy(own.at[hi], full.at[3, hi], here.to(dx=1))
        self.core = copy(own, full.at[0, pl.ds(n, n)], here.mate())
        full[0, :n] = own[...]

    def ready0(self):
        self.core.wait_recv()

    def relay(self):
        here, full, copy = self.here, self.full, self.lines.copy
        n = self.own.shape[0]
        h = n // 2
        lo, hi = pl.ds(0, h), pl.ds(h, h)
        right, left = here.to(dx=1), here.to(dx=3)
        self.a0.wait_recv()
        self.a2 = copy(full.at[3, lo], full.at[2, lo], right)
        self.b0.wait_recv()
        self.b2 = copy(full.at[1, hi], full.at[2, hi], left)

    def forward(self):
        full, copy = self.full, self.lines.copy
        n = self.own.shape[0]
        both, other = pl.ds(0, n), pl.ds(n, n)
        mate = self.here.mate()
        self.a1.wait_recv()
        self.f3 = copy(full.at[3, both], full.at[3, other], mate)
        self.b1.wait_recv()
        self.f1 = copy(full.at[1, both], full.at[1, other], mate)

    def ready3(self):
        self.f3.wait_recv()

    def ready1(self):
        self.f1.wait_recv()

    def ready2(self):
        n = self.own.shape[0]
        self.a2.wait_recv()
        self.b2.wait_recv()
        f2 = self.lines.copy(
            self.full.at[2, pl.ds(0, n)], self.full.at[2, pl.ds(n, n)], self.here.mate()
        )
        f2.wait_recv()


class RingSum:
    def __init__(self, here, lines, mine, landed, cross, stage_core, stage_ring):
        self.here, self.lines, self.mine = here, lines, mine
        self.landed, self.cross = landed, cross
        self.stage_core, self.stage_ring = stage_core, stage_ring
        self.pending = []

    def add(self, r, term):
        here = self.here
        self.stage_core[r] = term(1).astype(BF16)
        made = self.lines.copy(self.stage_core.at[r], self.cross.at[r], here.mate())
        near = term(0)
        made.wait_recv()
        near = near + self.cross[r].astype(F32)
        if r == 0:
            self.mine[...] = near
        else:
            self.stage_ring[r - 1] = near.astype(BF16)
            self.pending.append(
                self.lines.copy(
                    self.stage_ring.at[r - 1], self.landed.at[3 - r], here.to(dx=r)
                )
            )

    def total(self):
        for made in self.pending:
            made.wait_recv()
        out = self.mine[...]
        for j in range(3):
            out = out + self.landed[j].astype(F32)
        return out


def norm_back(v, u, n):
    r = lax.rsqrt(jnp.sum(v * v, axis=-1, keepdims=True) * (1.0 / n) + EPS)
    inner = jnp.sum(u * v, axis=-1, keepdims=True) * (1.0 / n)
    return r, r * u - v * (r * r * r * inner)


def mlp_kernel(
    xs_h, middle_h, cot_h, gains, w_gate_h, w_up_h, w_down_h,
    layer_out, middle_grad, d_gain_in, d_gain_out, half_a, half_b, near_a, near_b,
    down_half_a, down_half_b, down_near_a, down_near_b, d_in_h, d_down_h,
    xs, middle, cot, w_gate, w_up, w_down, d_in, gs, act, slope, hidden, cross_f, cross_b, landed_f, landed_b, stage_core, stage_ring,
    mine, mixed_grad, d_down, *rest,
):
    here = Place()
    moves = Moves(rest[-1])
    load_first = [
        moves.start(a, b)
        for a, b in ((xs_h.at[2], xs.at[2]), (w_gate_h, w_gate), (w_up_h, w_up), (w_down_h, w_down))
    ]
    load_xs = {r: moves.start(xs_h.at[r], xs.at[r]) for r in (3, 1, 0)}
    load_last = [moves.start(a, b) for a, b in ((middle_h, middle), (cot_h, cot))]
    greet([here.mate()] + [here.to(dx=d) for d in (1, 2, 3)] + plane_peers(here))
    lines = Lines(*rest[-3:-1])
    n, width = middle.shape
    gain_in, gain_out = gains[2:3, :width], gains[3:4, :width]

    sums = RingSum(here, lines, mine, landed_f, cross_f, stage_core, stage_ring)
    in_sum = PlaneSum(here, lines, d_in, *[None] * 8)
    down_sum = PlaneSum(here, lines, d_down, *[None] * 8)

    def forward(r):
        x = xs[r]
        a, s, h = gate_terms(dot(x, w_gate[...]), dot(x, w_up[...]))
        act[r] = a.astype(BF16)
        slope[r] = s.astype(BF16)
        hidden[r] = h.astype(BF16)
        sums.add(r, lambda q: dot(hidden[r, q * n : (q + 1) * n], w_down[...]))

    for made in load_first:
        made.wait()
    forward(2)
    for r in (3, 1, 0):
        load_xs[r].wait()
        forward(r)
    for made in load_last:
        made.wait()
    mixed = sums.total()
    lines.drain()

    cot_f = cot[...].astype(F32)
    u = cot_f * (1.0 + gain_out)
    factor, grad = norm_back(mixed, u, width)
    mixed_grad[...] = grad.astype(BF16)

    ring = RingGather(here, lines, mixed_grad, gs)
    sums = RingSum(here, lines, mine, landed_b, cross_b, stage_core, stage_ring)
    ring.start()
    layer_out[...] = (middle[...] + mixed * factor * (1.0 + gain_out)).astype(BF16)
    d_gain_out[...] = jnp.sum(cot_f * mixed * factor, axis=0, keepdims=True)

    def backward(r):
        hidden_grad = dot(gs[r], w_down[...], NT)
        act[r] = (hidden_grad * act[r].astype(F32)).astype(BF16)
        slope[r] = (hidden_grad * slope[r].astype(F32)).astype(BF16)

        def term(q):
            rows = slice(q * n, (q + 1) * n)
            return dot(slope[r, rows], w_gate[...], NT) + dot(act[r, rows], w_up[...], NT)

        sums.add(r, term)

    ring.ready0()
    backward(0)
    ring.relay()
    ring.forward()
    ring.ready3()
    backward(3)
    ring.ready1()
    backward(1)
    ring.ready2()
    backward(2)

    flat = lambda ref: ref[...].reshape(ref.shape[0] * ref.shape[1], ref.shape[2])
    send_in = in_sum.begin_by_owner(half_a, half_b, near_a, near_b)
    for mat, side in ((0, slope), (1, act)):
        grad_side = dot(flat(xs), flat(side), TN)
        for f in range(16):
            d_in[f // 4, (f // 2) % 2, mat, f % 2] = grad_side[72 * f : 72 * f + 72].astype(BF16)
        send_in(mat)
    moves.store(d_in, d_in_h)
    grad_down = dot(flat(hidden), flat(gs), TN)
    for k in range(8):
        for p in range(4):
            rows = min(32, PART - 32 * p)
            at = PART * k + 32 * p
            d_down[k // 2, k % 2, p // 2, p % 2, :rows] = grad_down[at : at + rows].astype(BF16)
        d_down[k // 2, k % 2, 1, 1, PART - 96 :] = jnp.zeros((128 - PART, width), BF16)
    down_sum.begin(
        down_half_a, down_half_b, [down_near_a.at[0], down_near_a.at[1]],
        [down_near_b.at[0], down_near_b.at[1]],
    )
    moves.store(d_down, d_down_h)

    update = sums.total()
    base = middle[...]
    u = update * (1.0 + gain_in)
    factor, grad = norm_back(base, u, width)
    d_gain_in[...] = jnp.sum(update * base * factor, axis=0, keepdims=True)
    middle_grad[...] = cot[...].astype(F32) + grad
    down_sum.begun()
    in_sum.begun()
    lines.drain()
    moves.drain()


def mlp_block(xs, middle, cot, gains, w_gate, w_up, w_down):
    n, width = middle.shape
    units = w_gate.shape[1]
    vmem, hbm = pl.BlockSpec(memory_space=pltpu.VMEM), pl.BlockSpec(memory_space=pl.ANY)
    shape = jax.ShapeDtypeStruct
    d_in = shape((4, 2, 2, 2, width // 16, units), BF16)
    d_down = shape((4, 2, 2, 2, 32, width), BF16)
    scratch = (
        [pltpu.VMEM(a.shape, a.dtype) for a in (xs, middle, cot, w_gate, w_up, w_down, d_in)]
        + [pltpu.VMEM((4, 2 * n, width), BF16)]
        + [pltpu.VMEM((4, 2 * n, units), BF16)] * 3
        + [pltpu.VMEM((4, n, width), BF16)] * 2
        + [pltpu.VMEM((3, n, width), BF16)] * 2
        + [pltpu.VMEM((4, n, width), BF16), pltpu.VMEM((3, n, width), BF16)]
        + [pltpu.VMEM((n, width), F32), pltpu.VMEM((n, width), BF16)]
        + [pltpu.VMEM(d_down.shape, BF16)]
        + [pltpu.SemaphoreType.DMA((44,))] * 2
        + [pltpu.SemaphoreType.DMA((11,))]
    )
    return pl.pallas_call(
        mlp_kernel,
        out_shape=(
            shape((n, width), BF16),
            shape((n, width), F32),
            shape((1, width), F32),
            shape((1, width), F32),
            *[shape((2, 2, *d_in.shape[4:]), BF16)] * 4,
            *[shape((2, 2, *d_down.shape[4:]), BF16)] * 4,
            d_in,
            d_down,
        ),
        in_specs=[hbm] * 3 + [vmem] + [hbm] * 3,
        out_specs=(vmem,) * 12 + (hbm,) * 2,
        scratch_shapes=scratch,
        compiler_params=pltpu.CompilerParams(
            collective_id=1, has_side_effects=True, vmem_limit_bytes=63 * MIB
        ),
        name="mlp_block",
    )(xs, middle, cot, gains, w_gate, w_up, w_down)


def plane_peers(here):
    return [here.to(dz=d) for d in (1, 2, 3)] + [here.to(dy=d) for d in (1, 2, 3)]


class PlaneGather:
    def __init__(self, here, lines, local, own, full):
        self.here, self.lines, self.local, self.own, self.full = here, lines, local, own, full

    def first(self):
        here, own, full, copy = self.here, self.own, self.full, self.lines.copy
        z, yh, yl = here.z, here.yh, here.yl
        keep = pltpu.make_async_copy(own.at[yl], full.at[z, yh, yl], self.local)
        keep.start()
        self.a, self.b = [], []
        for d in (1, 3, 2):
            self.a.append(copy(own.at[yl, 0], full.at[z, yh, yl, 0], here.to(dz=d)))
            self.b.append(copy(own.at[yl, 1], full.at[z, yh, yl, 1], here.to(dy=d)))
        keep.wait()

    def blocks(self, dy, dz):
        _, shard, yl = self.here.to(dy=dy)
        yh = lax.rem(shard // 2, 2)
        z = self.here.to(dz=dz)[1] // 4
        full = self.full
        return (
            [full.at[pl.ds(0, 2), yh, yl, 0], full.at[pl.ds(2, 2), yh, yl, 0]],
            [full.at[z, 0, :, 1], full.at[z, 1, :, 1]],
        )

    def second(self):
        here, copy = self.here, self.lines.copy
        for made in self.a + self.b:
            made.wait_recv()
        by_y, by_z = self.blocks(0, 0)
        self.early, self.late = [], []
        for block, up, down in (
            (by_y, here.to(dy=1), here.to(dy=3)),
            (by_z, here.to(dz=1), here.to(dz=3)),
        ):
            self.early.append(copy(block[0], block[0], up))
            self.early.append(copy(block[1], block[1], down))
        for block, up, down in (
            (by_y, here.to(dy=1), here.to(dy=3)),
            (by_z, here.to(dz=1), here.to(dz=3)),
        ):
            self.late.append(copy(block[1], block[1], up))
            self.late.append(copy(block[0], block[0], down))

    def relay(self):
        here, copy = self.here, self.lines.copy
        left_y, left_z = self.blocks(3, 3)
        right_y, right_z = self.blocks(1, 1)
        for made, block, to in zip(
            self.early,
            (left_y[0], right_y[1], left_z[0], right_z[1]),
            (here.to(dy=1), here.to(dy=3), here.to(dz=1), here.to(dz=3)),
        ):
            made.wait_recv()
            self.late.append(copy(block, block, to))

    def wait(self):
        for made in self.late:
            made.wait_recv()


def head_forward(pre, scale, cosine, sine, factor):
    r = lax.rsqrt(jnp.mean(pre * pre, axis=-1, keepdims=True) + EPS)
    v = pre * r * (1.0 + scale)
    half = v.shape[1] // 2
    a, b = v[:, :half], v[:, half:]
    turned = jnp.concatenate([a * cosine - b * sine, b * cosine + a * sine], axis=1)
    return (turned * factor).astype(BF16)


def head_backward(grad, pre, scale, cosine, sine, factor):
    grad = grad * factor
    half = grad.shape[1] // 2
    a, b = grad[:, :half], grad[:, half:]
    dy = jnp.concatenate([a * cosine + b * sine, b * cosine - a * sine], axis=1)
    r, out = norm_back(pre, dy * (1.0 + scale), pre.shape[1])
    return out.astype(BF16), jnp.sum(dy * pre * r, axis=0, keepdims=True)


def attend_kernel(
    tokens, cosine, sine, tail, w_query, w_key, w_value, own_out, w_gate_h, w_up_h, w_down_h,
    *refs,
):
    kept = refs[:14]
    gains = refs[14]
    held = refs[15:29]
    (
        xs, gate_full, up_full, down_full, w_qkv, w_out, normed, queries, kv, probs, context,
        attended, qkv_pre, middle,
    ) = held
    mlp_in, own_qkv, own_in, own_down, full_qkv, full_in, full_down, chip_in = refs[29:37]
    w_gate, w_up, w_down, send, recv, local, moved = refs[37:]
    moves = Moves(moved)
    load_gate, load_up, load_down = [
        moves.start(a, b) for a, b in ((w_gate_h, w_gate), (w_up_h, w_up), (w_down_h, w_down))
    ]
    place = {id(a): b for a, b in zip(held, kept)}
    keep = lambda ref: moves.store(ref, place[id(ref)])
    here = Place()
    x_at, c, yl = here.x, here.c, here.yl
    n, width = tokens.shape
    rows, units = w_gate.shape
    block = units // 16
    head_dim = w_key.shape[1]
    at = w_query.shape[1]
    heads = at // head_dim
    wide = own_qkv.shape[-1]
    lines = Lines(send, recv)
    gather = [
        PlaneGather(here, lines, local.at[k], own, full)
        for k, (own, full) in enumerate(
            (
                (own_qkv, full_qkv.at[:, :, c]),
                (own_out, w_out.at[:, :, c]),
                (chip_in, full_in),
                (own_down, full_down),
            )
        )
    ]

    sides = [(w_query, 0), (w_key, at), (w_value, at + head_dim)]
    for p in range(4):
        for side, start in sides:
            lo, hi = max(p * wide, start), min((p + 1) * wide, start + side.shape[1])
            if lo < hi:
                own_qkv[p // 2, p % 2, :rows, lo - p * wide : hi - p * wide] = side[
                    :, lo - start : hi - start
                ]
        own_qkv[p // 2, p % 2, rows:] = tail[:, p * wide : (p + 1) * wide]
    greet([here.mate()] + plane_peers(here) + [here.to(dx=d) for d in (1, 2, 3)])
    gather[0].first()
    gather[1].first()
    lane = lax.broadcasted_iota(jnp.int32, (rows, PART), 1)
    inside = lane < block - x_at * PART
    for mat, weight, load in ((0, w_gate, load_gate), (1, w_up, load_up)):
        load.wait()
        turned = pltpu.roll(weight[...].astype(F32), lax.rem(units - PART * x_at, units), 1)
        for core in range(2):
            parts = [
                jnp.where(inside, turned[:, block * f : block * f + PART], 0.0)
                for f in range(core, 16, 2)
            ]
            own_in[core, mat] = jnp.concatenate(parts, axis=1).astype(BF16)
    across = lines.copy(own_in.at[1 - c], chip_in.at[:, c], here.mate())
    chip_in[:, c] = own_in[c]
    gather[0].second()
    load_down.wait()
    for p in range(3):
        start = pl.multiple_of(PART * x_at + 32 * p, 16)
        own_down[p // 2, p % 2] = w_down[pl.ds(start, 32)]
    start = pl.multiple_of(jnp.minimum(PART * x_at + 96, block - 16), 16)
    last = w_down[pl.ds(start, 16)].astype(F32)
    own_down[1, 1, :16] = jnp.where(x_at < 3, last, 0.0).astype(BF16)
    own_down[1, 1, 16:] = jnp.zeros((16, width), BF16)
    x = tokens[...].astype(F32)
    lean = x * lax.rsqrt(jnp.mean(x * x, axis=-1, keepdims=True) + EPS)
    gather[0].relay()
    gather[1].second()
    across.wait_recv()
    gather[2].first()
    gather[0].wait()
    core_qkv = [
        lines.copy(full_qkv.at[:, :, c, k], full_qkv.at[:, :, c, k], here.mate()) for k in (0, 1)
    ]
    for p in range(4):
        if p % 2 == 0:
            core_qkv[p // 2].wait_recv()
        if p == 1:
            gather[1].relay()
        total = jnp.zeros((8, wide), F32)
        cols = slice(p * wide, (p + 1) * wide)
        for f in range(16):
            part = full_qkv[f // 4, (f // 2) % 2, f % 2, p // 2, p % 2]
            w_qkv[rows * f : rows * f + rows, cols] = part[:rows]
            total = total + part.astype(F32)[rows : rows + 8]
        gains[:, cols] = total
    keep(w_qkv)
    normed[...] = (lean * (1.0 + gains[0:1, :width])).astype(BF16)
    qkv_pre[...] = dot(normed[...], w_qkv[...])
    cos_v, sin_v = cosine[...], sine[...]
    q_scale, k_scale = (gains[k : k + 1, width : width + head_dim] for k in (0, 1))
    key = head_forward(qkv_pre[:, at : at + head_dim], k_scale, cos_v, sin_v, 1.0)
    kv[yl, :, :head_dim] = key
    kv[yl, :, head_dim:] = qkv_pre[:, at + head_dim :].astype(BF16)
    kv_sent = lines.copy(kv.at[yl], kv.at[yl], here.pair())
    gather[2].second()
    keep(normed)
    keep(qkv_pre)
    for h in range(heads):
        cols = slice(h * head_dim, (h + 1) * head_dim)
        queries[:, cols] = head_forward(qkv_pre[:, cols], q_scale, cos_v, sin_v, head_dim**-0.5)
    gather[1].wait()
    core_out = lines.copy(w_out.at[:, :, c], w_out.at[:, :, c], here.mate())
    kv_sent.wait_recv()
    keep(queries)
    keep(kv)
    keys = kv[:, :, :head_dim].reshape(2 * n, head_dim)
    values = kv[:, :, head_dim:].reshape(2 * n, head_dim)
    ring = RingGather(here, lines, mlp_in, xs)
    half = n // 2
    for part in range(2):
        spot = slice(part * half, (part + 1) * half)
        row = lax.broadcasted_iota(jnp.int32, (half, 2 * n), 0) + (yl * n + part * half)
        allowed = lax.broadcasted_iota(jnp.int32, (half, 2 * n), 1) <= row
        for h in range(heads):
            if part == 0 and h == 2:
                gather[3].first()
            cols = slice(h * head_dim, (h + 1) * head_dim)
            scores = jnp.where(allowed, dot(queries[spot, cols], keys, NT), -1e30)
            terms = jnp.exp(scores - jnp.max(scores, axis=-1, keepdims=True))
            low = (terms * (1.0 / jnp.sum(terms, axis=-1, keepdims=True))).astype(BF16)
            probs[h, spot] = low
            context[spot, cols] = dot(low, values).astype(BF16)
        if part == 0:
            core_out.wait_recv()
        att = dot(context[spot, :], w_out[...].reshape(at, width))
        attended[spot, :] = att
        r = lax.rsqrt(jnp.mean(att * att, axis=-1, keepdims=True) + EPS)
        mid = x[spot] + att * r * (1.0 + gains[1:2, :width])
        middle[spot, :] = mid
        r = lax.rsqrt(jnp.mean(mid * mid, axis=-1, keepdims=True) + EPS)
        mlp_in[spot, :] = (mid * r * (1.0 + gains[2:3, :width])).astype(BF16)
        if part == 0:
            ring.start_low()
        else:
            ring.start_high()
    gather[2].relay()
    gather[3].second()
    for ref in (probs, context, w_out, attended, middle):
        keep(ref)
    ring.relay()
    gather[2].wait()
    for f in range(16):
        for mat, whole in ((0, gate_full), (1, up_full)):
            whole[rows * f : rows * f + rows] = full_in[f // 4, (f // 2) % 2, mat, f % 2]
    keep(gate_full)
    keep(up_full)
    ring.forward()
    gather[3].relay()
    ring.ready0()
    gather[3].wait()
    for k in range(8):
        for p in range(4):
            count = min(32, PART - 32 * p)
            down_full[PART * k + 32 * p : PART * k + 32 * p + count] = full_down[
                k // 2, k % 2, p // 2, p % 2, :count
            ]
    keep(down_full)
    ring.ready3()
    ring.ready1()
    ring.ready2()
    keep(xs)
    lines.drain()
    moves.drain()


def attend_block(tokens, cosine, sine, tail, w_query, w_key, w_value, own_out, w_gate, w_up, w_down):
    n, width = tokens.shape
    vmem = pl.BlockSpec(memory_space=pltpu.VMEM)
    shape = jax.ShapeDtypeStruct
    low = lambda *s: shape(s, BF16)
    rows, out_width = w_query.shape
    head_dim, cols = w_key.shape[1], tail.shape[1]
    p_qkv, p_out = (rows + 8, cols // 4), own_out.shape[2:]
    p_in, p_down = (rows, CORE_UNITS), (32, width)
    vm = lambda *s: pltpu.VMEM(s, BF16)
    held = (
        low(4, 2 * n, width),
        low(width, CORE_UNITS),
        low(width, CORE_UNITS),
        low(CORE_UNITS, width),
        low(width, cols),
        low(4, 2, 2, 2, 2, *p_out),
        low(n, width),
        low(n, out_width),
        low(2, n, 2 * head_dim),
        low(out_width // head_dim, n, 2 * n),
        low(n, out_width),
        shape((n, width), F32),
        shape((n, cols), F32),
        shape((n, width), F32),
    )
    return pl.pallas_call(
        attend_kernel,
        out_shape=held + (shape((8, cols), F32),),
        in_specs=[vmem] * 8 + [pl.BlockSpec(memory_space=pl.ANY)] * 3,
        out_specs=(pl.BlockSpec(memory_space=pl.ANY),) * 14 + (vmem,),
        scratch_shapes=[pltpu.VMEM(a.shape, a.dtype) for a in held]
        + [
            vm(n, width),
            vm(2, 2, *p_qkv),
            vm(2, 2, *p_in),
            vm(2, 2, *p_down),
            vm(4, 2, 2, 2, 2, *p_qkv),
            vm(4, 2, 2, 2, *p_in),
            vm(4, 2, 2, 2, *p_down),
            vm(2, 2, *p_in),
            vm(*w_gate.shape),
            vm(*w_up.shape),
            vm(*w_down.shape),
            pltpu.SemaphoreType.DMA((87,)),
            pltpu.SemaphoreType.DMA((87,)),
            pltpu.SemaphoreType.DMA((4,)),
            pltpu.SemaphoreType.DMA((17,)),
        ],
        compiler_params=pltpu.CompilerParams(
            collective_id=0, has_side_effects=True, vmem_limit_bytes=62 * MIB
        ),
        name="attend",
    )(tokens, cosine, sine, tail, w_query, w_key, w_value, own_out, w_gate, w_up, w_down)


class PlaneSum:
    def __init__(
        self, here, lines, grads, landed_a, half_a, sums_a, landed_b, half_b, sums_b, last_a, last_b
    ):
        self.here, self.lines, self.grads = here, lines, grads
        self.landed_a, self.half_a, self.sums_a, self.last_a = landed_a, half_a, sums_a, last_a
        self.landed_b, self.half_b, self.sums_b, self.last_b = landed_b, half_b, sums_b, last_b

    @staticmethod
    def scratch(piece):
        vm = lambda *lead: pltpu.VMEM((*lead, *piece), BF16)
        return [vm(2, 4), vm(2, 2), vm(4), vm(2, 2, 2), vm(2, 2), vm(2, 2), vm(3), vm(3)]

    def spots(self, d):
        _, shard, yl = self.here.to(dy=d)
        yh = lax.rem(shard // 2, 2)
        z = self.here.to(dz=d)[1] // 4
        low, high = pl.ds(0, 2), pl.ds(2, 2)
        return ((low, yh, yl, 0), (high, yh, yl, 0)), ((z, 0, slice(None), 1), (z, 1, slice(None), 1))

    def first(self):
        low, high = pl.ds(0, 2), pl.ds(2, 2)
        self.begin(
            self.half_a,
            self.half_b,
            [self.landed_a.at[0, high], self.landed_a.at[1, low]],
            [self.landed_b.at[0, 1], self.landed_b.at[1, 0]],
        )

    def begin(self, half_a, half_b, near_a, near_b):
        here, g, copy = self.here, self.grads, self.lines.copy
        up_y, down_y, up_z, down_z = here.to(dy=1), here.to(dy=3), here.to(dz=1), here.to(dz=3)
        a, b = self.spots(2)
        self.half = [
            copy(g.at[a[0]], half_a.at[0], up_y),
            copy(g.at[a[1]], half_a.at[1], down_y),
            copy(g.at[b[0]], half_b.at[0], up_z),
            copy(g.at[b[1]], half_b.at[1], down_z),
        ]
        (a1, b1), (a3, b3) = self.spots(1), self.spots(3)
        self.a = [copy(g.at[a1[1]], near_a[0], up_y), copy(g.at[a3[0]], near_a[1], down_y)]
        self.b = [copy(g.at[b1[1]], near_b[0], up_z), copy(g.at[b3[0]], near_b[1], down_z)]

    def begin_by_owner(self, half_a, half_b, near_a, near_b):
        here, g, plan = self.here, self.grads, self.lines.plan
        up_y, down_y, up_z, down_z = here.to(dy=1), here.to(dy=3), here.to(dz=1), here.to(dz=3)
        (a, b), (a1, b1), (a3, b3) = self.spots(2), self.spots(1), self.spots(3)
        same = [plan(g.at[a[0]], half_a.at[0], up_y), plan(g.at[a[1]], half_a.at[1], down_y)]
        other = [plan(g.at[a1[1]], near_a.at[0], up_y), plan(g.at[a3[0]], near_a.at[1], down_y)]
        by_z = [
            [
                plan(g.at[b[0][0], 0, k, 1], half_b.at[0, k], up_z),
                plan(g.at[b[0][0], 1, k, 1], half_b.at[1, k], down_z),
                plan(g.at[b1[0][0], 1, k, 1], near_b.at[0, k], up_z),
                plan(g.at[b3[0][0], 0, k, 1], near_b.at[1, k], down_z),
            ]
            for k in range(2)
        ]
        self.half, self.a, self.b = same, other, by_z[0] + by_z[1]

        def send(k):
            @pl.when(here.yl == k)
            def _():
                for made in same:
                    made.start()

            @pl.when(here.yl != k)
            def _():
                for made in other:
                    made.start()

            for made in by_z[k]:
                made.start()

        return send

    def begun(self):
        for made in self.half + self.a + self.b:
            made.wait_recv()

    def resume(self, moves, half_a, half_b, near_a, near_b):
        low, high = pl.ds(0, 2), pl.ds(2, 2)
        self.half = [moves.start(half_a, self.half_a), moves.start(half_b, self.half_b)]
        self.a = [
            moves.start(near_a.at[0], self.landed_a.at[0, high]),
            moves.start(near_a.at[1], self.landed_a.at[1, low]),
        ]
        self.b = [
            moves.start(near_b.at[0], self.landed_b.at[0, 1]),
            moves.start(near_b.at[1], self.landed_b.at[1, 0]),
        ]

    def resumed(self):
        for made in self.half + self.a + self.b:
            made.wait()
        self.half, self.a, self.b = [], [], []

    def middle(self):
        here, g, copy = self.here, self.grads, self.lines.copy
        low, high = pl.ds(0, 2), pl.ds(2, 2)
        (a1, b1), (a3, b3) = self.spots(1), self.spots(3)
        for made in self.half:
            made.wait_recv()
        for spot, half in zip(
            (a1[0], a3[1], b1[0], b3[1]),
            (self.half_a.at[0], self.half_a.at[1], self.half_b.at[0], self.half_b.at[1]),
        ):
            g[spot] = (g[spot].astype(F32) + half[...].astype(F32)).astype(BF16)
        self.a += [
            copy(g.at[a1[0]], self.landed_a.at[0, low], here.to(dy=1)),
            copy(g.at[a3[1]], self.landed_a.at[1, high], here.to(dy=3)),
        ]
        self.b += [
            copy(g.at[b1[0]], self.landed_b.at[0, 0], here.to(dz=1)),
            copy(g.at[b3[1]], self.landed_b.at[1, 1], here.to(dz=3)),
        ]

    def second(self):
        here, g, copy = self.here, self.grads, self.lines.copy
        for made in self.a:
            made.wait_recv()
        for k in range(4):
            total = g[k, here.yh, here.yl, 0].astype(F32)
            for j in range(2):
                total = total + self.landed_a[j, k].astype(F32)
            self.sums_a[k] = total.astype(BF16)
        self.a = []
        for d in (1, 3, 2):
            z = here.to(dz=d)[1] // 4
            self.a.append(copy(self.sums_a.at[z], self.last_a.at[d - 1], here.to(dz=d)))
        for made in self.b:
            made.wait_recv()
        for k in range(4):
            total = g[here.z, k // 2, k % 2, 1].astype(F32)
            for j in range(2):
                total = total + self.landed_b[j, k // 2, k % 2].astype(F32)
            self.sums_b[k // 2, k % 2] = total.astype(BF16)
        self.b = []
        for d in (1, 3, 2):
            _, shard, yl = here.to(dy=d)
            yh = lax.rem(shard // 2, 2)
            self.b.append(copy(self.sums_b.at[yh, yl], self.last_b.at[d - 1], here.to(dy=d)))

    def result(self, path):
        here = self.here
        for made in (self.a, self.b)[path]:
            made.wait_recv()
        own = self.sums_a[here.z] if path == 0 else self.sums_b[here.yh, here.yl]
        last = (self.last_a, self.last_b)[path]
        total = own.astype(F32)
        for j in range(3):
            total = total + last[j].astype(F32)
        return total


def retreat_kernel(
    middle_grad_h, attended_h, context_h, probs_h, kv_h, queries_h, qkv_pre_h, normed_h, tokens_h,
    w_qkv_h, w_out_h, g_down_h, g_in_h, half_a, half_b, near_a, near_b,
    down_half_a, down_half_b, down_near_a, down_near_b,
    cosine, sine, gains, d_gain_in, d_gain_out,
    grad_tokens, laid_h, o_down, o_qkv, o_out,
    laid, row, o_in, middle_grad, attended, context, probs, kv, queries, qkv_pre, normed, tokens, w_qkv, w_out,
    g_down, g_in,
    context_grad, attn_side, kv_part, kv_give, kv_land, g_qkv, g_out, d_gains,
    chip_qkv, chip_out, cross_qkv, cross_out, swap, half_qkv, half_out, land_qkv, land_out, *rest,
):
    here = Place()
    send, recv, moved = rest[-3:]
    x, yl, c = here.x, here.yl, here.c
    moves = Moves(moved)
    lines = Lines(send, recv)
    copy = lines.copy
    sums = [
        PlaneSum(here, lines, g, *rest[8 * k : 8 * k + 8])
        for k, g in enumerate((g_down, chip_qkv, chip_out, g_in))
    ]
    loads = {"g_in": moves.start(g_in_h, g_in)}
    sums[3].resume(moves, half_a, half_b, near_a, near_b)
    loads["g_down"] = moves.start(g_down_h, g_down)
    sums[0].resume(moves, down_half_a, down_half_b, down_near_a, down_near_b)
    loads |= {
        name: moves.start(a, b)
        for name, a, b in (
            ("attended", attended_h, attended),
            ("middle_grad", middle_grad_h, middle_grad),
            ("w_out", w_out_h, w_out),
            ("context", context_h, context),
            ("probs", probs_h, probs),
            ("kv", kv_h, kv),
            ("queries", queries_h, queries),
            ("qkv_pre", qkv_pre_h, qkv_pre),
            ("w_qkv", w_qkv_h, w_qkv),
            ("normed", normed_h, normed),
            ("tokens", tokens_h, tokens),
        )
    }

    def ready(*names):
        for name in names:
            loads[name].wait()

    greet([here.mate()] + plane_peers(here) + [here.to(dx=d) for d in (1, 2, 3)])
    n, width = middle_grad.shape
    head_dim = 2 * cosine.shape[1]
    heads = queries.shape[1] // head_dim
    rows = width // 16
    at = heads * head_dim
    ready("g_in")
    sums[3].resumed()
    sums[3].middle()
    ready("g_down")
    sums[0].resumed()
    sums[0].middle()
    ready("attended", "middle_grad", "w_out", "context")

    att, dy = attended[...], middle_grad[...]
    r, grad = norm_back(att, dy * (1.0 + gains[1:2, :width]), width)
    d_gains[...] = jnp.zeros_like(d_gains)
    d_gains[1:2, :width] = jnp.sum(dy * att * r, axis=0, keepdims=True)
    d_gains[2:3, :width] = d_gain_in[...]
    d_gains[3:4, :width] = d_gain_out[...]
    attended_grad = grad.astype(BF16)
    out_full = w_out[...].reshape(at, width)
    context_grad[...] = dot(attended_grad, out_full, NT).astype(BF16)
    grad_out = dot(context[...], attended_grad, TN)
    g_out[...] = grad_out.astype(BF16).reshape(g_out.shape)
    give_out = copy(g_out.at[:, :, 1 - c], cross_out, here.mate())
    ready("probs", "kv", "queries", "qkv_pre")
    keys = kv[:, :, :head_dim].reshape(2 * n, head_dim)
    values = kv[:, :, head_dim:].reshape(2 * n, head_dim)
    cos_v, sin_v = cosine[...], sine[...]
    q_scale, k_scale = (gains[k : k + 1, width : width + head_dim] for k in (0, 1))
    d_query = jnp.zeros((1, head_dim), F32)
    for h in range(heads):
        cols = slice(h * head_dim, (h + 1) * head_dim)
        low = probs[h]
        high = low.astype(F32)
        prob_grad = dot(context_grad[:, cols], values, NT)
        inner = jnp.sum(high * prob_grad, axis=-1, keepdims=True)
        score_grad = (high * (prob_grad - inner)).astype(BF16)
        key_part = dot(score_grad, queries[:, cols], TN)
        value_part = dot(low, context_grad[:, cols], TN)
        if h == 0:
            kv_part[:, :, :head_dim] = key_part.reshape(2, n, head_dim)
            kv_part[:, :, head_dim:] = value_part.reshape(2, n, head_dim)
        else:
            kv_part[:, :, :head_dim] += key_part.reshape(2, n, head_dim)
            kv_part[:, :, head_dim:] += value_part.reshape(2, n, head_dim)
        query_grad = dot(score_grad, keys).astype(BF16).astype(F32)
        side, d_scale = head_backward(
            query_grad, qkv_pre[:, cols], q_scale, cos_v, sin_v, head_dim**-0.5
        )
        attn_side[:, cols] = side
        d_query = d_query + d_scale
        if h == 1:
            sums[3].second()
        if h == 2:
            sums[0].second()
    kv_give[...] = kv_part[1 - yl].astype(BF16)
    kv_sent = copy(kv_give, kv_land, here.pair())
    ready("w_qkv", "normed", "tokens")
    normed_grad = dot(attn_side[:, :at], w_qkv[:, :at], NT)
    grad_query = dot(normed[...], attn_side[:, :at], TN)
    for path in (0, 1):
        swap[path] = sums[3].result(path).astype(BF16)
    across = copy(swap.at[1 - c], o_in.at[x, yl, c], here.mate())
    o_in[x, yl, c] = swap[c]
    for path in (0, 1):
        o_down[x, yl, path] = sums[0].result(path).astype(BF16)
    down_pair = copy(o_down.at[x, yl], o_down.at[x, yl], here.pair())
    give_out.wait_recv()
    across.wait_recv()
    in_pair = copy(o_in.at[x, yl], o_in.at[x, yl], here.pair())
    for z in range(4):
        for yh in range(2):
            chip_out[z, yh] = (g_out[z, yh, c].astype(F32) + cross_out[z, yh].astype(F32)).astype(BF16)
    kv_sent.wait_recv()
    kv_grad = (kv_part[yl] + kv_land[...].astype(F32)).astype(BF16)
    side, d_key = head_backward(
        kv_grad[:, :head_dim].astype(F32), qkv_pre[:, at : at + head_dim], k_scale, cos_v, sin_v, 1.0
    )
    attn_side[:, at : at + head_dim] = side
    attn_side[:, at + head_dim :] = kv_grad[:, head_dim:]
    d_gains[0:1, width : width + head_dim] = d_query
    d_gains[1:2, width : width + head_dim] = d_key
    down_pair.wait_recv()
    down_x = [copy(o_down.at[x], o_down.at[x], here.to(dx=d)) for d in (1, 3, 2)]

    normed_grad = normed_grad + dot(attn_side[:, at:], w_qkv[:, at:], NT)
    tok = tokens[...].astype(F32)
    r, grad = norm_back(tok, normed_grad * (1.0 + gains[0:1, :width]), width)
    grad_tokens[...] = (middle_grad[...] + grad).astype(BF16)
    d_gains[0:1, :width] = jnp.sum(normed_grad * tok * r, axis=0, keepdims=True)
    grad_kv = dot(normed[...], attn_side[:, at:], TN)
    wide = g_qkv.shape[-1]
    for p in range(4):
        cols = slice(p * wide, (p + 1) * wide)
        for f in range(16):
            spot = (f // 4, (f // 2) % 2, f % 2, p // 2, p % 2)
            span = slice(rows * f, rows * f + rows)
            parts = []
            if p * wide < at:
                parts.append(grad_query[span, p * wide : min((p + 1) * wide, at)])
            if (p + 1) * wide > at:
                parts.append(grad_kv[span, max(p * wide - at, 0) : (p + 1) * wide - at])
            block = parts[0] if len(parts) == 1 else jnp.concatenate(parts, axis=1)
            g_qkv[spot] = jnp.concatenate([block, d_gains[:, cols]], axis=0).astype(BF16)
    give_qkv = copy(g_qkv.at[:, :, 1 - c], cross_qkv, here.mate())
    sums[2].first()
    in_pair.wait_recv()
    right, left = here.to(dx=1), here.to(dx=3)
    own = [o_in.at[x, m] for m in (0, 1)]
    early = [copy(own[0], own[0], right), copy(own[1], own[1], left)]
    late = [copy(own[1], own[1], right), copy(own[0], own[0], left)]
    give_qkv.wait_recv()
    for z in range(4):
        for yh in range(2):
            chip_qkv[z, yh] = (g_qkv[z, yh, c].astype(F32) + cross_qkv[z, yh].astype(F32)).astype(BF16)
    sums[1].first()
    sums[2].middle()
    sums[1].middle()
    for made, at_x, m, to in ((early[0], left[0], 0, right), (early[1], right[0], 1, left)):
        made.wait_recv()
        late.append(copy(o_in.at[at_x, m], o_in.at[at_x, m], to))
    sums[2].second()
    sums[1].second()
    for path in (0, 1):
        half_out[path] = sums[2].result(path).astype(BF16)
        half_qkv[path] = sums[1].result(path).astype(BF16)
    by_x = []
    for d in (1, 3, 2):
        by_x.append(copy(half_qkv, land_qkv.at[d - 1], here.to(dx=d)))
        by_x.append(copy(half_out, land_out.at[d - 1], here.to(dx=d)))
    for made in late:
        made.wait_recv()
    block = row.shape[1] // 16
    for m in range(2):
        for k in range(4):
            count = min(PART, block - PART * k)
            for f in range(16):
                piece = o_in[k, m, f % 2].astype(F32)[:, PART * (f // 2) : PART * (f // 2) + count]
                row[:, block * f + PART * k : block * f + PART * k + count] = piece
        laid[m] = row[...].astype(BF16)
        moves.store(laid.at[m], laid_h.at[m])
    for made in by_x:
        made.wait_recv()
    for half, land, out in ((half_qkv, land_qkv, o_qkv), (half_out, land_out, o_out)):
        for path in (0, 1):
            total = half[path].astype(F32)
            for j in range(3):
                total = total + land[j, path].astype(F32)
            out[yl, path] = total.astype(BF16)
    ends = [copy(o.at[yl], o.at[yl], here.pair()) for o in (o_qkv, o_out)]
    for made in down_x + ends:
        made.wait_recv()
    lines.drain()
    moves.drain()


def retreat_block(*args):
    (
        middle_grad, attended, context, probs, kv, queries, qkv_pre, normed, tokens, w_qkv, w_out,
        g_down, g_in, *_, cosine, _, _, _, _,
    ) = args
    vmem, hbm = pl.BlockSpec(memory_space=pltpu.VMEM), pl.BlockSpec(memory_space=pl.ANY)
    shape = jax.ShapeDtypeStruct
    n, width = middle_grad.shape
    out_width, head_dim = queries.shape[1], 2 * cosine.shape[1]
    cols = qkv_pre.shape[1]
    p_in, p_down, p_out = g_in.shape[4:], g_down.shape[4:], w_out.shape[5:]
    p_qkv = (width // 16 + 8, cols // 4)
    vm = lambda *s: pltpu.VMEM(s, BF16)
    units = 16 * UNITS_OF_SHARD
    scratch = [vm(2, width // 16, units), pltpu.VMEM((width // 16, units), F32), vm(4, 2, 2, *p_in)]
    scratch += [pltpu.VMEM(a.shape, a.dtype) for a in args[:11]]
    scratch += [vm(*g_down.shape), vm(*g_in.shape)]
    scratch += [vm(n, out_width), vm(n, cols), pltpu.VMEM((2, n, 2 * head_dim), F32)]
    scratch += [vm(n, 2 * head_dim)] * 2
    scratch += [vm(4, 2, 2, 2, 2, *p_qkv), vm(4, 2, 2, 2, 2, *p_out), pltpu.VMEM((8, cols), F32)]
    scratch += [vm(4, 2, 2, 2, *p_qkv), vm(4, 2, 2, 2, *p_out)] * 2
    scratch += [vm(2, *p_in), vm(2, *p_qkv), vm(2, *p_out), vm(3, 2, *p_qkv), vm(3, 2, *p_out)]
    for piece in (p_down, p_qkv, p_out, p_in):
        scratch += PlaneSum.scratch(piece)
    scratch += [pltpu.SemaphoreType.DMA((79,))] * 2 + [pltpu.SemaphoreType.DMA((27,))]
    low = lambda *s: shape(s, BF16)
    return pl.pallas_call(
        retreat_kernel,
        out_shape=(
            low(n, width),
            low(2, width // 16, units),
            low(4, 2, 2, *p_down),
            low(2, 2, *p_qkv),
            low(2, 2, *p_out),
        ),
        in_specs=[hbm] * 21 + [vmem] * 5,
        out_specs=(vmem, hbm) + (vmem,) * 3,
        scratch_shapes=scratch,
        compiler_params=pltpu.CompilerParams(
            collective_id=2, has_side_effects=True, vmem_limit_bytes=63 * MIB
        ),
        name="retreat",
    )(*args)


def finish_kernel(
    o_in_h, o_down_h, o_qkv_h, o_out_h, shown_h, taken_h,
    layer_out_h, grad_tokens_h, out_query, out_key, out_value, out_out, out_gate_h, out_up_h, out_down_h,
    *rest,
):
    out_gains = rest[:6]
    o_in, o_down, o_qkv, o_out, out_gate, out_up, out_down, shown, taken, moved = rest[6:]
    moves = Moves(moved)
    load_in = [moves.start(o_in_h.at[m], o_in.at[m]) for m in (0, 1)]
    load_tokens = [moves.start(shown_h, shown), moves.start(taken_h, taken)]
    load_down = moves.start(o_down_h, o_down)
    load_rest = [moves.start(o_qkv_h, o_qkv), moves.start(o_out_h, o_out)]
    rows, units = out_gate.shape
    block = units // 16
    wide = o_qkv.shape[-1]
    at, head_dim = out_query.shape[1], out_key.shape[1]
    for m, out, out_h in ((0, out_gate, out_gate_h), (1, out_up, out_up_h)):
        load_in[m].wait()
        out[...] = o_in[m].astype(F32)
        moves.store(out, out_h)
    for made, held, out_h in zip(load_tokens, (shown, taken), (layer_out_h, grad_tokens_h)):
        made.wait()
        moves.store(held, out_h)
    load_down.wait()
    for k in range(4):
        for p in range(4):
            start = PART * k + 32 * p
            count = min(32, PART - 32 * p, block - start)
            if count > 0:
                out_down[start : start + count] = o_down[k, p // 2, p % 2, :count].astype(F32)
    moves.store(out_down, out_down_h)
    for made in load_rest:
        made.wait()
    tail = []
    for p in range(4):
        piece = o_qkv[p // 2, p % 2].astype(F32)
        for out, start in ((out_query, 0), (out_key, at), (out_value, at + head_dim)):
            lo, hi = max(p * wide, start), min((p + 1) * wide, start + out.shape[1])
            if lo < hi:
                out[:, lo - start : hi - start] = piece[:rows, lo - p * wide : hi - p * wide]
        tail.append(piece[rows:])
        height = o_out.shape[2]
        out_out[p * height : (p + 1) * height] = o_out[p // 2, p % 2].astype(F32)
    tail = jnp.concatenate(tail, axis=1)
    width = out_out.shape[1]
    shard = lax.axis_index("fsdp")
    turned = pltpu.roll(tail[:, :width], lax.rem(width - rows * shard, width), 1)
    for k in range(4):
        out_gains[k][...] = turned[k, :rows]
    piece = head_dim // 16
    turned = pltpu.roll(tail[:, width : width + head_dim], lax.rem(head_dim - piece * shard, head_dim), 1)
    for k in range(2):
        out_gains[4 + k][...] = turned[k, :piece]
    moves.drain()


def finish_block(o_in, o_down, o_qkv, o_out, layer_out, grad_tokens, out_shape):
    vmem, hbm = pl.BlockSpec(memory_space=pltpu.VMEM), pl.BlockSpec(memory_space=pl.ANY)
    big = out_shape[6:9]
    return pl.pallas_call(
        finish_kernel,
        out_shape=out_shape,
        in_specs=[hbm] * 6,
        out_specs=(hbm,) * 2 + (vmem,) * 4 + (hbm,) * 3 + (vmem,) * 6,
        scratch_shapes=[pltpu.VMEM(a.shape, a.dtype) for a in (o_in, o_down, o_qkv, o_out, *big, layer_out, grad_tokens)]
        + [pltpu.SemaphoreType.DMA((12,))],
        compiler_params=pltpu.CompilerParams(vmem_limit_bytes=62 * MIB),
        name="finish",
    )(o_in, o_down, o_qkv, o_out, layer_out, grad_tokens)


def body(
    tokens,
    w_query,
    w_key,
    w_value,
    w_out,
    w_gate,
    w_up,
    w_down,
    pre_attn_gain,
    post_attn_gain,
    pre_mlp_gain,
    post_mlp_gain,
    query_gain,
    key_gain,
    cotangent,
):
    n, width = tokens.shape
    rows = w_query.shape[0]
    head_dim = w_key.shape[1]
    out_width = w_query.shape[1]
    shard = lax.axis_index("fsdp")

    mine = jnp.arange(16) == shard
    spread = lambda g: jnp.where(mine[:, None], g[None, :], 0).reshape(1, -1)
    gains_d = [spread(g) for g in (pre_attn_gain, post_attn_gain, pre_mlp_gain, post_mlp_gain)]
    gains_h = jnp.concatenate([spread(query_gain), spread(key_gain)], axis=0)
    tail = jnp.concatenate(
        [
            jnp.pad(jnp.concatenate(gains_d, axis=0), ((0, 4), (0, 0))),
            jnp.pad(gains_h, ((0, 6), (0, out_width + head_dim - width))),
        ],
        axis=1,
    )
    own_out = w_out.reshape(2, 2, -1, width)
    positions = (lax.axis_index("seq") * n + jnp.arange(n, dtype=jnp.int32)).astype(F32)
    frequency = jnp.exp(
        jnp.arange(head_dim // 2, dtype=F32) * (-2.0 * math.log(1000000.0) / head_dim)
    )
    angles = positions[:, None] * frequency[None, :]
    cosine, sine = jnp.cos(angles), jnp.sin(angles)

    (
        xs, gate_full, up_full, down_full, w_qkv, w_out_full, normed, queries, kv, probs, context,
        attended, qkv_pre, middle, gains,
    ) = attend_block(
        tokens, cosine, sine, tail, w_query, w_key, w_value, own_out, w_gate, w_up, w_down
    )
    layer_out, middle_grad, d_gain_in, d_gain_out, *begun, g_in, g_down = mlp_block(
        xs, middle, cotangent, gains, gate_full, up_full, down_full
    )
    grad_tokens, o_in, o_down, o_qkv, o_out = retreat_block(
        middle_grad, attended, context, probs, kv, queries, qkv_pre, normed, tokens, w_qkv,
        w_out_full, g_down, g_in, *begun, cosine, sine, gains, d_gain_in, d_gain_out,
    )
    like = lambda a, kind: jax.ShapeDtypeStruct(a.shape, kind)
    weights = (w_query, w_key, w_value, w_out, w_gate, w_up, w_down)
    gain_args = (pre_attn_gain, post_attn_gain, pre_mlp_gain, post_mlp_gain, query_gain, key_gain)
    shapes = [like(tokens, BF16)] * 2 + [like(a, F32) for a in weights + gain_args]
    return tuple(finish_block(o_in, o_down, o_qkv, o_out, layer_out, grad_tokens, shapes))


def solution(mesh):
    tokens = P(("dp", "fsdp", "seq"), None)
    weight, gain = P("fsdp", None), P("fsdp")
    return jax.shard_map(
        body,
        mesh=mesh,
        in_specs=(tokens,) + (weight,) * 7 + (gain,) * 6 + (tokens,),
        out_specs=(tokens,) * 2 + (weight,) * 7 + (gain,) * 6,
        check_vma=False,
    )
```
